32 devices in a mesh: chan: 2 (over y), point: 16 (over z, x, core).
Axes of the slice: x: 2, y: 2, z: 4, core: 2. Of those that a mesh axis runs over, the one named last changes fastest.
Arguments:
- images: bfloat16 [32, 4, 4, 256, 256], P('point', None, 'chan'), may hold values from -6 to 6
- beam: bfloat16 [32, 4, 256, 256], P('point'), may hold values from 0.049804688 to 1
- exponent: float32 [4], replicated, may hold values from 0.6 to 1.6
- intersection: int32 [32, 4], P('point'), may hold values from 0 to 127
- counts: int32 [32], P('point'), may hold values from 1 to 4
- owner: int32 [128], replicated, may hold values from 0 to 127, each once
- psf: bfloat16 [4, 2, 256, 256], P('chan'), may hold values from -0.375 to 0.375
Outputs:
- sky_tiles: bfloat16 [128, 4, 256, 256], P('point', 'chan')
The draws below stay inside these ranges and needn't reach their ends.
Inputs may be any that keep to these rules, and one draw needn't show every extreme that they name: `intersection`: slots at or after counts[p] are ignored. `owner`: each sky tile appears once.
All inputs are finite; a program needn't handle non-finite values.
Results may differ from the reference program's by a relative error of at most 0.0065.
Values may be sent and summed in bfloat16 or wider, within the bound.
No kernel may reach another device: no remote copies, remote signals or barrier semaphores. Data moves between devices by JAX's collectives and lax.ppermute only.
A program may use at most 64 MiB of HBM per device.

```python
import math
import jax
import jax.numpy as jnp
from jax import lax

TILE = 256
SLOTS = 4
CH = 4
POINTINGS = 32
NSKY = 128


def place_ends(array, rng, smallest, top_value):
    index_at = [jax.random.randint(jax.random.fold_in(rng, axis), (), 0, length) for axis, length in enumerate(array.shape)]
    main_axis = array.shape.index(max(array.shape))
    next_to = index_at[:main_axis] + [(index_at[main_axis] + 1) % array.shape[main_axis]] + index_at[main_axis + 1:]
    return array.at[tuple(index_at)].set(smallest).at[tuple(next_to)].set(top_value)


def block_levels(key, shape, pieces, smallest, top_value):
    gain = 1.0
    for axis_at, blocks in pieces:
        heights = jax.random.uniform(jax.random.fold_in(jax.random.fold_in(key, 6), axis_at), (blocks,), jnp.float32, smallest / len(pieces), top_value / len(pieces))
        gain = gain * jnp.repeat(jnp.exp(heights), shape[axis_at] // blocks).reshape((-1,) + (1,) * (len(shape) - 1 - axis_at))
    return gain


def scatter_about(rng, shape, deviation, bound, shards=(), dtype=jnp.bfloat16):
    values = jax.random.normal(rng, shape, jnp.float32) * deviation
    if len(shards) > 0:
        values = block_levels(rng, shape, shards, -0.22, 0.18) * values
    return jnp.clip(values, min=-bound, max=bound).astype(dtype)


def setup_inputs(seed: int = 0) -> dict:
    streams_of = jax.random.split(jax.random.key(seed), 8)
    images = scatter_about(streams_of[0], (POINTINGS, SLOTS, CH, TILE, TILE), 1.0, 6.0, ((0, 16), (2, 2)))
    beam = jnp.clip(jnp.exp(math.log(1.0) - 2.9996462 * jax.random.uniform(streams_of[1], (POINTINGS, SLOTS, TILE, TILE), jnp.float32) ** block_levels(streams_of[1], (POINTINGS, SLOTS, TILE, TILE), ((0, 16),), -0.2, 0.2)), 0.049804688, 1.0).astype(jnp.bfloat16)
    exponent = jnp.clip(jax.random.uniform(streams_of[2], (CH,), jnp.float32, 0.6, 1.6), 0.6, 1.6)
    intersection = place_ends(jax.random.randint(streams_of[3], (POINTINGS, SLOTS), 0, NSKY), jax.random.fold_in(streams_of[3], 1), 0, NSKY - 1).astype(jnp.int32)
    counts = place_ends(jax.random.randint(streams_of[4], (POINTINGS,), 1, SLOTS + 1), jax.random.fold_in(streams_of[4], 1), 1, SLOTS).astype(jnp.int32)
    owner = jax.random.permutation(streams_of[5], NSKY).astype(jnp.int32)
    psf = scatter_about(streams_of[6], (CH, 2, TILE, TILE), TILE ** -0.5, 0.375, ((0, 2),))
    return dict(images=images, beam=beam, exponent=exponent, intersection=intersection, counts=counts, owner=owner, psf=psf)


weight_floor = 0.05


def reference(images, beam, exponent, intersection, counts, owner, psf):
    live = jnp.arange(SLOTS)[None, :] < counts[:, None]
    slot_ids = jnp.where(live, intersection, NSKY).reshape(-1).astype(jnp.int32)
    beam_log = jnp.log(beam.reshape(-1, TILE, TILE).astype(jnp.float32))

    def weight_step(index, accum):
        power = jnp.exp(exponent[index] * beam_log)
        return accum + power * power

    wsum = lax.fori_loop(0, CH, weight_step, jnp.zeros(beam_log.shape, jnp.float32)) / CH
    total = jax.ops.segment_sum(wsum, slot_ids, NSKY + 1)[:NSKY]
    floored = jnp.maximum(total, weight_floor)

    def one_channel(chan_index):
        plane = images[:, :, chan_index].reshape(-1, TILE, TILE).astype(jnp.float32)
        weighted = (jnp.exp(exponent[chan_index] * beam_log) * plane).astype(jnp.bfloat16)
        weighted = lax.optimization_barrier(weighted).astype(jnp.float32)
        numer = jax.ops.segment_sum(weighted, slot_ids, NSKY + 1)[:NSKY]
        normal = (numer / floored).astype(jnp.bfloat16)
        ordered = normal[owner].astype(jnp.float32)
        left = jnp.einsum('sij,kj->sik', ordered, psf[chan_index, 1].astype(jnp.float32)).astype(jnp.bfloat16)
        left = lax.optimization_barrier(left).astype(jnp.float32)
        return jnp.einsum('ki,sij->skj', psf[chan_index, 0].astype(jnp.float32), left).astype(jnp.bfloat16)

    result = lax.map(one_channel, jnp.arange(CH))
    return jnp.transpose(result, (1, 0, 2, 3))
```

```python
import functools

import jax
import jax.numpy as jnp
from jax import lax
from jax.experimental import pallas as pl
from jax.experimental.pallas import tpu as pltpu
from jax.sharding import PartitionSpec as P

weight_floor = 0.05
VMEM_LIMIT = 48 * 1024 * 1024


def params():
    return pltpu.CompilerParams(vmem_limit_bytes=VMEM_LIMIT)


def put_rows(out_ref, at, value):
    group, rows = out_ref.shape[0], out_ref.shape[-2]
    for g in range(group):
        out_ref[(g,) + at] = value[g * rows:(g + 1) * rows].astype(jnp.bfloat16)


def row_block(tile, npoint):
    rows = tile // npoint
    block = max(rows, 16)
    return rows, block, block // rows


def weight_body(exp_ref, images_ref, beam_ref, out_ref):
    slots = images_ref.shape[1]
    for p in range(images_ref.shape[0]):
        for s in range(slots):
            logs = jnp.log(beam_ref[p, s].astype(jnp.float32))
            for c in range(images_ref.shape[2]):
                power = jnp.exp(exp_ref[c] * logs)
                plane = images_ref[p, s, c].astype(jnp.float32)
                put_rows(out_ref, (p * slots + s, c), power * plane)


def weigh(own_exp, images, beam, npoint):
    pts, slots, ch, tile, _ = images.shape
    rows, block, group = row_block(tile, npoint)
    return pl.pallas_call(
        weight_body,
        grid=(npoint // group,),
        in_specs=[
            pl.BlockSpec(memory_space=pltpu.SMEM),
            pl.BlockSpec((pts, slots, ch, block, tile), lambda i: (0, 0, 0, i, 0)),
            pl.BlockSpec((pts, slots, block, tile), lambda i: (0, 0, i, 0)),
        ],
        out_specs=pl.BlockSpec((group, pts * slots, ch, rows, tile), lambda i: (i, 0, 0, 0, 0)),
        out_shape=jax.ShapeDtypeStruct((npoint, pts * slots, ch, rows, tile), jnp.bfloat16),
        compiler_params=params(),
    )(own_exp, images, beam)


def split_body(beam_ref, out_ref):
    for s in range(beam_ref.shape[0]):
        put_rows(out_ref, (s,), beam_ref[s].astype(jnp.float32))


def split_rows(beam, npoint):
    s, tile, _ = beam.shape
    rows, block, group = row_block(tile, npoint)
    return pl.pallas_call(
        split_body,
        grid=(npoint // group,),
        in_specs=[pl.BlockSpec((s, block, tile), lambda i: (0, i, 0))],
        out_specs=pl.BlockSpec((group, s, rows, tile), lambda i: (i, 0, 0, 0)),
        out_shape=jax.ShapeDtypeStruct((npoint, s, rows, tile), jnp.bfloat16),
        compiler_params=params(),
    )(beam)


def total_body(s_dev, ids_ref, exp_ref, beam_ref, out_ref, acc_ref):
    nchan, npoint, part = beam_ref.shape[:3]
    nsky = out_ref.shape[0]
    ch = exp_ref.shape[0]
    acc_ref[...] = jnp.zeros_like(acc_ref)

    def step(d, carry):
        for share in range(nchan):
            for k in range(part):
                at = ids_ref[d, share * part + k]

                @pl.when(at < nsky)
                def _():
                    logs = jnp.log(beam_ref[share, d, k].astype(jnp.float32))
                    pw = jnp.zeros_like(logs)
                    for c in range(ch):
                        power = jnp.exp(exp_ref[c] * logs)
                        pw = pw + power * power
                    acc_ref[at] += pw * (1.0 / ch)

        return carry

    lax.fori_loop(0, npoint, step, 0)
    out_ref[...] = jnp.maximum(acc_ref[...], weight_floor)


def totals(ids, exponent, beams, nsky):
    rows, tile = beams.shape[3:]
    s_dev = ids.shape[1]
    return pl.pallas_call(
        functools.partial(total_body, s_dev),
        in_specs=[
            pl.BlockSpec(memory_space=pltpu.SMEM),
            pl.BlockSpec(memory_space=pltpu.SMEM),
            pl.BlockSpec(memory_space=pltpu.VMEM),
        ],
        out_specs=pl.BlockSpec(memory_space=pltpu.VMEM),
        out_shape=jax.ShapeDtypeStruct((nsky, rows, tile), jnp.float32),
        scratch_shapes=[pltpu.VMEM((nsky, rows, tile), jnp.float32)],
        compiler_params=params(),
    )(ids, exponent, beams)


def normal_body(ids_ref, owner_ref, tiles_ref, floor_ref, out_ref, acc_ref):
    npoint, s_dev, ch = tiles_ref.shape[:3]
    nsky = floor_ref.shape[0]
    acc_ref[...] = jnp.zeros_like(acc_ref)

    def step(d, carry):
        for s in range(s_dev):
            at = ids_ref[d, s]

            @pl.when(at < nsky)
            def _():
                acc_ref[at] += tiles_ref[d, s].astype(jnp.float32)

        return carry

    lax.fori_loop(0, npoint, step, 0)
    per = out_ref.shape[1]

    def emit(d, carry):
        for k in range(per):
            t = owner_ref[d * per + k]
            inv = floor_ref[t]
            for c in range(ch):
                out_ref[d, k, c] = (acc_ref[t, c] / inv).astype(jnp.bfloat16)
        return carry

    lax.fori_loop(0, npoint, emit, 0)


def normalise(ids, owner, tiles, floored):
    npoint, s_dev, ch, rows, tile = tiles.shape
    nsky = owner.shape[0]
    return pl.pallas_call(
        normal_body,
        in_specs=[
            pl.BlockSpec(memory_space=pltpu.SMEM),
            pl.BlockSpec(memory_space=pltpu.SMEM),
            pl.BlockSpec(memory_space=pltpu.VMEM),
            pl.BlockSpec(memory_space=pltpu.VMEM),
        ],
        out_specs=pl.BlockSpec(memory_space=pltpu.VMEM),
        out_shape=jax.ShapeDtypeStruct((npoint, nsky // npoint, ch, rows, tile), jnp.bfloat16),
        scratch_shapes=[pltpu.VMEM((nsky, ch, rows, tile), jnp.float32)],
        compiler_params=params(),
    )(ids, owner, tiles, floored)


def conv_body(tiles_ref, psf_ref, out_ref):
    tile = psf_ref.shape[-1]
    for c in range(tiles_ref.shape[2]):
        plane = tiles_ref[:, 0, c].reshape(tile, tile)
        left = lax.dot_general(
            plane, psf_ref[c, 1], (((1,), (1,)), ((), ())), preferred_element_type=jnp.float32
        ).astype(jnp.bfloat16)
        out_ref[0, c] = jnp.dot(
            psf_ref[c, 0], left, preferred_element_type=jnp.float32
        ).astype(jnp.bfloat16)


def convolve(tiles, psf):
    npoint, per, ch, rows, tile = tiles.shape
    return pl.pallas_call(
        conv_body,
        grid=(per,),
        in_specs=[
            pl.BlockSpec((npoint, 1, ch, rows, tile), lambda i: (0, i, 0, 0, 0)),
            pl.BlockSpec(psf.shape, lambda i: (0, 0, 0, 0)),
        ],
        out_specs=pl.BlockSpec((1, ch, tile, tile), lambda i: (i, 0, 0, 0)),
        out_shape=jax.ShapeDtypeStruct((per, ch, tile, tile), jnp.bfloat16),
        compiler_params=params(),
    )(tiles, psf)


def shards(images, beam, exponent, intersection, counts, owner, psf):
    pts, slots, ch, tile, _ = images.shape
    npoint = lax.axis_size("point")
    nchan = lax.axis_size("chan")
    s_dev = pts * slots
    part = s_dev // nchan
    nsky = owner.shape[0]
    chan_pos = lax.axis_index("chan")

    live = jnp.arange(slots)[None, :] < counts[:, None]
    own_ids = jnp.where(live, intersection, nsky).reshape(1, s_dev)
    ids = lax.all_to_all(
        jnp.broadcast_to(own_ids, (npoint, s_dev)), "point", split_axis=0, concat_axis=0, tiled=True
    )
    own_beam = lax.dynamic_slice_in_dim(
        beam.reshape(s_dev, tile, tile), chan_pos * part, part, axis=0
    )
    beam_rows = lax.all_to_all(
        split_rows(own_beam, npoint), "point", split_axis=0, concat_axis=0, tiled=True
    )
    own_exp = lax.dynamic_slice_in_dim(exponent, chan_pos * ch, ch)
    weighted = weigh(own_exp, images, beam, npoint)
    tiles = lax.all_to_all(weighted, "point", split_axis=0, concat_axis=0, tiled=True)
    beams = lax.all_gather(beam_rows, "chan", axis=0, tiled=False)
    floored = totals(ids, exponent, beams, nsky)
    ordered = normalise(ids, owner, tiles, floored)
    returned = lax.all_to_all(ordered, "point", split_axis=0, concat_axis=0, tiled=True)
    return convolve(returned, psf)


def solution(mesh):
    return jax.shard_map(
        shards,
        mesh=mesh,
        in_specs=(
            P("point", None, "chan", None, None),
            P("point", None, None, None),
            P(),
            P("point", None),
            P("point"),
            P(),
            P("chan", None, None, None),
        ),
        out_specs=P("point", "chan", None, None),
        check_vma=False,
    )
```

```python
import functools

import jax
import jax.numpy as jnp
from jax import lax
from jax.experimental import pallas as pl
from jax.experimental.pallas import tpu as pltpu
from jax.sharding import PartitionSpec as P

weight_floor = 0.05
VMEM_LIMIT = 48 * 1024 * 1024


def params():
    return pltpu.CompilerParams(vmem_limit_bytes=VMEM_LIMIT)


def put_rows(out_ref, at, value):
    group, rows = out_ref.shape[0], out_ref.shape[-2]
    for g in range(group):
        out_ref[(g,) + at] = value[g * rows:(g + 1) * rows].astype(jnp.bfloat16)


def row_block(tile, npoint):
    rows = tile // npoint
    block = max(rows, 16)
    return rows, block, block // rows


def weight_body(exp_ref, images_ref, beam_ref, out_ref):
    slots = images_ref.shape[1]
    for p in range(images_ref.shape[0]):
        for s in range(slots):
            logs = jnp.log(beam_ref[p, s].astype(jnp.float32))
            for c in range(images_ref.shape[2]):
                power = jnp.exp(exp_ref[c] * logs)
                plane = images_ref[p, s, c].astype(jnp.float32)
                put_rows(out_ref, (p * slots + s, c), power * plane)


def weigh(own_exp, images, beam, npoint):
    pts, slots, ch, tile, _ = images.shape
    rows, block, group = row_block(tile, npoint)
    return pl.pallas_call(
        weight_body,
        grid=(npoint // group,),
        in_specs=[
            pl.BlockSpec(memory_space=pltpu.SMEM),
            pl.BlockSpec((pts, slots, ch, block, tile), lambda i: (0, 0, 0, i, 0)),
            pl.BlockSpec((pts, slots, block, tile), lambda i: (0, 0, i, 0)),
        ],
        out_specs=pl.BlockSpec((group, pts * slots, ch, rows, tile), lambda i: (i, 0, 0, 0, 0)),
        out_shape=jax.ShapeDtypeStruct((npoint, pts * slots, ch, rows, tile), jnp.bfloat16),
        compiler_params=params(),
    )(own_exp, images, beam)


def split_body(beam_ref, out_ref):
    for s in range(beam_ref.shape[0]):
        put_rows(out_ref, (s,), beam_ref[s].astype(jnp.float32))


def split_rows(beam, npoint):
    s, tile, _ = beam.shape
    rows, block, group = row_block(tile, npoint)
    return pl.pallas_call(
        split_body,
        grid=(npoint // group,),
        in_specs=[pl.BlockSpec((s, block, tile), lambda i: (0, i, 0))],
        out_specs=pl.BlockSpec((group, s, rows, tile), lambda i: (i, 0, 0, 0)),
        out_shape=jax.ShapeDtypeStruct((npoint, s, rows, tile), jnp.bfloat16),
        compiler_params=params(),
    )(beam)


def total_body(s_dev, ids_ref, exp_ref, beam_ref, out_ref, acc_ref):
    nchan, npoint, part = beam_ref.shape[:3]
    nsky = out_ref.shape[0]
    ch = exp_ref.shape[0]
    acc_ref[...] = jnp.zeros_like(acc_ref)

    def step(d, carry):
        for share in range(nchan):
            for k in range(part):
                at = ids_ref[d, share * part + k]

                @pl.when(at < nsky)
                def _():
                    logs = jnp.log(beam_ref[share, d, k].astype(jnp.float32))
                    pw = jnp.zeros_like(logs)
                    for c in range(ch):
                        power = jnp.exp(exp_ref[c] * logs)
                        pw = pw + power * power
                    acc_ref[at] += pw * (1.0 / ch)

        return carry

    lax.fori_loop(0, npoint, step, 0)
    out_ref[...] = jnp.maximum(acc_ref[...], weight_floor)


def totals(ids, exponent, beams, nsky):
    rows, tile = beams.shape[3:]
    s_dev = ids.shape[1]
    return pl.pallas_call(
        functools.partial(total_body, s_dev),
        in_specs=[
            pl.BlockSpec(memory_space=pltpu.SMEM),
            pl.BlockSpec(memory_space=pltpu.SMEM),
            pl.BlockSpec(memory_space=pltpu.VMEM),
        ],
        out_specs=pl.BlockSpec(memory_space=pltpu.VMEM),
        out_shape=jax.ShapeDtypeStruct((nsky, rows, tile), jnp.float32),
        scratch_shapes=[pltpu.VMEM((nsky, rows, tile), jnp.float32)],
        compiler_params=params(),
    )(ids, exponent, beams)


def normal_body(ids_ref, owner_ref, tiles_ref, floor_ref, out_ref, acc_ref):
    npoint, s_dev, ch = tiles_ref.shape[:3]
    nsky = floor_ref.shape[0]
    acc_ref[...] = jnp.zeros_like(acc_ref)

    def step(d, carry):
        for s in range(s_dev):
            at = ids_ref[d, s]

            @pl.when(at < nsky)
            def _():
                acc_ref[at] += tiles_ref[d, s].astype(jnp.float32)

        return carry

    lax.fori_loop(0, npoint, step, 0)
    per = out_ref.shape[1]

    def emit(d, carry):
        for k in range(per):
            t = owner_ref[d * per + k]
            inv = floor_ref[t]
            for c in range(ch):
                out_ref[d, k, c] = (acc_ref[t, c] / inv).astype(jnp.bfloat16)
        return carry

    lax.fori_loop(0, npoint, emit, 0)


def normalise(ids, owner, tiles, floored):
    npoint, s_dev, ch, rows, tile = tiles.shape
    nsky = owner.shape[0]
    return pl.pallas_call(
        normal_body,
        in_specs=[
            pl.BlockSpec(memory_space=pltpu.SMEM),
            pl.BlockSpec(memory_space=pltpu.SMEM),
            pl.BlockSpec(memory_space=pltpu.VMEM),
            pl.BlockSpec(memory_space=pltpu.VMEM),
        ],
        out_specs=pl.BlockSpec(memory_space=pltpu.VMEM),
        out_shape=jax.ShapeDtypeStruct((npoint, nsky // npoint, ch, rows, tile), jnp.bfloat16),
        scratch_shapes=[pltpu.VMEM((nsky, ch, rows, tile), jnp.float32)],
        compiler_params=params(),
    )(ids, owner, tiles, floored)


def conv_body(tiles_ref, psf_ref, out_ref):
    tile = psf_ref.shape[-1]
    for c in range(tiles_ref.shape[2]):
        plane = tiles_ref[:, 0, c].reshape(tile, tile)
        left = lax.dot_general(
            plane, psf_ref[c, 1], (((1,), (1,)), ((), ())), preferred_element_type=jnp.float32
        ).astype(jnp.bfloat16)
        out_ref[0, c] = jnp.dot(
            psf_ref[c, 0], left, preferred_element_type=jnp.float32
        ).astype(jnp.bfloat16)


def convolve(tiles, psf):
    npoint, per, ch, rows, tile = tiles.shape
    return pl.pallas_call(
        conv_body,
        grid=(per,),
        in_specs=[
            pl.BlockSpec((npoint, 1, ch, rows, tile), lambda i: (0, i, 0, 0, 0)),
            pl.BlockSpec(psf.shape, lambda i: (0, 0, 0, 0)),
        ],
        out_specs=pl.BlockSpec((1, ch, tile, tile), lambda i: (i, 0, 0, 0)),
        out_shape=jax.ShapeDtypeStruct((per, ch, tile, tile), jnp.bfloat16),
        compiler_params=params(),
    )(tiles, psf)


def row_split_shards(images, beam, exponent, intersection, counts, owner, psf):
    pts, slots, ch, tile, _ = images.shape
    npoint = lax.axis_size("point")
    nchan = lax.axis_size("chan")
    s_dev = pts * slots
    part = s_dev // nchan
    nsky = owner.shape[0]
    chan_pos = lax.axis_index("chan")

    live = jnp.arange(slots)[None, :] < counts[:, None]
    own_ids = jnp.where(live, intersection, nsky).reshape(1, s_dev)
    ids = lax.all_to_all(
        jnp.broadcast_to(own_ids, (npoint, s_dev)), "point", split_axis=0, concat_axis=0, tiled=True
    )
    own_beam = lax.dynamic_slice_in_dim(
        beam.reshape(s_dev, tile, tile), chan_pos * part, part, axis=0
    )
    beam_rows = lax.all_to_all(
        split_rows(own_beam, npoint), "point", split_axis=0, concat_axis=0, tiled=True
    )
    own_exp = lax.dynamic_slice_in_dim(exponent, chan_pos * ch, ch)
    weighted = weigh(own_exp, images, beam, npoint)
    tiles = lax.all_to_all(weighted, "point", split_axis=0, concat_axis=0, tiled=True)
    beams = lax.all_gather(beam_rows, "chan", axis=0, tiled=False)
    floored = totals(ids, exponent, beams, nsky)
    ordered = normalise(ids, owner, tiles, floored)
    returned = lax.all_to_all(ordered, "point", split_axis=0, concat_axis=0, tiled=True)
    return convolve(returned, psf)


INNER = 4


def vmem():
    return pl.BlockSpec(memory_space=pltpu.VMEM)


def smem():
    return pl.BlockSpec(memory_space=pltpu.SMEM)


def quarter_body(here_ref, exp_ref, images_ref, beam_ref, *outs):
    pts, slots, ch, tile, _ = images_ref.shape
    rows, share = outs[INNER].shape[1], outs[0].shape[1]
    inner, chan = here_ref[0], here_ref[1]
    for j in range(INNER):
        base = pl.multiple_of((inner ^ j) * rows, rows)
        half = pl.multiple_of(base + chan * share, share)
        for p in range(pts):

            def step(s, carry):
                at = p * slots + s
                outs[j][at] = beam_ref[p, s, pl.ds(half, share), :]
                logs = jnp.log2(beam_ref[p, s, pl.ds(base, rows), :].astype(jnp.float32))
                for c in range(ch):
                    plane = images_ref[p, s, c, pl.ds(base, rows), :].astype(jnp.float32)
                    power = jnp.exp2(exp_ref[c] * logs)
                    outs[INNER + c * INNER + j][at] = (power * plane).astype(jnp.bfloat16)
                return carry

            lax.fori_loop(0, slots, step, 0)


def quarters(here, own_exp, images, beam, nchan):
    pts, slots, ch, tile, _ = images.shape
    rows = tile // INNER
    s_dev = pts * slots
    out = [jax.ShapeDtypeStruct((s_dev, rows // nchan, tile), jnp.bfloat16)] * INNER
    out += [jax.ShapeDtypeStruct((s_dev, rows, tile), jnp.bfloat16)] * (ch * INNER)
    res = pl.pallas_call(
        quarter_body,
        in_specs=[smem(), smem(), vmem(), vmem()],
        out_specs=[vmem()] * len(out),
        out_shape=out,
        compiler_params=params(),
    )(here, own_exp, images, beam)
    return res[:INNER], [res[INNER + c * INNER:INNER + (c + 1) * INNER] for c in range(ch)]


def pack_body(per_plane, here_ref, pos_ref, *refs):
    got, outs = refs[:INNER], refs[INNER:]
    s_dev = got[0].shape[0]
    inner, plane = here_ref[0], here_ref[2]
    counts = tuple(jnp.int32(0) for _ in outs)
    for j in range(INNER):
        device = plane * INNER + (inner ^ j)

        def step(s, counts):
            dist = (pos_ref[device, s] // per_plane) ^ plane
            nxt = []
            for k, out in enumerate(outs):
                hit = dist == k + 1

                @pl.when(hit)
                def _():
                    out[counts[k]] = got[j][s]

                nxt.append(counts[k] + hit.astype(jnp.int32))
            return tuple(nxt)

        counts = lax.fori_loop(0, s_dev, step, counts)


def pack(here, pos, got, caps, per_plane):
    _, rows, tile = got[0].shape
    return pl.pallas_call(
        functools.partial(pack_body, per_plane),
        in_specs=[smem(), smem()] + [vmem()] * INNER,
        out_specs=[vmem()] * len(caps),
        out_shape=[jax.ShapeDtypeStruct((cap, rows, tile), jnp.bfloat16) for cap in caps],
        compiler_params=params(),
    )(here, pos, *got)


def each_tile(here_ref, pos_ref, got, recv, per_plane, add):
    s_dev = got[0].shape[0]
    inner, plane = here_ref[0], here_ref[2]
    for k in range(len(recv) + 1):
        count = jnp.int32(0)
        for j in range(INNER):
            device = (plane ^ k) * INNER + (inner ^ j)

            def step(s, count):
                row = pos_ref[device, s]
                hit = row // per_plane == plane

                @pl.when(hit)
                def _():
                    add(row - plane * per_plane, got[j][s] if k == 0 else recv[k - 1][count])

                return count + hit.astype(jnp.int32)

            count = lax.fori_loop(0, s_dev, step, count)


def inverse_body(per_plane, here_ref, pos_ref, exp_ref, *refs):
    got, recv, out_ref, acc_ref = refs[:INNER], refs[INNER:-2], refs[-2], refs[-1]
    ch = exp_ref.shape[0]
    acc_ref[...] = jnp.zeros_like(acc_ref)

    def add(t, tile):
        logs = jnp.log2(tile.astype(jnp.float32))
        weight = jnp.zeros_like(logs)
        for c in range(ch):
            power = jnp.exp2(exp_ref[c] * logs)
            weight = weight + power * power
        acc_ref[t] += weight * (1.0 / ch)

    each_tile(here_ref, pos_ref, got, recv, per_plane, add)
    out_ref[...] = (1.0 / jnp.maximum(acc_ref[...], weight_floor)).astype(out_ref.dtype)


def inverse_totals(here, pos, exponent, got, recv, per_plane):
    _, rows, tile = got[0].shape
    shape = (per_plane, rows, tile)
    return pl.pallas_call(
        functools.partial(inverse_body, per_plane),
        in_specs=[smem()] * 3 + [vmem()] * (INNER + len(recv)),
        out_specs=vmem(),
        out_shape=jax.ShapeDtypeStruct(shape, jnp.bfloat16),
        scratch_shapes=[pltpu.VMEM(shape, jnp.float32)],
        compiler_params=params(),
    )(here, pos, exponent, *got, *recv)


def sum_body(per_plane, nrecv, here_ref, pos_ref, *refs):
    got, recv = refs[:INNER], refs[INNER:INNER + nrecv]
    inverse, outs, acc_ref = refs[INNER + nrecv:-1 - INNER], refs[-1 - INNER:-1], refs[-1]
    inner, chan = here_ref[0], here_ref[1]
    share = inverse[0].shape[1]
    per = per_plane // INNER
    acc_ref[...] = jnp.zeros_like(acc_ref)

    def add(t, tile):
        acc_ref[t] += tile.astype(jnp.float32)

    each_tile(here_ref, pos_ref, got, recv, per_plane, add)
    for j in range(INNER):

        def emit(k, carry):
            t = (inner ^ j) * per + k
            for y, inv in enumerate(inverse):
                part = pl.ds(pl.multiple_of((chan ^ y) * share, share), share)
                value = acc_ref[t, part, :] * inv[t].astype(jnp.float32)
                outs[j][k, part, :] = value.astype(jnp.bfloat16)
            return carry

        lax.fori_loop(0, per, emit, 0)


def sum_normal(here, pos, got, recv, inverse, per_plane):
    _, rows, tile = got[0].shape
    return pl.pallas_call(
        functools.partial(sum_body, per_plane, len(recv)),
        in_specs=[smem()] * 2 + [vmem()] * (INNER + len(recv) + len(inverse)),
        out_specs=[vmem()] * INNER,
        out_shape=[jax.ShapeDtypeStruct((per_plane // INNER, rows, tile), jnp.bfloat16)] * INNER,
        scratch_shapes=[pltpu.VMEM((per_plane, rows, tile), jnp.float32)],
        compiler_params=params(),
    )(here, pos, *got, *recv, *inverse)


def plane_conv_body(here_ref, psf_ref, *refs):
    quarter, out_ref, left_ref = refs[:INNER], refs[-2], refs[-1]
    rows = quarter[0].shape[1]
    inner = here_ref[0]
    for j in range(INNER):
        left = lax.dot_general(
            quarter[j][0], psf_ref[0, 1], (((1,), (1,)), ((), ())), preferred_element_type=jnp.float32
        )
        left_ref[pl.ds(pl.multiple_of((inner ^ j) * rows, rows), rows), :] = left.astype(jnp.bfloat16)
    out_ref[0, 0] = jnp.dot(
        psf_ref[0, 0], left_ref[...], preferred_element_type=jnp.float32
    ).astype(jnp.bfloat16)


def plane_convolve(here, psf, quarter, chan, before):
    per, rows, tile = quarter[0].shape
    ch = psf.shape[0]
    extra = [] if before is None else [before]
    return pl.pallas_call(
        plane_conv_body,
        grid=(per,),
        in_specs=[smem(), pl.BlockSpec((1, 2, tile, tile), lambda t: (chan, 0, 0, 0))]
        + [pl.BlockSpec((1, rows, tile), lambda t: (t, 0, 0))] * INNER
        + [pl.BlockSpec(memory_space=pl.ANY)] * len(extra),
        out_specs=pl.BlockSpec((1, 1, tile, tile), lambda t: (t, chan, 0, 0)),
        out_shape=jax.ShapeDtypeStruct((per, ch, tile, tile), jnp.bfloat16),
        scratch_shapes=[pltpu.VMEM((tile, tile), jnp.bfloat16)],
        input_output_aliases={2 + INNER: 0} if extra else {},
        compiler_params=params(),
    )(here, psf, *quarter, *extra)


def swap(value, axis, distance):
    n = lax.axis_size(axis)
    return lax.ppermute(value, axis, [(d, d ^ distance) for d in range(n)])


def inside(parts):
    return [parts[0]] + [swap(parts[j], "point", j) for j in range(1, INNER)]


def between(parts):
    return [swap(part, "point", (k + 1) * INNER) for k, part in enumerate(parts)]


def plane_shards(images, beam, exponent, intersection, counts, owner, psf):
    pts, slots, ch, tile, _ = images.shape
    npoint, nchan = lax.axis_size("point"), lax.axis_size("chan")
    planes = npoint // INNER
    s_dev = pts * slots
    nsky = owner.shape[0]
    per_plane = nsky // planes
    chan_pos, point_pos = lax.axis_index("chan"), lax.axis_index("point")
    here = jnp.stack([point_pos % INNER, chan_pos, point_pos // INNER]).astype(jnp.int32)

    live = jnp.arange(slots)[None, :] < counts[:, None]
    match = intersection[..., None] == owner
    rows = jnp.sum(jnp.where(match, jnp.arange(nsky), 0), axis=-1)
    own_pos = jnp.where(live, rows, nsky).astype(jnp.int32).reshape(1, s_dev)
    pos = lax.all_to_all(
        jnp.broadcast_to(own_pos, (npoint, s_dev)), "point", split_axis=0, concat_axis=0, tiled=True
    )
    own_exp = lax.dynamic_slice_in_dim(exponent, chan_pos * ch, ch)
    beam_parts, weighted = quarters(here, own_exp, images, beam, nchan)

    goes = pos.reshape(planes, 1, INNER * s_dev) // per_plane == jnp.arange(planes)[None, :, None]
    number = jnp.sum(goes.astype(jnp.int32), axis=-1)
    ids = jnp.arange(planes)
    distance = ids[:, None] ^ ids[None, :]
    most = INNER * s_dev
    choices = [(12, 7, 7), (12, 8, 8), (12, 9, 9), (14, 11, 11), (most, most, most)]
    limit = jnp.array([(most,) + c for c in choices[:-1]], jnp.int32)
    over = jnp.any(number[None] > limit[:, distance], axis=(1, 2))
    choice = jnp.sum(over.astype(jnp.int32))

    def branch(caps):
        def run(here, pos, beam_parts, weighted, exponent, psf):
            beams = inside(beam_parts)
            beam_recv = between(pack(here, pos, beams, caps, per_plane))
            inverse = inverse_totals(here, pos, exponent, beams, beam_recv, per_plane)
            inverses = [inverse] + [swap(inverse, "chan", y) for y in range(1, nchan)]
            out = None
            for c in range(ch):
                got = inside(weighted[c])
                recv = between(pack(here, pos, got, caps, per_plane))
                normal = inside(sum_normal(here, pos, got, recv, inverses, per_plane))
                out = plane_convolve(here, psf, normal, c, out)
            return out

        return run

    return lax.switch(
        choice, [branch(c) for c in choices], here, pos, beam_parts, weighted, exponent, psf
    )


def shards(*args):
    if lax.axis_size("point") == 4 * INNER:
        return plane_shards(*args)
    return row_split_shards(*args)


def solution(mesh):
    return jax.shard_map(
        shards,
        mesh=mesh,
        in_specs=(
            P("point", None, "chan", None, None),
            P("point", None, None, None),
            P(),
            P("point", None),
            P("point"),
            P(),
            P("chan", None, None, None),
        ),
        out_specs=P("point", "chan", None, None),
        check_vma=False,
    )
```

```python
import functools

import jax
import jax.numpy as jnp
from jax import lax
from jax.experimental import pallas as pl
from jax.experimental.pallas import tpu as pltpu
from jax.sharding import PartitionSpec as P

weight_floor = 0.05
VMEM_LIMIT = 48 * 1024 * 1024


def params():
    return pltpu.CompilerParams(vmem_limit_bytes=VMEM_LIMIT)


def put_rows(out_ref, at, value):
    group, rows = out_ref.shape[0], out_ref.shape[-2]
    for g in range(group):
        out_ref[(g,) + at] = value[g * rows:(g + 1) * rows].astype(jnp.bfloat16)


def row_block(tile, npoint):
    rows = tile // npoint
    block = max(rows, 16)
    return rows, block, block // rows


def weight_body(exp_ref, images_ref, beam_ref, out_ref):
    slots = images_ref.shape[1]
    for p in range(images_ref.shape[0]):
        for s in range(slots):
            logs = jnp.log(beam_ref[p, s].astype(jnp.float32))
            for c in range(images_ref.shape[2]):
                power = jnp.exp(exp_ref[c] * logs)
                plane = images_ref[p, s, c].astype(jnp.float32)
                put_rows(out_ref, (p * slots + s, c), power * plane)


def weigh(own_exp, images, beam, npoint):
    pts, slots, ch, tile, _ = images.shape
    rows, block, group = row_block(tile, npoint)
    return pl.pallas_call(
        weight_body,
        grid=(npoint // group,),
        in_specs=[
            pl.BlockSpec(memory_space=pltpu.SMEM),
            pl.BlockSpec((pts, slots, ch, block, tile), lambda i: (0, 0, 0, i, 0)),
            pl.BlockSpec((pts, slots, block, tile), lambda i: (0, 0, i, 0)),
        ],
        out_specs=pl.BlockSpec((group, pts * slots, ch, rows, tile), lambda i: (i, 0, 0, 0, 0)),
        out_shape=jax.ShapeDtypeStruct((npoint, pts * slots, ch, rows, tile), jnp.bfloat16),
        compiler_params=params(),
    )(own_exp, images, beam)


def split_body(beam_ref, out_ref):
    for s in range(beam_ref.shape[0]):
        put_rows(out_ref, (s,), beam_ref[s].astype(jnp.float32))


def split_rows(beam, npoint):
    s, tile, _ = beam.shape
    rows, block, group = row_block(tile, npoint)
    return pl.pallas_call(
        split_body,
        grid=(npoint // group,),
        in_specs=[pl.BlockSpec((s, block, tile), lambda i: (0, i, 0))],
        out_specs=pl.BlockSpec((group, s, rows, tile), lambda i: (i, 0, 0, 0)),
        out_shape=jax.ShapeDtypeStruct((npoint, s, rows, tile), jnp.bfloat16),
        compiler_params=params(),
    )(beam)


def total_body(s_dev, ids_ref, exp_ref, beam_ref, out_ref, acc_ref):
    nchan, npoint, part = beam_ref.shape[:3]
    nsky = out_ref.shape[0]
    ch = exp_ref.shape[0]
    acc_ref[...] = jnp.zeros_like(acc_ref)

    def step(d, carry):
        for share in range(nchan):
            for k in range(part):
                at = ids_ref[d, share * part + k]

                @pl.when(at < nsky)
                def _():
                    logs = jnp.log(beam_ref[share, d, k].astype(jnp.float32))
                    pw = jnp.zeros_like(logs)
                    for c in range(ch):
                        power = jnp.exp(exp_ref[c] * logs)
                        pw = pw + power * power
                    acc_ref[at] += pw * (1.0 / ch)

        return carry

    lax.fori_loop(0, npoint, step, 0)
    out_ref[...] = jnp.maximum(acc_ref[...], weight_floor)


def totals(ids, exponent, beams, nsky):
    rows, tile = beams.shape[3:]
    s_dev = ids.shape[1]
    return pl.pallas_call(
        functools.partial(total_body, s_dev),
        in_specs=[
            pl.BlockSpec(memory_space=pltpu.SMEM),
            pl.BlockSpec(memory_space=pltpu.SMEM),
            pl.BlockSpec(memory_space=pltpu.VMEM),
        ],
        out_specs=pl.BlockSpec(memory_space=pltpu.VMEM),
        out_shape=jax.ShapeDtypeStruct((nsky, rows, tile), jnp.float32),
        scratch_shapes=[pltpu.VMEM((nsky, rows, tile), jnp.float32)],
        compiler_params=params(),
    )(ids, exponent, beams)


def normal_body(ids_ref, owner_ref, tiles_ref, floor_ref, out_ref, acc_ref):
    npoint, s_dev, ch = tiles_ref.shape[:3]
    nsky = floor_ref.shape[0]
    acc_ref[...] = jnp.zeros_like(acc_ref)

    def step(d, carry):
        for s in range(s_dev):
            at = ids_ref[d, s]

            @pl.when(at < nsky)
            def _():
                acc_ref[at] += tiles_ref[d, s].astype(jnp.float32)

        return carry

    lax.fori_loop(0, npoint, step, 0)
    per = out_ref.shape[1]

    def emit(d, carry):
        for k in range(per):
            t = owner_ref[d * per + k]
            inv = floor_ref[t]
            for c in range(ch):
                out_ref[d, k, c] = (acc_ref[t, c] / inv).astype(jnp.bfloat16)
        return carry

    lax.fori_loop(0, npoint, emit, 0)


def normalise(ids, owner, tiles, floored):
    npoint, s_dev, ch, rows, tile = tiles.shape
    nsky = owner.shape[0]
    return pl.pallas_call(
        normal_body,
        in_specs=[
            pl.BlockSpec(memory_space=pltpu.SMEM),
            pl.BlockSpec(memory_space=pltpu.SMEM),
            pl.BlockSpec(memory_space=pltpu.VMEM),
            pl.BlockSpec(memory_space=pltpu.VMEM),
        ],
        out_specs=pl.BlockSpec(memory_space=pltpu.VMEM),
        out_shape=jax.ShapeDtypeStruct((npoint, nsky // npoint, ch, rows, tile), jnp.bfloat16),
        scratch_shapes=[pltpu.VMEM((nsky, ch, rows, tile), jnp.float32)],
        compiler_params=params(),
    )(ids, owner, tiles, floored)


def conv_body(tiles_ref, psf_ref, out_ref):
    tile = psf_ref.shape[-1]
    for c in range(tiles_ref.shape[2]):
        plane = tiles_ref[:, 0, c].reshape(tile, tile)
        left = lax.dot_general(
            plane, psf_ref[c, 1], (((1,), (1,)), ((), ())), preferred_element_type=jnp.float32
        ).astype(jnp.bfloat16)
        out_ref[0, c] = jnp.dot(
            psf_ref[c, 0], left, preferred_element_type=jnp.float32
        ).astype(jnp.bfloat16)


def convolve(tiles, psf):
    npoint, per, ch, rows, tile = tiles.shape
    return pl.pallas_call(
        conv_body,
        grid=(per,),
        in_specs=[
            pl.BlockSpec((npoint, 1, ch, rows, tile), lambda i: (0, i, 0, 0, 0)),
            pl.BlockSpec(psf.shape, lambda i: (0, 0, 0, 0)),
        ],
        out_specs=pl.BlockSpec((1, ch, tile, tile), lambda i: (i, 0, 0, 0)),
        out_shape=jax.ShapeDtypeStruct((per, ch, tile, tile), jnp.bfloat16),
        compiler_params=params(),
    )(tiles, psf)


def row_split_shards(images, beam, exponent, intersection, counts, owner, psf):
    pts, slots, ch, tile, _ = images.shape
    npoint = lax.axis_size("point")
    nchan = lax.axis_size("chan")
    s_dev = pts * slots
    part = s_dev // nchan
    nsky = owner.shape[0]
    chan_pos = lax.axis_index("chan")

    live = jnp.arange(slots)[None, :] < counts[:, None]
    own_ids = jnp.where(live, intersection, nsky).reshape(1, s_dev)
    ids = lax.all_to_all(
        jnp.broadcast_to(own_ids, (npoint, s_dev)), "point", split_axis=0, concat_axis=0, tiled=True
    )
    own_beam = lax.dynamic_slice_in_dim(
        beam.reshape(s_dev, tile, tile), chan_pos * part, part, axis=0
    )
    beam_rows = lax.all_to_all(
        split_rows(own_beam, npoint), "point", split_axis=0, concat_axis=0, tiled=True
    )
    own_exp = lax.dynamic_slice_in_dim(exponent, chan_pos * ch, ch)
    weighted = weigh(own_exp, images, beam, npoint)
    tiles = lax.all_to_all(weighted, "point", split_axis=0, concat_axis=0, tiled=True)
    beams = lax.all_gather(beam_rows, "chan", axis=0, tiled=False)
    floored = totals(ids, exponent, beams, nsky)
    ordered = normalise(ids, owner, tiles, floored)
    returned = lax.all_to_all(ordered, "point", split_axis=0, concat_axis=0, tiled=True)
    return convolve(returned, psf)


INNER = 4
PLANES = 4
SEND, OWN, RECV, COUNT = 0, 16, 20, 24
PLAN_ROWS = 32


def vmem():
    return pl.BlockSpec(memory_space=pltpu.VMEM)


def smem():
    return pl.BlockSpec(memory_space=pltpu.SMEM)


def plan_body(limits, here_ref, ids_ref, owner_ref, plan_ref, choice_ref, row_ref, tally_ref):
    s_dev = ids_ref.shape[1]
    nsky = owner_ref.shape[0]
    per_plane = nsky // PLANES
    most = plan_ref.shape[1] - 1
    inner, plane = here_ref[0], here_ref[2]
    row_ref[nsky] = nsky

    def place(r, carry):
        row_ref[owner_ref[r]] = r
        return carry

    lax.fori_loop(0, nsky, place, 0, unroll=8)
    for n in range(PLANES * 2 * PLANES):
        tally_ref[n] = 0
    for k0 in range(PLANES):
        source = plane ^ k0
        for j in range(INNER):
            device = source * INNER + (inner ^ j)
            if k0 == 0:
                for k in range(2 * PLANES):
                    tally_ref[PLANES * 2 * PLANES + k] = 0
            for s in range(s_dev):
                row = row_ref[ids_ref[device, s]]
                far = lax.div(row, per_plane) ^ source
                n = tally_ref[k0 * 2 * PLANES + far]
                tally_ref[k0 * 2 * PLANES + far] = n + 1
                local = row - plane * per_plane
                if k0 > 0:
                    plan_ref[RECV + k0, jnp.where(far == k0, n, most)] = local
                else:
                    m = tally_ref[PLANES * 2 * PLANES + far]
                    tally_ref[PLANES * 2 * PLANES + far] = m + 1
                    known = far < PLANES
                    plan_ref[SEND + j * PLANES + jnp.where(known, far, 0), jnp.where(known, m, most)] = s
                    plan_ref[OWN + j, jnp.where(far == 0, m, most)] = local
            if k0 == 0:
                for k in range(PLANES):
                    plan_ref[COUNT, j * PLANES + k] = tally_ref[PLANES * 2 * PLANES + k]
        plan_ref[COUNT + 1, k0] = tally_ref[k0 * 2 * PLANES + k0]
    choice = jnp.int32(0)
    need = []
    for k in range(1, PLANES):
        value = tally_ref[k]
        for k0 in range(1, PLANES):
            value = jnp.maximum(value, tally_ref[k0 * 2 * PLANES + k])
        need.append(value)
    for caps in limits:
        over = need[0] > caps[0]
        for k in range(1, PLANES - 1):
            over = over | (need[k] > caps[k])
        choice = choice + over.astype(jnp.int32)
    choice_ref[0] = choice


def make_plan(here, ids, owner, limits):
    most = INNER * ids.shape[1]
    return pl.pallas_call(
        functools.partial(plan_body, limits),
        in_specs=[smem()] * 3,
        out_specs=[smem()] * 2,
        out_shape=[
            jax.ShapeDtypeStruct((PLAN_ROWS, most + 1), jnp.int32),
            jax.ShapeDtypeStruct((1,), jnp.int32),
        ],
        scratch_shapes=[
            pltpu.SMEM((owner.shape[0] + 1,), jnp.int32),
            pltpu.SMEM(((PLANES + 1) * 2 * PLANES,), jnp.int32),
        ],
        compiler_params=params(),
    )(here, ids, owner)


def quarter_body(chan, share, here_ref, exp_ref, images_ref, beam_ref, *outs):
    slots, tile = images_ref.shape[1], images_ref.shape[-1]
    rows = tile // INNER
    inner = here_ref[0]
    for j in range(INNER):
        base = pl.multiple_of((inner ^ j) * rows, rows)

        def step(s, carry):
            if share:
                half = pl.multiple_of(base + here_ref[1] * share, share)
                outs[j][s, :share] = beam_ref[0, s, pl.ds(half, share), :]
            logs = jnp.log2(beam_ref[0, s, pl.ds(base, rows), :].astype(jnp.float32))
            plane = images_ref[0, s, 0, pl.ds(base, rows), :].astype(jnp.float32)
            outs[j][s, share:] = (jnp.exp2(exp_ref[chan] * logs) * plane).astype(jnp.bfloat16)
            return carry

        lax.fori_loop(0, slots, step, 0)


def quarters(here, own_exp, images, beam, chan, share):
    pts, slots, ch, tile, _ = images.shape
    rows = tile // INNER + share
    return pl.pallas_call(
        functools.partial(quarter_body, chan, share),
        grid=(pts,),
        in_specs=[
            smem(),
            smem(),
            pl.BlockSpec((1, slots, 1, tile, tile), lambda p: (p, 0, chan, 0, 0)),
            pl.BlockSpec((1, slots, tile, tile), lambda p: (p, 0, 0, 0)),
        ],
        out_specs=[pl.BlockSpec((slots, rows, tile), lambda p: (p, 0, 0))] * INNER,
        out_shape=[jax.ShapeDtypeStruct((pts * slots, rows, tile), jnp.bfloat16)] * INNER,
        compiler_params=params(),
    )(here, own_exp, images, beam)


def pack_body(plan_ref, *refs):
    got, outs = refs[:INNER], refs[INNER:]
    for k, out in enumerate(outs, 1):
        start = jnp.int32(0)
        for j in range(INNER):
            count = plan_ref[COUNT, j * PLANES + k]

            def step(n, carry):
                out[start + n] = got[j][plan_ref[SEND + j * PLANES + k, n]]
                return carry

            lax.fori_loop(0, count, step, 0)
            start = start + count


def pack(plan, got, caps):
    _, rows, tile = got[0].shape
    return pl.pallas_call(
        pack_body,
        in_specs=[smem()] + [vmem()] * INNER,
        out_specs=[vmem()] * len(caps),
        out_shape=[jax.ShapeDtypeStruct((cap, rows, tile), jnp.bfloat16) for cap in caps],
        compiler_params=params(),
    )(plan, *got)


def each_tile(plan_ref, got, recv, lines, add):
    for j in range(INNER):

        def own(n, carry):
            add(plan_ref[OWN + j, n], got[j][plan_ref[SEND + j * PLANES, n], lines, :])
            return carry

        lax.fori_loop(0, plan_ref[COUNT, j * PLANES], own, 0)
    for k, tiles in enumerate(recv, 1):

        def other(n, carry):
            add(plan_ref[RECV + k, n], tiles[n, lines, :])
            return carry

        lax.fori_loop(0, plan_ref[COUNT + 1, k], other, 0)


def inverse_body(share, plan_ref, exp_ref, *refs):
    got, recv, out_ref, acc_ref = refs[:INNER], refs[INNER:-2], refs[-2], refs[-1]
    ch = exp_ref.shape[0]
    acc_ref[...] = jnp.zeros_like(acc_ref)

    def add(t, tile):
        logs = jnp.log2(tile.astype(jnp.float32))
        weight = jnp.zeros_like(logs)
        for c in range(ch):
            weight = weight + jnp.exp2((2.0 * exp_ref[c]) * logs)
        acc_ref[t] += weight * (1.0 / ch)

    each_tile(plan_ref, got, recv, slice(0, share), add)
    out_ref[...] = (1.0 / jnp.maximum(acc_ref[...], weight_floor)).astype(out_ref.dtype)


def inverse_totals(plan, exponent, got, recv, share, per_plane):
    shape = (per_plane, share, got[0].shape[-1])
    return pl.pallas_call(
        functools.partial(inverse_body, share),
        in_specs=[smem()] * 2 + [vmem()] * (INNER + len(recv)),
        out_specs=vmem(),
        out_shape=jax.ShapeDtypeStruct(shape, jnp.bfloat16),
        scratch_shapes=[pltpu.VMEM(shape, jnp.float32)],
        compiler_params=params(),
    )(plan, exponent, *got, *recv)


def sum_body(skip, nrecv, here_ref, plan_ref, *refs):
    got, recv = refs[:INNER], refs[INNER:INNER + nrecv]
    inverse, outs, acc_ref = refs[INNER + nrecv:-1 - INNER], refs[-1 - INNER:-1], refs[-1]
    inner, chan = here_ref[0], here_ref[1]
    share = inverse[0].shape[1]
    per, rows = outs[0].shape[:2]
    acc_ref[...] = jnp.zeros_like(acc_ref)

    def add(t, tile):
        acc_ref[t] += tile.astype(jnp.float32)

    each_tile(plan_ref, got, recv, slice(skip, skip + rows), add)
    for j in range(INNER):

        def emit(k, carry):
            t = (inner ^ j) * per + k
            for y, inv in enumerate(inverse):
                part = pl.ds(pl.multiple_of((chan ^ y) * share, share), share)
                value = acc_ref[t, part, :] * inv[t].astype(jnp.float32)
                outs[j][k, part, :] = value.astype(jnp.bfloat16)
            return carry

        lax.fori_loop(0, per, emit, 0)


def sum_normal(here, plan, got, recv, inverse, skip, per_plane):
    _, rows, tile = got[0].shape
    rows = rows - skip
    return pl.pallas_call(
        functools.partial(sum_body, skip, len(recv)),
        in_specs=[smem()] * 2 + [vmem()] * (INNER + len(recv) + len(inverse)),
        out_specs=[vmem()] * INNER,
        out_shape=[jax.ShapeDtypeStruct((per_plane // INNER, rows, tile), jnp.bfloat16)] * INNER,
        scratch_shapes=[pltpu.VMEM((per_plane, rows, tile), jnp.float32)],
        compiler_params=params(),
    )(here, plan, *got, *recv, *inverse)


def plane_conv_body(here_ref, psf_ref, *refs):
    quarter, out_ref, left_ref = refs[:INNER], refs[-2], refs[-1]
    per, rows, tile = quarter[0].shape
    inner = here_ref[0]
    for j in range(INNER):
        left = lax.dot_general(
            quarter[j][...].reshape(per * rows, tile),
            psf_ref[0, 1],
            (((1,), (1,)), ((), ())),
            preferred_element_type=jnp.float32,
        )
        part = pl.ds(pl.multiple_of((inner ^ j) * rows, rows), rows)
        left_ref[:, part, :] = left.astype(jnp.bfloat16).reshape(per, rows, tile)
    for t in range(per):
        out_ref[t, 0] = jnp.dot(
            psf_ref[0, 0], left_ref[t], preferred_element_type=jnp.float32
        ).astype(jnp.bfloat16)


def plane_convolve(here, psf, quarter, chan, before):
    per, rows, tile = quarter[0].shape
    ch = psf.shape[0]
    extra = [] if before is None else [before]
    block = per // 2
    return pl.pallas_call(
        plane_conv_body,
        grid=(per // block,),
        in_specs=[smem(), pl.BlockSpec((1, 2, tile, tile), lambda t: (chan, 0, 0, 0))]
        + [pl.BlockSpec((block, rows, tile), lambda t: (t, 0, 0))] * INNER
        + [pl.BlockSpec(memory_space=pl.ANY)] * len(extra),
        out_specs=pl.BlockSpec((block, 1, tile, tile), lambda t: (t, chan, 0, 0)),
        out_shape=jax.ShapeDtypeStruct((per, ch, tile, tile), jnp.bfloat16),
        scratch_shapes=[pltpu.VMEM((block, tile, tile), jnp.bfloat16)],
        input_output_aliases={2 + INNER: 0} if extra else {},
        compiler_params=params(),
    )(here, psf, *quarter, *extra)


def swap(value, axis, distance):
    n = lax.axis_size(axis)
    return lax.ppermute(value, axis, [(d, d ^ distance) for d in range(n)])


def inside(parts):
    return [parts[0]] + [swap(parts[j], "point", j) for j in range(1, INNER)]


def between(parts):
    return [swap(part, "point", (k + 1) * INNER) for k, part in enumerate(parts)]


def plane_shards(images, beam, exponent, intersection, counts, owner, psf):
    pts, slots, ch, tile, _ = images.shape
    npoint, nchan = lax.axis_size("point"), lax.axis_size("chan")
    s_dev = pts * slots
    nsky = owner.shape[0]
    per_plane = nsky // PLANES
    share = tile // INNER // nchan
    chan_pos, point_pos = lax.axis_index("chan"), lax.axis_index("point")
    here = jnp.stack([point_pos % INNER, chan_pos, point_pos // INNER]).astype(jnp.int32)
    own_exp = lax.dynamic_slice_in_dim(exponent, chan_pos * ch, ch)

    first = quarters(here, own_exp, images, beam, 0, share)
    live = jnp.arange(slots)[None, :] < counts[:, None]
    own_ids = jnp.where(live, intersection, nsky).reshape(1, s_dev)
    ids = lax.all_to_all(
        jnp.broadcast_to(own_ids, (npoint, s_dev)), "point", split_axis=0, concat_axis=0, tiled=True
    )
    first = inside(first)
    most = INNER * s_dev
    choices = [(12, 7, 7), (12, 8, 8), (12, 9, 9), (14, 11, 11), (most, most, most)]
    plan, choice = make_plan(here, ids, owner, choices[:-1])
    later = [quarters(here, own_exp, images, beam, c, 0) for c in range(1, ch)]

    def branch(caps):
        def run(here, plan, first, later, exponent, psf):
            recv = between(pack(plan, first, caps))
            inverse = inverse_totals(plan, exponent, first, recv, share, per_plane)
            inverses = [inverse] + [swap(inverse, "chan", y) for y in range(1, nchan)]
            normal = inside(sum_normal(here, plan, first, recv, inverses, share, per_plane))
            out = plane_convolve(here, psf, normal, 0, None)
            for c in range(1, ch):
                got = inside(later[c - 1])
                recv = between(pack(plan, got, caps))
                normal = inside(sum_normal(here, plan, got, recv, inverses, 0, per_plane))
                out = plane_convolve(here, psf, normal, c, out)
            return out

        return run

    return lax.switch(choice[0], [branch(c) for c in choices], here, plan, first, later, exponent, psf)


def shards(*args):
    if lax.axis_size("point") == PLANES * INNER:
        return plane_shards(*args)
    return row_split_shards(*args)


def solution(mesh):
    return jax.shard_map(
        shards,
        mesh=mesh,
        in_specs=(
            P("point", None, "chan", None, None),
            P("point", None, None, None),
            P(),
            P("point", None),
            P("point"),
            P(),
            P("chan", None, None, None),
        ),
        out_specs=P("point", "chan", None, None),
        check_vma=False,
    )
```

```python
import functools

import jax
import jax.numpy as jnp
from jax import lax
from jax.experimental import pallas as pl
from jax.experimental.pallas import tpu as pltpu
from jax.sharding import PartitionSpec as P

weight_floor = 0.05
VMEM_LIMIT = 48 * 1024 * 1024


def params():
    return pltpu.CompilerParams(vmem_limit_bytes=VMEM_LIMIT)


def put_rows(out_ref, at, value):
    group, rows = out_ref.shape[0], out_ref.shape[-2]
    for g in range(group):
        out_ref[(g,) + at] = value[g * rows:(g + 1) * rows].astype(jnp.bfloat16)


def row_block(tile, npoint):
    rows = tile // npoint
    block = max(rows, 16)
    return rows, block, block // rows


def weight_body(exp_ref, images_ref, beam_ref, out_ref):
    slots = images_ref.shape[1]
    for p in range(images_ref.shape[0]):
        for s in range(slots):
            logs = jnp.log(beam_ref[p, s].astype(jnp.float32))
            for c in range(images_ref.shape[2]):
                power = jnp.exp(exp_ref[c] * logs)
                plane = images_ref[p, s, c].astype(jnp.float32)
                put_rows(out_ref, (p * slots + s, c), power * plane)


def weigh(own_exp, images, beam, npoint):
    pts, slots, ch, tile, _ = images.shape
    rows, block, group = row_block(tile, npoint)
    return pl.pallas_call(
        weight_body,
        grid=(npoint // group,),
        in_specs=[
            pl.BlockSpec(memory_space=pltpu.SMEM),
            pl.BlockSpec((pts, slots, ch, block, tile), lambda i: (0, 0, 0, i, 0)),
            pl.BlockSpec((pts, slots, block, tile), lambda i: (0, 0, i, 0)),
        ],
        out_specs=pl.BlockSpec((group, pts * slots, ch, rows, tile), lambda i: (i, 0, 0, 0, 0)),
        out_shape=jax.ShapeDtypeStruct((npoint, pts * slots, ch, rows, tile), jnp.bfloat16),
        compiler_params=params(),
    )(own_exp, images, beam)


def split_body(beam_ref, out_ref):
    for s in range(beam_ref.shape[0]):
        put_rows(out_ref, (s,), beam_ref[s].astype(jnp.float32))


def split_rows(beam, npoint):
    s, tile, _ = beam.shape
    rows, block, group = row_block(tile, npoint)
    return pl.pallas_call(
        split_body,
        grid=(npoint // group,),
        in_specs=[pl.BlockSpec((s, block, tile), lambda i: (0, i, 0))],
        out_specs=pl.BlockSpec((group, s, rows, tile), lambda i: (i, 0, 0, 0)),
        out_shape=jax.ShapeDtypeStruct((npoint, s, rows, tile), jnp.bfloat16),
        compiler_params=params(),
    )(beam)


def total_body(s_dev, ids_ref, exp_ref, beam_ref, out_ref, acc_ref):
    nchan, npoint, part = beam_ref.shape[:3]
    nsky = out_ref.shape[0]
    ch = exp_ref.shape[0]
    acc_ref[...] = jnp.zeros_like(acc_ref)

    def step(d, carry):
        for share in range(nchan):
            for k in range(part):
                at = ids_ref[d, share * part + k]

                @pl.when(at < nsky)
                def _():
                    logs = jnp.log(beam_ref[share, d, k].astype(jnp.float32))
                    pw = jnp.zeros_like(logs)
                    for c in range(ch):
                        power = jnp.exp(exp_ref[c] * logs)
                        pw = pw + power * power
                    acc_ref[at] += pw * (1.0 / ch)

        return carry

    lax.fori_loop(0, npoint, step, 0)
    out_ref[...] = jnp.maximum(acc_ref[...], weight_floor)


def totals(ids, exponent, beams, nsky):
    rows, tile = beams.shape[3:]
    s_dev = ids.shape[1]
    return pl.pallas_call(
        functools.partial(total_body, s_dev),
        in_specs=[
            pl.BlockSpec(memory_space=pltpu.SMEM),
            pl.BlockSpec(memory_space=pltpu.SMEM),
            pl.BlockSpec(memory_space=pltpu.VMEM),
        ],
        out_specs=pl.BlockSpec(memory_space=pltpu.VMEM),
        out_shape=jax.ShapeDtypeStruct((nsky, rows, tile), jnp.float32),
        scratch_shapes=[pltpu.VMEM((nsky, rows, tile), jnp.float32)],
        compiler_params=params(),
    )(ids, exponent, beams)


def normal_body(ids_ref, owner_ref, tiles_ref, floor_ref, out_ref, acc_ref):
    npoint, s_dev, ch = tiles_ref.shape[:3]
    nsky = floor_ref.shape[0]
    acc_ref[...] = jnp.zeros_like(acc_ref)

    def step(d, carry):
        for s in range(s_dev):
            at = ids_ref[d, s]

            @pl.when(at < nsky)
            def _():
                acc_ref[at] += tiles_ref[d, s].astype(jnp.float32)

        return carry

    lax.fori_loop(0, npoint, step, 0)
    per = out_ref.shape[1]

    def emit(d, carry):
        for k in range(per):
            t = owner_ref[d * per + k]
            inv = floor_ref[t]
            for c in range(ch):
                out_ref[d, k, c] = (acc_ref[t, c] / inv).astype(jnp.bfloat16)
        return carry

    lax.fori_loop(0, npoint, emit, 0)


def normalise(ids, owner, tiles, floored):
    npoint, s_dev, ch, rows, tile = tiles.shape
    nsky = owner.shape[0]
    return pl.pallas_call(
        normal_body,
        in_specs=[
            pl.BlockSpec(memory_space=pltpu.SMEM),
            pl.BlockSpec(memory_space=pltpu.SMEM),
            pl.BlockSpec(memory_space=pltpu.VMEM),
            pl.BlockSpec(memory_space=pltpu.VMEM),
        ],
        out_specs=pl.BlockSpec(memory_space=pltpu.VMEM),
        out_shape=jax.ShapeDtypeStruct((npoint, nsky // npoint, ch, rows, tile), jnp.bfloat16),
        scratch_shapes=[pltpu.VMEM((nsky, ch, rows, tile), jnp.float32)],
        compiler_params=params(),
    )(ids, owner, tiles, floored)


def conv_body(tiles_ref, psf_ref, out_ref):
    tile = psf_ref.shape[-1]
    for c in range(tiles_ref.shape[2]):
        plane = tiles_ref[:, 0, c].reshape(tile, tile)
        left = lax.dot_general(
            plane, psf_ref[c, 1], (((1,), (1,)), ((), ())), preferred_element_type=jnp.float32
        ).astype(jnp.bfloat16)
        out_ref[0, c] = jnp.dot(
            psf_ref[c, 0], left, preferred_element_type=jnp.float32
        ).astype(jnp.bfloat16)


def convolve(tiles, psf):
    npoint, per, ch, rows, tile = tiles.shape
    return pl.pallas_call(
        conv_body,
        grid=(per,),
        in_specs=[
            pl.BlockSpec((npoint, 1, ch, rows, tile), lambda i: (0, i, 0, 0, 0)),
            pl.BlockSpec(psf.shape, lambda i: (0, 0, 0, 0)),
        ],
        out_specs=pl.BlockSpec((1, ch, tile, tile), lambda i: (i, 0, 0, 0)),
        out_shape=jax.ShapeDtypeStruct((per, ch, tile, tile), jnp.bfloat16),
        compiler_params=params(),
    )(tiles, psf)


def row_split_shards(images, beam, exponent, intersection, counts, owner, psf):
    pts, slots, ch, tile, _ = images.shape
    npoint = lax.axis_size("point")
    nchan = lax.axis_size("chan")
    s_dev = pts * slots
    part = s_dev // nchan
    nsky = owner.shape[0]
    chan_pos = lax.axis_index("chan")

    live = jnp.arange(slots)[None, :] < counts[:, None]
    own_ids = jnp.where(live, intersection, nsky).reshape(1, s_dev)
    ids = lax.all_to_all(
        jnp.broadcast_to(own_ids, (npoint, s_dev)), "point", split_axis=0, concat_axis=0, tiled=True
    )
    own_beam = lax.dynamic_slice_in_dim(
        beam.reshape(s_dev, tile, tile), chan_pos * part, part, axis=0
    )
    beam_rows = lax.all_to_all(
        split_rows(own_beam, npoint), "point", split_axis=0, concat_axis=0, tiled=True
    )
    own_exp = lax.dynamic_slice_in_dim(exponent, chan_pos * ch, ch)
    weighted = weigh(own_exp, images, beam, npoint)
    tiles = lax.all_to_all(weighted, "point", split_axis=0, concat_axis=0, tiled=True)
    beams = lax.all_gather(beam_rows, "chan", axis=0, tiled=False)
    floored = totals(ids, exponent, beams, nsky)
    ordered = normalise(ids, owner, tiles, floored)
    returned = lax.all_to_all(ordered, "point", split_axis=0, concat_axis=0, tiled=True)
    return convolve(returned, psf)


INNER = 4
PLANES = 4
SEND, OWN, RECV, COUNT = 0, 16, 20, 24
PLAN_ROWS = 32
NEAR = 12
FAR = (6, 8, 10)
WIDE = 14


def vmem():
    return pl.BlockSpec(memory_space=pltpu.VMEM)


def smem():
    return pl.BlockSpec(memory_space=pltpu.SMEM)


def plan_body(here_ref, ids_ref, owner_ref, plan_ref, choice_ref, row_ref, tally_ref):
    s_dev = ids_ref.shape[1]
    nsky = owner_ref.shape[0]
    per_plane = nsky // PLANES
    most = plan_ref.shape[1] - 1
    wide = 2 * PLANES
    local_tally = PLANES * wide
    plane = here_ref[1]
    row_ref[nsky] = nsky

    def place(r, carry):
        row_ref[owner_ref[r]] = r
        return carry

    lax.fori_loop(0, nsky, place, 0, unroll=8)
    for n in range(PLANES * wide):
        tally_ref[n] = 0
    for k0 in range(PLANES):
        source = plane ^ k0
        for a in range(INNER):
            if k0 == 0:
                for k in range(wide):
                    tally_ref[local_tally + k] = 0
            for s in range(s_dev):
                row = row_ref[ids_ref[source * INNER + a, s]]
                far = lax.div(row, per_plane) ^ source
                n = tally_ref[k0 * wide + far]
                tally_ref[k0 * wide + far] = n + 1
                local = row - plane * per_plane
                if k0 > 0:
                    plan_ref[RECV + k0, jnp.where(far == k0, n, most)] = local
                else:
                    m = tally_ref[local_tally + far]
                    tally_ref[local_tally + far] = m + 1
                    known = far < PLANES
                    line = SEND + a * PLANES + jnp.where(known, far, 0)
                    plan_ref[line, jnp.where(known, m, most)] = s
                    plan_ref[OWN + a, jnp.where(far == 0, m, most)] = local
            if k0 == 0:
                for k in range(PLANES):
                    plan_ref[COUNT, a * PLANES + k] = tally_ref[local_tally + k]
        plan_ref[COUNT + 1, k0] = tally_ref[k0 * wide + k0]
    need = []
    for k in range(1, PLANES):
        value = tally_ref[k]
        for k0 in range(1, PLANES):
            value = jnp.maximum(value, tally_ref[k0 * wide + k])
        need.append(value)
    steps = len(FAR)
    choice = jnp.int32(0)
    for cap in FAR[:-1]:
        choice = choice + jnp.where(need[1] > cap, steps, 0) + jnp.where(need[2] > cap, 1, 0)
    far = jnp.maximum(need[1], need[2])
    over = (need[0] > NEAR) | (far > FAR[-1])
    choice = jnp.where(over, steps * steps, choice)
    choice = jnp.where(jnp.maximum(need[0], far) > WIDE, steps * steps + 1, choice)
    choice_ref[0] = choice


def capacities(most):
    return [(NEAR, a, b) for a in FAR for b in FAR] + [(WIDE,) * 3, (most,) * 3]


def make_plan(here, ids, owner):
    most = INNER * ids.shape[1]
    return pl.pallas_call(
        plan_body,
        in_specs=[smem()] * 3,
        out_specs=[smem()] * 2,
        out_shape=[
            jax.ShapeDtypeStruct((PLAN_ROWS, most + 1), jnp.int32),
            jax.ShapeDtypeStruct((1,), jnp.int32),
        ],
        scratch_shapes=[
            pltpu.SMEM((owner.shape[0] + 1,), jnp.int32),
            pltpu.SMEM(((PLANES + 1) * 2 * PLANES,), jnp.int32),
        ],
        compiler_params=params(),
    )(here, ids, owner)


def share_body(here_ref, beam_ref, out_ref):
    pts, slots = beam_ref.shape[:2]
    share = out_ref.shape[2]
    part = pl.ds(pl.multiple_of(here_ref[0] * share, share), share)
    for p in range(pts):
        for s in range(slots):
            out_ref[0, p * slots + s] = beam_ref[p, s, part, :]


def beam_shares(here, beam, share):
    pts, slots, tile, _ = beam.shape
    return pl.pallas_call(
        share_body,
        grid=(INNER,),
        in_specs=[smem(), pl.BlockSpec((pts, slots, tile // INNER, tile), lambda q: (0, 0, q, 0))],
        out_specs=pl.BlockSpec((1, pts * slots, share, tile), lambda q: (q, 0, 0, 0)),
        out_shape=jax.ShapeDtypeStruct((INNER, pts * slots, share, tile), jnp.bfloat16),
        compiler_params=params(),
    )(here, beam)


def quarter_body(exp_ref, images_ref, beam_ref, *outs):
    pts, slots = images_ref.shape[:2]
    for p in range(pts):

        def step(s, carry):
            logs = jnp.log2(beam_ref[p, s].astype(jnp.float32))
            for c, out in enumerate(outs):
                plane = images_ref[p, s, c].astype(jnp.float32)
                out[0, p * slots + s] = (jnp.exp2(exp_ref[c] * logs) * plane).astype(jnp.bfloat16)
            return carry

        lax.fori_loop(0, slots, step, 0)


def quarters(own_exp, images, beam):
    pts, slots, ch, tile, _ = images.shape
    rows = tile // INNER
    return pl.pallas_call(
        quarter_body,
        grid=(INNER,),
        in_specs=[
            smem(),
            pl.BlockSpec((pts, slots, ch, rows, tile), lambda q: (0, 0, 0, q, 0)),
            pl.BlockSpec((pts, slots, rows, tile), lambda q: (0, 0, q, 0)),
        ],
        out_specs=[pl.BlockSpec((1, pts * slots, rows, tile), lambda q: (q, 0, 0, 0))] * ch,
        out_shape=[jax.ShapeDtypeStruct((INNER, pts * slots, rows, tile), jnp.bfloat16)] * ch,
        compiler_params=params(),
    )(own_exp, images, beam)


def pack_body(plan_ref, got, *outs):
    for k, out in enumerate(outs, 1):
        start = jnp.int32(0)
        for a in range(INNER):
            count = plan_ref[COUNT, a * PLANES + k]

            def step(n, carry):
                out[start + n] = got[a, plan_ref[SEND + a * PLANES + k, n]]
                return carry

            lax.fori_loop(0, count, step, 0)
            start = start + count


def pack(plan, got, caps):
    rows, tile = got.shape[2:]
    return pl.pallas_call(
        pack_body,
        in_specs=[smem(), vmem()],
        out_specs=[vmem()] * len(caps),
        out_shape=[jax.ShapeDtypeStruct((cap, rows, tile), jnp.bfloat16) for cap in caps],
        compiler_params=params(),
    )(plan, got)


def each_tile(plan_ref, got, recv, add):
    for a in range(INNER):

        def own(n, carry):
            add(plan_ref[OWN + a, n], got[a, plan_ref[SEND + a * PLANES, n]])
            return carry

        lax.fori_loop(0, plan_ref[COUNT, a * PLANES], own, 0)
    for k, tiles in enumerate(recv, 1):

        def other(n, carry):
            add(plan_ref[RECV + k, n], tiles[n])
            return carry

        lax.fori_loop(0, plan_ref[COUNT + 1, k], other, 0)


def inverse_body(plan_ref, exp_ref, got, *refs):
    recv, out_ref, acc_ref = refs[:-2], refs[-2], refs[-1]
    ch = exp_ref.shape[0]
    acc_ref[...] = jnp.zeros_like(acc_ref)

    def add(t, tile):
        logs = jnp.log2(tile.astype(jnp.float32))
        weight = jnp.zeros_like(logs)
        for c in range(ch):
            weight = weight + jnp.exp2((2.0 * exp_ref[c]) * logs)
        acc_ref[t] += weight * (1.0 / ch)

    each_tile(plan_ref, got, recv, add)
    out_ref[...] = (1.0 / jnp.maximum(acc_ref[...], weight_floor)).astype(out_ref.dtype)


def inverse_totals(plan, exponent, got, recv, per_plane):
    shape = (per_plane,) + got.shape[2:]
    return pl.pallas_call(
        inverse_body,
        in_specs=[smem()] * 2 + [vmem()] * (1 + len(recv)),
        out_specs=vmem(),
        out_shape=jax.ShapeDtypeStruct(shape, jnp.bfloat16),
        scratch_shapes=[pltpu.VMEM(shape, jnp.float32)],
        compiler_params=params(),
    )(plan, exponent, got, *recv)


def sum_body(nrecv, here_ref, plan_ref, got, *refs):
    recv, inverse, out_ref, acc_ref = refs[:nrecv], refs[nrecv:-2], refs[-2], refs[-1]
    chan = here_ref[0]
    share = inverse[0].shape[1]
    per = out_ref.shape[1]
    acc_ref[...] = jnp.zeros_like(acc_ref)

    def add(t, tile):
        acc_ref[t] += tile.astype(jnp.float32)

    each_tile(plan_ref, got, recv, add)
    for a in range(INNER):

        def emit(k, carry):
            t = a * per + k
            for y, inv in enumerate(inverse):
                part = pl.ds(pl.multiple_of((chan ^ y) * share, share), share)
                value = acc_ref[t, part, :] * inv[t].astype(jnp.float32)
                out_ref[a, k, part, :] = value.astype(jnp.bfloat16)
            return carry

        lax.fori_loop(0, per, emit, 0)


def sum_normal(here, plan, got, recv, inverse, per_plane):
    rows, tile = got.shape[2:]
    return pl.pallas_call(
        functools.partial(sum_body, len(recv)),
        in_specs=[smem()] * 2 + [vmem()] * (1 + len(recv) + len(inverse)),
        out_specs=vmem(),
        out_shape=jax.ShapeDtypeStruct((INNER, per_plane // INNER, rows, tile), jnp.bfloat16),
        scratch_shapes=[pltpu.VMEM((per_plane, rows, tile), jnp.float32)],
        compiler_params=params(),
    )(here, plan, got, *recv, *inverse)


def plane_conv_body(psf_ref, quarter_ref, *refs):
    out_ref, left_ref = refs[-2], refs[-1]
    _, per, rows, tile = quarter_ref.shape
    for a in range(INNER):
        left = lax.dot_general(
            quarter_ref[a].reshape(per * rows, tile),
            psf_ref[0, 1],
            (((1,), (1,)), ((), ())),
            preferred_element_type=jnp.float32,
        )
        left_ref[:, a * rows:(a + 1) * rows, :] = left.astype(jnp.bfloat16).reshape(per, rows, tile)
    for t in range(per):
        out_ref[t, 0] = jnp.dot(
            psf_ref[0, 0], left_ref[t], preferred_element_type=jnp.float32
        ).astype(jnp.bfloat16)


def plane_convolve(psf, quarter, chan, before):
    _, per, rows, tile = quarter.shape
    ch = psf.shape[0]
    extra = [] if before is None else [before]
    block = per // 2
    return pl.pallas_call(
        plane_conv_body,
        grid=(per // block,),
        in_specs=[
            pl.BlockSpec((1, 2, tile, tile), lambda t: (chan, 0, 0, 0)),
            pl.BlockSpec((INNER, block, rows, tile), lambda t: (0, t, 0, 0)),
        ]
        + [pl.BlockSpec(memory_space=pl.ANY)] * len(extra),
        out_specs=pl.BlockSpec((block, 1, tile, tile), lambda t: (t, chan, 0, 0)),
        out_shape=jax.ShapeDtypeStruct((per, ch, tile, tile), jnp.bfloat16),
        scratch_shapes=[pltpu.VMEM((block, tile, tile), jnp.bfloat16)],
        input_output_aliases={2: 0} if extra else {},
        compiler_params=params(),
    )(psf, quarter, *extra)


def swap(value, axis, distance):
    n = lax.axis_size(axis)
    return lax.ppermute(value, axis, [(d, d ^ distance) for d in range(n)])


def inside(parts):
    groups = [[p * INNER + a for a in range(INNER)] for p in range(PLANES)]
    return lax.all_to_all(
        parts, "point", split_axis=0, concat_axis=0, axis_index_groups=groups, tiled=True
    )


def between(parts):
    return [swap(part, "point", (k + 1) * INNER) for k, part in enumerate(parts)]


def plane_shards(images, beam, exponent, intersection, counts, owner, psf):
    pts, slots, ch, tile, _ = images.shape
    npoint, nchan = lax.axis_size("point"), lax.axis_size("chan")
    s_dev = pts * slots
    nsky = owner.shape[0]
    per_plane = nsky // PLANES
    share = tile // INNER // nchan
    chan_pos, point_pos = lax.axis_index("chan"), lax.axis_index("point")
    here = jnp.stack([chan_pos, point_pos // INNER]).astype(jnp.int32)
    own_exp = lax.dynamic_slice_in_dim(exponent, chan_pos * ch, ch)

    live = jnp.arange(slots)[None, :] < counts[:, None]
    own_ids = jnp.where(live, intersection, nsky).reshape(1, s_dev)
    ids = lax.all_to_all(
        jnp.broadcast_to(own_ids, (npoint, s_dev)), "point", split_axis=0, concat_axis=0, tiled=True
    )
    beams = inside(beam_shares(here, beam, share))
    weighted = quarters(own_exp, images, beam)
    plan, choice = make_plan(here, ids, owner)

    def branch(caps):
        def run(here, plan, beams, weighted, exponent, psf):
            beam_recv = between(pack(plan, beams, caps))
            got, recv = [], []
            earlier = beam_recv
            for c in range(ch):
                parts = weighted[c]
                if c:
                    parts, got[-1] = lax.optimization_barrier((parts, got[-1]))
                got.append(inside(parts))
                packed, earlier = lax.optimization_barrier((pack(plan, got[c], caps), earlier))
                if c:
                    recv[-1] = earlier
                else:
                    beam_recv = earlier
                earlier = between(packed)
                recv.append(earlier)
            inverse = inverse_totals(plan, exponent, beams, beam_recv, per_plane)
            inverses = [inverse] + [swap(inverse, "chan", y) for y in range(1, nchan)]
            out = None
            for c in range(ch):
                normal = inside(sum_normal(here, plan, got[c], recv[c], inverses, per_plane))
                out = plane_convolve(psf, normal, c, out)
            return out

        return run

    branches = [branch(caps) for caps in capacities(INNER * s_dev)]
    return lax.switch(choice[0], branches, here, plan, beams, weighted, exponent, psf)


def shards(*args):
    if lax.axis_size("point") == PLANES * INNER:
        return plane_shards(*args)
    return row_split_shards(*args)


def solution(mesh):
    return jax.shard_map(
        shards,
        mesh=mesh,
        in_specs=(
            P("point", None, "chan", None, None),
            P("point", None, None, None),
            P(),
            P("point", None),
            P("point"),
            P(),
            P("chan", None, None, None),
        ),
        out_specs=P("point", "chan", None, None),
        check_vma=False,
    )
```

```python
import functools

import jax
import jax.numpy as jnp
from jax import lax
from jax.experimental import pallas as pl
from jax.experimental.pallas import tpu as pltpu
from jax.sharding import PartitionSpec as P

weight_floor = 0.05
VMEM_LIMIT = 48 * 1024 * 1024


def params():
    return pltpu.CompilerParams(vmem_limit_bytes=VMEM_LIMIT)


def put_rows(out_ref, at, value):
    group, rows = out_ref.shape[0], out_ref.shape[-2]
    for g in range(group):
        out_ref[(g,) + at] = value[g * rows:(g + 1) * rows].astype(jnp.bfloat16)


def row_block(tile, npoint):
    rows = tile // npoint
    block = max(rows, 16)
    return rows, block, block // rows


def weight_body(exp_ref, images_ref, beam_ref, out_ref):
    slots = images_ref.shape[1]
    for p in range(images_ref.shape[0]):
        for s in range(slots):
            logs = jnp.log(beam_ref[p, s].astype(jnp.float32))
            for c in range(images_ref.shape[2]):
                power = jnp.exp(exp_ref[c] * logs)
                plane = images_ref[p, s, c].astype(jnp.float32)
                put_rows(out_ref, (p * slots + s, c), power * plane)


def weigh(own_exp, images, beam, npoint):
    pts, slots, ch, tile, _ = images.shape
    rows, block, group = row_block(tile, npoint)
    return pl.pallas_call(
        weight_body,
        grid=(npoint // group,),
        in_specs=[
            pl.BlockSpec(memory_space=pltpu.SMEM),
            pl.BlockSpec((pts, slots, ch, block, tile), lambda i: (0, 0, 0, i, 0)),
            pl.BlockSpec((pts, slots, block, tile), lambda i: (0, 0, i, 0)),
        ],
        out_specs=pl.BlockSpec((group, pts * slots, ch, rows, tile), lambda i: (i, 0, 0, 0, 0)),
        out_shape=jax.ShapeDtypeStruct((npoint, pts * slots, ch, rows, tile), jnp.bfloat16),
        compiler_params=params(),
    )(own_exp, images, beam)


def split_body(beam_ref, out_ref):
    for s in range(beam_ref.shape[0]):
        put_rows(out_ref, (s,), beam_ref[s].astype(jnp.float32))


def split_rows(beam, npoint):
    s, tile, _ = beam.shape
    rows, block, group = row_block(tile, npoint)
    return pl.pallas_call(
        split_body,
        grid=(npoint // group,),
        in_specs=[pl.BlockSpec((s, block, tile), lambda i: (0, i, 0))],
        out_specs=pl.BlockSpec((group, s, rows, tile), lambda i: (i, 0, 0, 0)),
        out_shape=jax.ShapeDtypeStruct((npoint, s, rows, tile), jnp.bfloat16),
        compiler_params=params(),
    )(beam)


def total_body(s_dev, ids_ref, exp_ref, beam_ref, out_ref, acc_ref):
    nchan, npoint, part = beam_ref.shape[:3]
    nsky = out_ref.shape[0]
    ch = exp_ref.shape[0]
    acc_ref[...] = jnp.zeros_like(acc_ref)

    def step(d, carry):
        for share in range(nchan):
            for k in range(part):
                at = ids_ref[d, share * part + k]

                @pl.when(at < nsky)
                def _():
                    logs = jnp.log(beam_ref[share, d, k].astype(jnp.float32))
                    pw = jnp.zeros_like(logs)
                    for c in range(ch):
                        power = jnp.exp(exp_ref[c] * logs)
                        pw = pw + power * power
                    acc_ref[at] += pw * (1.0 / ch)

        return carry

    lax.fori_loop(0, npoint, step, 0)
    out_ref[...] = jnp.maximum(acc_ref[...], weight_floor)


def totals(ids, exponent, beams, nsky):
    rows, tile = beams.shape[3:]
    s_dev = ids.shape[1]
    return pl.pallas_call(
        functools.partial(total_body, s_dev),
        in_specs=[
            pl.BlockSpec(memory_space=pltpu.SMEM),
            pl.BlockSpec(memory_space=pltpu.SMEM),
            pl.BlockSpec(memory_space=pltpu.VMEM),
        ],
        out_specs=pl.BlockSpec(memory_space=pltpu.VMEM),
        out_shape=jax.ShapeDtypeStruct((nsky, rows, tile), jnp.float32),
        scratch_shapes=[pltpu.VMEM((nsky, rows, tile), jnp.float32)],
        compiler_params=params(),
    )(ids, exponent, beams)


def normal_body(ids_ref, owner_ref, tiles_ref, floor_ref, out_ref, acc_ref):
    npoint, s_dev, ch = tiles_ref.shape[:3]
    nsky = floor_ref.shape[0]
    acc_ref[...] = jnp.zeros_like(acc_ref)

    def step(d, carry):
        for s in range(s_dev):
            at = ids_ref[d, s]

            @pl.when(at < nsky)
            def _():
                acc_ref[at] += tiles_ref[d, s].astype(jnp.float32)

        return carry

    lax.fori_loop(0, npoint, step, 0)
    per = out_ref.shape[1]

    def emit(d, carry):
        for k in range(per):
            t = owner_ref[d * per + k]
            inv = floor_ref[t]
            for c in range(ch):
                out_ref[d, k, c] = (acc_ref[t, c] / inv).astype(jnp.bfloat16)
        return carry

    lax.fori_loop(0, npoint, emit, 0)


def normalise(ids, owner, tiles, floored):
    npoint, s_dev, ch, rows, tile = tiles.shape
    nsky = owner.shape[0]
    return pl.pallas_call(
        normal_body,
        in_specs=[
            pl.BlockSpec(memory_space=pltpu.SMEM),
            pl.BlockSpec(memory_space=pltpu.SMEM),
            pl.BlockSpec(memory_space=pltpu.VMEM),
            pl.BlockSpec(memory_space=pltpu.VMEM),
        ],
        out_specs=pl.BlockSpec(memory_space=pltpu.VMEM),
        out_shape=jax.ShapeDtypeStruct((npoint, nsky // npoint, ch, rows, tile), jnp.bfloat16),
        scratch_shapes=[pltpu.VMEM((nsky, ch, rows, tile), jnp.float32)],
        compiler_params=params(),
    )(ids, owner, tiles, floored)


def conv_body(tiles_ref, psf_ref, out_ref):
    tile = psf_ref.shape[-1]
    for c in range(tiles_ref.shape[2]):
        plane = tiles_ref[:, 0, c].reshape(tile, tile)
        left = lax.dot_general(
            plane, psf_ref[c, 1], (((1,), (1,)), ((), ())), preferred_element_type=jnp.float32
        ).astype(jnp.bfloat16)
        out_ref[0, c] = jnp.dot(
            psf_ref[c, 0], left, preferred_element_type=jnp.float32
        ).astype(jnp.bfloat16)


def convolve(tiles, psf):
    npoint, per, ch, rows, tile = tiles.shape
    return pl.pallas_call(
        conv_body,
        grid=(per,),
        in_specs=[
            pl.BlockSpec((npoint, 1, ch, rows, tile), lambda i: (0, i, 0, 0, 0)),
            pl.BlockSpec(psf.shape, lambda i: (0, 0, 0, 0)),
        ],
        out_specs=pl.BlockSpec((1, ch, tile, tile), lambda i: (i, 0, 0, 0)),
        out_shape=jax.ShapeDtypeStruct((per, ch, tile, tile), jnp.bfloat16),
        compiler_params=params(),
    )(tiles, psf)


def row_split_shards(images, beam, exponent, intersection, counts, owner, psf):
    pts, slots, ch, tile, _ = images.shape
    npoint = lax.axis_size("point")
    nchan = lax.axis_size("chan")
    s_dev = pts * slots
    part = s_dev // nchan
    nsky = owner.shape[0]
    chan_pos = lax.axis_index("chan")

    live = jnp.arange(slots)[None, :] < counts[:, None]
    own_ids = jnp.where(live, intersection, nsky).reshape(1, s_dev)
    ids = lax.all_to_all(
        jnp.broadcast_to(own_ids, (npoint, s_dev)), "point", split_axis=0, concat_axis=0, tiled=True
    )
    own_beam = lax.dynamic_slice_in_dim(
        beam.reshape(s_dev, tile, tile), chan_pos * part, part, axis=0
    )
    beam_rows = lax.all_to_all(
        split_rows(own_beam, npoint), "point", split_axis=0, concat_axis=0, tiled=True
    )
    own_exp = lax.dynamic_slice_in_dim(exponent, chan_pos * ch, ch)
    weighted = weigh(own_exp, images, beam, npoint)
    tiles = lax.all_to_all(weighted, "point", split_axis=0, concat_axis=0, tiled=True)
    beams = lax.all_gather(beam_rows, "chan", axis=0, tiled=False)
    floored = totals(ids, exponent, beams, nsky)
    ordered = normalise(ids, owner, tiles, floored)
    returned = lax.all_to_all(ordered, "point", split_axis=0, concat_axis=0, tiled=True)
    return convolve(returned, psf)


INNER = 4
PLANES = 4
SEND, OWN, RECV, COUNT = 0, 16, 20, 24
PLAN_ROWS = 32
NEAR = 12
FAR = (6, 8, 10)
WIDE = 14


def vmem():
    return pl.BlockSpec(memory_space=pltpu.VMEM)


def smem():
    return pl.BlockSpec(memory_space=pltpu.SMEM)


def plan_body(here_ref, ids_ref, owner_ref, plan_ref, choice_ref, row_ref, tally_ref):
    s_dev = ids_ref.shape[1]
    nsky = owner_ref.shape[0]
    per_plane = nsky // PLANES
    most = plan_ref.shape[1] - 1
    wide = 2 * PLANES
    local_tally = PLANES * wide
    inner, plane = here_ref[0], here_ref[2]
    row_ref[nsky] = nsky

    def place(r, carry):
        row_ref[owner_ref[r]] = r
        return carry

    lax.fori_loop(0, nsky, place, 0, unroll=8)
    for n in range(PLANES * wide):
        tally_ref[n] = 0
    for k0 in range(PLANES):
        source = plane ^ k0
        for a in range(INNER):
            if k0 == 0:
                for k in range(wide):
                    tally_ref[local_tally + k] = 0
            for s in range(s_dev):
                row = row_ref[ids_ref[source * INNER + (inner ^ a), s]]
                far = lax.div(row, per_plane) ^ source
                n = tally_ref[k0 * wide + far]
                tally_ref[k0 * wide + far] = n + 1
                local = row - plane * per_plane
                if k0 > 0:
                    plan_ref[RECV + k0, jnp.where(far == k0, n, most)] = local
                else:
                    m = tally_ref[local_tally + far]
                    tally_ref[local_tally + far] = m + 1
                    known = far < PLANES
                    line = SEND + a * PLANES + jnp.where(known, far, 0)
                    plan_ref[line, jnp.where(known, m, most)] = s
                    plan_ref[OWN + a, jnp.where(far == 0, m, most)] = local
            if k0 == 0:
                for k in range(PLANES):
                    plan_ref[COUNT, a * PLANES + k] = tally_ref[local_tally + k]
        plan_ref[COUNT + 1, k0] = tally_ref[k0 * wide + k0]
    need = []
    for k in range(1, PLANES):
        value = tally_ref[k]
        for k0 in range(1, PLANES):
            value = jnp.maximum(value, tally_ref[k0 * wide + k])
        need.append(value)
    steps = len(FAR)
    choice = jnp.int32(0)
    for cap in FAR[:-1]:
        choice = choice + jnp.where(need[1] > cap, steps, 0) + jnp.where(need[2] > cap, 1, 0)
    far = jnp.maximum(need[1], need[2])
    over = (need[0] > NEAR) | (far > FAR[-1])
    choice = jnp.where(over, steps * steps, choice)
    choice = jnp.where(jnp.maximum(need[0], far) > WIDE, steps * steps + 1, choice)
    choice_ref[0] = choice


def capacities(most):
    return [(NEAR, a, b) for a in FAR for b in FAR] + [(WIDE,) * 3, (most,) * 3]


def make_plan(here, ids, owner):
    most = INNER * ids.shape[1]
    return pl.pallas_call(
        plan_body,
        in_specs=[smem()] * 3,
        out_specs=[smem()] * 2,
        out_shape=[
            jax.ShapeDtypeStruct((PLAN_ROWS, most + 1), jnp.int32),
            jax.ShapeDtypeStruct((1,), jnp.int32),
        ],
        scratch_shapes=[
            pltpu.SMEM((owner.shape[0] + 1,), jnp.int32),
            pltpu.SMEM(((PLANES + 1) * 2 * PLANES,), jnp.int32),
        ],
        compiler_params=params(),
    )(here, ids, owner)


def quarter_body(chan, share, here_ref, exp_ref, images_ref, beam_ref, *outs):
    slots, tile = images_ref.shape[1], images_ref.shape[-1]
    rows = tile // INNER
    inner = here_ref[0]
    for j in range(INNER):
        base = pl.multiple_of((inner ^ j) * rows, rows)

        def step(s, carry):
            if share:
                half = pl.multiple_of(base + here_ref[1] * share, share)
                outs[j][s, :share] = beam_ref[0, s, pl.ds(half, share), :]
            logs = jnp.log2(beam_ref[0, s, pl.ds(base, rows), :].astype(jnp.float32))
            plane = images_ref[0, s, 0, pl.ds(base, rows), :].astype(jnp.float32)
            outs[j][s, share:] = (jnp.exp2(exp_ref[chan] * logs) * plane).astype(jnp.bfloat16)
            return carry

        lax.fori_loop(0, slots, step, 0)


def quarters(here, own_exp, images, beam, chan, share):
    pts, slots, ch, tile, _ = images.shape
    rows = tile // INNER + share
    return pl.pallas_call(
        functools.partial(quarter_body, chan, share),
        grid=(pts,),
        in_specs=[
            smem(),
            smem(),
            pl.BlockSpec((1, slots, 1, tile, tile), lambda p: (p, 0, chan, 0, 0)),
            pl.BlockSpec((1, slots, tile, tile), lambda p: (p, 0, 0, 0)),
        ],
        out_specs=[pl.BlockSpec((slots, rows, tile), lambda p: (p, 0, 0))] * INNER,
        out_shape=[jax.ShapeDtypeStruct((pts * slots, rows, tile), jnp.bfloat16)] * INNER,
        compiler_params=params(),
    )(here, own_exp, images, beam)


def pack_body(plan_ref, *refs):
    got, outs = refs[:INNER], refs[INNER:]
    for k, out in enumerate(outs, 1):
        start = jnp.int32(0)
        for j in range(INNER):
            count = plan_ref[COUNT, j * PLANES + k]

            def step(n, carry):
                out[start + n] = got[j][plan_ref[SEND + j * PLANES + k, n]]
                return carry

            lax.fori_loop(0, count, step, 0)
            start = start + count


def pack(plan, got, caps):
    _, rows, tile = got[0].shape
    return pl.pallas_call(
        pack_body,
        in_specs=[smem()] + [vmem()] * INNER,
        out_specs=[vmem()] * len(caps),
        out_shape=[jax.ShapeDtypeStruct((cap, rows, tile), jnp.bfloat16) for cap in caps],
        compiler_params=params(),
    )(plan, *got)


def each_tile(plan_ref, got, recv, lines, add):
    for j in range(INNER):

        def own(n, carry):
            add(plan_ref[OWN + j, n], got[j][plan_ref[SEND + j * PLANES, n], lines, :])
            return carry

        lax.fori_loop(0, plan_ref[COUNT, j * PLANES], own, 0)
    for k, tiles in enumerate(recv, 1):

        def other(n, carry):
            add(plan_ref[RECV + k, n], tiles[n, lines, :])
            return carry

        lax.fori_loop(0, plan_ref[COUNT + 1, k], other, 0)


def inverse_body(share, plan_ref, exp_ref, *refs):
    got, recv, out_ref, acc_ref = refs[:INNER], refs[INNER:-2], refs[-2], refs[-1]
    ch = exp_ref.shape[0]
    acc_ref[...] = jnp.zeros_like(acc_ref)

    def add(t, tile):
        logs = jnp.log2(tile.astype(jnp.float32))
        weight = jnp.zeros_like(logs)
        for c in range(ch):
            weight = weight + jnp.exp2((2.0 * exp_ref[c]) * logs)
        acc_ref[t] += weight * (1.0 / ch)

    each_tile(plan_ref, got, recv, slice(0, share), add)
    out_ref[...] = (1.0 / jnp.maximum(acc_ref[...], weight_floor)).astype(out_ref.dtype)


def inverse_totals(plan, exponent, got, recv, share, per_plane):
    shape = (per_plane, share, got[0].shape[-1])
    return pl.pallas_call(
        functools.partial(inverse_body, share),
        in_specs=[smem()] * 2 + [vmem()] * (INNER + len(recv)),
        out_specs=vmem(),
        out_shape=jax.ShapeDtypeStruct(shape, jnp.bfloat16),
        scratch_shapes=[pltpu.VMEM(shape, jnp.float32)],
        compiler_params=params(),
    )(plan, exponent, *got, *recv)


def sum_body(skip, nrecv, here_ref, plan_ref, *refs):
    got, recv = refs[:INNER], refs[INNER:INNER + nrecv]
    inverse, outs, acc_ref = refs[INNER + nrecv:-1 - INNER], refs[-1 - INNER:-1], refs[-1]
    inner, chan = here_ref[0], here_ref[1]
    share = inverse[0].shape[1]
    per, rows = outs[0].shape[:2]
    acc_ref[...] = jnp.zeros_like(acc_ref)

    def add(t, tile):
        acc_ref[t] += tile.astype(jnp.float32)

    each_tile(plan_ref, got, recv, slice(skip, skip + rows), add)
    for j in range(INNER):

        def emit(k, carry):
            t = (inner ^ j) * per + k
            for y, inv in enumerate(inverse):
                part = pl.ds(pl.multiple_of((chan ^ y) * share, share), share)
                value = acc_ref[t, part, :] * inv[t].astype(jnp.float32)
                outs[j][k, part, :] = value.astype(jnp.bfloat16)
            return carry

        lax.fori_loop(0, per, emit, 0)


def sum_normal(here, plan, got, recv, inverse, skip, per_plane):
    _, rows, tile = got[0].shape
    rows = rows - skip
    return pl.pallas_call(
        functools.partial(sum_body, skip, len(recv)),
        in_specs=[smem()] * 2 + [vmem()] * (INNER + len(recv) + len(inverse)),
        out_specs=[vmem()] * INNER,
        out_shape=[jax.ShapeDtypeStruct((per_plane // INNER, rows, tile), jnp.bfloat16)] * INNER,
        scratch_shapes=[pltpu.VMEM((per_plane, rows, tile), jnp.float32)],
        compiler_params=params(),
    )(here, plan, *got, *recv, *inverse)


def plane_conv_body(here_ref, psf_ref, *refs):
    quarter, out_ref, left_ref = refs[:INNER], refs[-2], refs[-1]
    per, rows, tile = quarter[0].shape
    inner = here_ref[0]
    for j in range(INNER):
        left = lax.dot_general(
            quarter[j][...].reshape(per * rows, tile),
            psf_ref[0, 1],
            (((1,), (1,)), ((), ())),
            preferred_element_type=jnp.float32,
        )
        part = pl.ds(pl.multiple_of((inner ^ j) * rows, rows), rows)
        left_ref[:, part, :] = left.astype(jnp.bfloat16).reshape(per, rows, tile)
    for t in range(per):
        out_ref[t, 0] = jnp.dot(
            psf_ref[0, 0], left_ref[t], preferred_element_type=jnp.float32
        ).astype(jnp.bfloat16)


def plane_convolve(here, psf, quarter, chan, before):
    per, rows, tile = quarter[0].shape
    ch = psf.shape[0]
    extra = [] if before is None else [before]
    block = per // 2
    return pl.pallas_call(
        plane_conv_body,
        grid=(per // block,),
        in_specs=[smem(), pl.BlockSpec((1, 2, tile, tile), lambda t: (chan, 0, 0, 0))]
        + [pl.BlockSpec((block, rows, tile), lambda t: (t, 0, 0))] * INNER
        + [pl.BlockSpec(memory_space=pl.ANY)] * len(extra),
        out_specs=pl.BlockSpec((block, 1, tile, tile), lambda t: (t, chan, 0, 0)),
        out_shape=jax.ShapeDtypeStruct((per, ch, tile, tile), jnp.bfloat16),
        scratch_shapes=[pltpu.VMEM((block, tile, tile), jnp.bfloat16)],
        input_output_aliases={2 + INNER: 0} if extra else {},
        compiler_params=params(),
    )(here, psf, *quarter, *extra)


def swap(value, axis, distance):
    n = lax.axis_size(axis)
    return lax.ppermute(value, axis, [(d, d ^ distance) for d in range(n)])


def inside(parts):
    return [parts[0]] + [swap(parts[j], "point", j) for j in range(1, INNER)]


def between(parts):
    return [swap(part, "point", (k + 1) * INNER) for k, part in enumerate(parts)]


def plane_shards(images, beam, exponent, intersection, counts, owner, psf):
    pts, slots, ch, tile, _ = images.shape
    npoint, nchan = lax.axis_size("point"), lax.axis_size("chan")
    s_dev = pts * slots
    nsky = owner.shape[0]
    per_plane = nsky // PLANES
    share = tile // INNER // nchan
    chan_pos, point_pos = lax.axis_index("chan"), lax.axis_index("point")
    here = jnp.stack([point_pos % INNER, chan_pos, point_pos // INNER]).astype(jnp.int32)
    own_exp = lax.dynamic_slice_in_dim(exponent, chan_pos * ch, ch)

    live = jnp.arange(slots)[None, :] < counts[:, None]
    own_ids = jnp.where(live, intersection, nsky).reshape(1, s_dev)
    ids = lax.all_to_all(
        jnp.broadcast_to(own_ids, (npoint, s_dev)), "point", split_axis=0, concat_axis=0, tiled=True
    )
    ids, here = lax.optimization_barrier((ids, here))
    first = inside(quarters(here, own_exp, images, beam, 0, share))
    plan, choice = make_plan(here, ids, owner)
    later = [quarters(here, own_exp, images, beam, c, 0) for c in range(1, ch)]

    def branch(caps):
        def run(here, plan, first, later, exponent, psf):
            got, packed, recv = [first], [pack(plan, first, caps)], []
            for c in range(1, ch):
                recv.append(between(packed[-1]))
                parts, _ = lax.optimization_barrier((later[c - 1], packed[-1]))
                got.append(inside(parts))
                packed.append(pack(plan, got[-1], caps))
                packed[-1], recv[-1] = lax.optimization_barrier((packed[-1], recv[-1]))
            recv.append(between(packed[-1]))
            inverse = inverse_totals(plan, exponent, first, recv[0], share, per_plane)
            inverses = [inverse] + [swap(inverse, "chan", y) for y in range(1, nchan)]
            out = None
            for c in range(ch):
                skip = 0 if c else share
                normal = inside(sum_normal(here, plan, got[c], recv[c], inverses, skip, per_plane))
                out = plane_convolve(here, psf, normal, c, out)
            return out

        return run

    branches = [branch(caps) for caps in capacities(INNER * s_dev)]
    return lax.switch(choice[0], branches, here, plan, first, later, exponent, psf)


def shards(*args):
    if lax.axis_size("point") == PLANES * INNER:
        return plane_shards(*args)
    return row_split_shards(*args)


def solution(mesh):
    return jax.shard_map(
        shards,
        mesh=mesh,
        in_specs=(
            P("point", None, "chan", None, None),
            P("point", None, None, None),
            P(),
            P("point", None),
            P("point"),
            P(),
            P("chan", None, None, None),
        ),
        out_specs=P("point", "chan", None, None),
        check_vma=False,
    )
```

```python
import functools

import jax
import jax.numpy as jnp
from jax import lax
from jax.experimental import pallas as pl
from jax.experimental.pallas import tpu as pltpu
from jax.sharding import PartitionSpec as P

weight_floor = 0.05
VMEM_LIMIT = 48 * 1024 * 1024


def params():
    return pltpu.CompilerParams(vmem_limit_bytes=VMEM_LIMIT)


def put_rows(out_ref, at, value):
    group, rows = out_ref.shape[0], out_ref.shape[-2]
    for g in range(group):
        out_ref[(g,) + at] = value[g * rows:(g + 1) * rows].astype(jnp.bfloat16)


def row_block(tile, npoint):
    rows = tile // npoint
    block = max(rows, 16)
    return rows, block, block // rows


def weight_body(exp_ref, images_ref, beam_ref, out_ref):
    slots = images_ref.shape[1]
    for p in range(images_ref.shape[0]):
        for s in range(slots):
            logs = jnp.log(beam_ref[p, s].astype(jnp.float32))
            for c in range(images_ref.shape[2]):
                power = jnp.exp(exp_ref[c] * logs)
                plane = images_ref[p, s, c].astype(jnp.float32)
                put_rows(out_ref, (p * slots + s, c), power * plane)


def weigh(own_exp, images, beam, npoint):
    pts, slots, ch, tile, _ = images.shape
    rows, block, group = row_block(tile, npoint)
    return pl.pallas_call(
        weight_body,
        grid=(npoint // group,),
        in_specs=[
            pl.BlockSpec(memory_space=pltpu.SMEM),
            pl.BlockSpec((pts, slots, ch, block, tile), lambda i: (0, 0, 0, i, 0)),
            pl.BlockSpec((pts, slots, block, tile), lambda i: (0, 0, i, 0)),
        ],
        out_specs=pl.BlockSpec((group, pts * slots, ch, rows, tile), lambda i: (i, 0, 0, 0, 0)),
        out_shape=jax.ShapeDtypeStruct((npoint, pts * slots, ch, rows, tile), jnp.bfloat16),
        compiler_params=params(),
    )(own_exp, images, beam)


def split_body(beam_ref, out_ref):
    for s in range(beam_ref.shape[0]):
        put_rows(out_ref, (s,), beam_ref[s].astype(jnp.float32))


def split_rows(beam, npoint):
    s, tile, _ = beam.shape
    rows, block, group = row_block(tile, npoint)
    return pl.pallas_call(
        split_body,
        grid=(npoint // group,),
        in_specs=[pl.BlockSpec((s, block, tile), lambda i: (0, i, 0))],
        out_specs=pl.BlockSpec((group, s, rows, tile), lambda i: (i, 0, 0, 0)),
        out_shape=jax.ShapeDtypeStruct((npoint, s, rows, tile), jnp.bfloat16),
        compiler_params=params(),
    )(beam)


def total_body(s_dev, ids_ref, exp_ref, beam_ref, out_ref, acc_ref):
    nchan, npoint, part = beam_ref.shape[:3]
    nsky = out_ref.shape[0]
    ch = exp_ref.shape[0]
    acc_ref[...] = jnp.zeros_like(acc_ref)

    def step(d, carry):
        for share in range(nchan):
            for k in range(part):
                at = ids_ref[d, share * part + k]

                @pl.when(at < nsky)
                def _():
                    logs = jnp.log(beam_ref[share, d, k].astype(jnp.float32))
                    pw = jnp.zeros_like(logs)
                    for c in range(ch):
                        power = jnp.exp(exp_ref[c] * logs)
                        pw = pw + power * power
                    acc_ref[at] += pw * (1.0 / ch)

        return carry

    lax.fori_loop(0, npoint, step, 0)
    out_ref[...] = jnp.maximum(acc_ref[...], weight_floor)


def totals(ids, exponent, beams, nsky):
    rows, tile = beams.shape[3:]
    s_dev = ids.shape[1]
    return pl.pallas_call(
        functools.partial(total_body, s_dev),
        in_specs=[
            pl.BlockSpec(memory_space=pltpu.SMEM),
            pl.BlockSpec(memory_space=pltpu.SMEM),
            pl.BlockSpec(memory_space=pltpu.VMEM),
        ],
        out_specs=pl.BlockSpec(memory_space=pltpu.VMEM),
        out_shape=jax.ShapeDtypeStruct((nsky, rows, tile), jnp.float32),
        scratch_shapes=[pltpu.VMEM((nsky, rows, tile), jnp.float32)],
        compiler_params=params(),
    )(ids, exponent, beams)


def normal_body(ids_ref, owner_ref, tiles_ref, floor_ref, out_ref, acc_ref):
    npoint, s_dev, ch = tiles_ref.shape[:3]
    nsky = floor_ref.shape[0]
    acc_ref[...] = jnp.zeros_like(acc_ref)

    def step(d, carry):
        for s in range(s_dev):
            at = ids_ref[d, s]

            @pl.when(at < nsky)
            def _():
                acc_ref[at] += tiles_ref[d, s].astype(jnp.float32)

        return carry

    lax.fori_loop(0, npoint, step, 0)
    per = out_ref.shape[1]

    def emit(d, carry):
        for k in range(per):
            t = owner_ref[d * per + k]
            inv = floor_ref[t]
            for c in range(ch):
                out_ref[d, k, c] = (acc_ref[t, c] / inv).astype(jnp.bfloat16)
        return carry

    lax.fori_loop(0, npoint, emit, 0)


def normalise(ids, owner, tiles, floored):
    npoint, s_dev, ch, rows, tile = tiles.shape
    nsky = owner.shape[0]
    return pl.pallas_call(
        normal_body,
        in_specs=[
            pl.BlockSpec(memory_space=pltpu.SMEM),
            pl.BlockSpec(memory_space=pltpu.SMEM),
            pl.BlockSpec(memory_space=pltpu.VMEM),
            pl.BlockSpec(memory_space=pltpu.VMEM),
        ],
        out_specs=pl.BlockSpec(memory_space=pltpu.VMEM),
        out_shape=jax.ShapeDtypeStruct((npoint, nsky // npoint, ch, rows, tile), jnp.bfloat16),
        scratch_shapes=[pltpu.VMEM((nsky, ch, rows, tile), jnp.float32)],
        compiler_params=params(),
    )(ids, owner, tiles, floored)


def conv_body(tiles_ref, psf_ref, out_ref):
    tile = psf_ref.shape[-1]
    for c in range(tiles_ref.shape[2]):
        plane = tiles_ref[:, 0, c].reshape(tile, tile)
        left = lax.dot_general(
            plane, psf_ref[c, 1], (((1,), (1,)), ((), ())), preferred_element_type=jnp.float32
        ).astype(jnp.bfloat16)
        out_ref[0, c] = jnp.dot(
            psf_ref[c, 0], left, preferred_element_type=jnp.float32
        ).astype(jnp.bfloat16)


def convolve(tiles, psf):
    npoint, per, ch, rows, tile = tiles.shape
    return pl.pallas_call(
        conv_body,
        grid=(per,),
        in_specs=[
            pl.BlockSpec((npoint, 1, ch, rows, tile), lambda i: (0, i, 0, 0, 0)),
            pl.BlockSpec(psf.shape, lambda i: (0, 0, 0, 0)),
        ],
        out_specs=pl.BlockSpec((1, ch, tile, tile), lambda i: (i, 0, 0, 0)),
        out_shape=jax.ShapeDtypeStruct((per, ch, tile, tile), jnp.bfloat16),
        compiler_params=params(),
    )(tiles, psf)


def row_split_shards(images, beam, exponent, intersection, counts, owner, psf):
    pts, slots, ch, tile, _ = images.shape
    npoint = lax.axis_size("point")
    nchan = lax.axis_size("chan")
    s_dev = pts * slots
    part = s_dev // nchan
    nsky = owner.shape[0]
    chan_pos = lax.axis_index("chan")

    live = jnp.arange(slots)[None, :] < counts[:, None]
    own_ids = jnp.where(live, intersection, nsky).reshape(1, s_dev)
    ids = lax.all_to_all(
        jnp.broadcast_to(own_ids, (npoint, s_dev)), "point", split_axis=0, concat_axis=0, tiled=True
    )
    own_beam = lax.dynamic_slice_in_dim(
        beam.reshape(s_dev, tile, tile), chan_pos * part, part, axis=0
    )
    beam_rows = lax.all_to_all(
        split_rows(own_beam, npoint), "point", split_axis=0, concat_axis=0, tiled=True
    )
    own_exp = lax.dynamic_slice_in_dim(exponent, chan_pos * ch, ch)
    weighted = weigh(own_exp, images, beam, npoint)
    tiles = lax.all_to_all(weighted, "point", split_axis=0, concat_axis=0, tiled=True)
    beams = lax.all_gather(beam_rows, "chan", axis=0, tiled=False)
    floored = totals(ids, exponent, beams, nsky)
    ordered = normalise(ids, owner, tiles, floored)
    returned = lax.all_to_all(ordered, "point", split_axis=0, concat_axis=0, tiled=True)
    return convolve(returned, psf)


INNER = 4
PLANES = 4
SEND, OWN, RECV, COUNT = 0, 16, 20, 24
PLAN_ROWS = 32
NEAR = 12
FAR = (6, 8, 10)
WIDE = 14


def vmem():
    return pl.BlockSpec(memory_space=pltpu.VMEM)


def smem():
    return pl.BlockSpec(memory_space=pltpu.SMEM)


def plan_body(here_ref, ids_ref, owner_ref, plan_ref, choice_ref, row_ref, tally_ref):
    s_dev = ids_ref.shape[1]
    nsky = owner_ref.shape[0]
    per_plane = nsky // PLANES
    most = plan_ref.shape[1] - 1
    wide = 2 * PLANES
    local_tally = PLANES * wide
    inner, plane = here_ref[0], here_ref[2]
    row_ref[nsky] = nsky

    def place(r, carry):
        row_ref[owner_ref[r]] = r
        return carry

    lax.fori_loop(0, nsky, place, 0, unroll=8)
    for n in range(PLANES * wide):
        tally_ref[n] = 0
    for k0 in range(PLANES):
        source = plane ^ k0
        for a in range(INNER):
            if k0 == 0:
                for k in range(wide):
                    tally_ref[local_tally + k] = 0
            for s in range(s_dev):
                row = row_ref[ids_ref[source * INNER + (inner ^ a), s]]
                far = lax.div(row, per_plane) ^ source
                n = tally_ref[k0 * wide + far]
                tally_ref[k0 * wide + far] = n + 1
                local = row - plane * per_plane
                if k0 > 0:
                    plan_ref[RECV + k0, jnp.where(far == k0, n, most)] = local
                else:
                    m = tally_ref[local_tally + far]
                    tally_ref[local_tally + far] = m + 1
                    known = far < PLANES
                    line = SEND + a * PLANES + jnp.where(known, far, 0)
                    plan_ref[line, jnp.where(known, m, most)] = s
                    plan_ref[OWN + a, jnp.where(far == 0, m, most)] = local
            if k0 == 0:
                for k in range(PLANES):
                    plan_ref[COUNT, a * PLANES + k] = tally_ref[local_tally + k]
        plan_ref[COUNT + 1, k0] = tally_ref[k0 * wide + k0]
    need = []
    for k in range(1, PLANES):
        value = tally_ref[k]
        for k0 in range(1, PLANES):
            value = jnp.maximum(value, tally_ref[k0 * wide + k])
        need.append(value)
    steps = len(FAR)
    choice = jnp.int32(0)
    for cap in FAR[:-1]:
        choice = choice + jnp.where(need[1] > cap, steps, 0) + jnp.where(need[2] > cap, 1, 0)
    far = jnp.maximum(need[1], need[2])
    over = (need[0] > NEAR) | (far > FAR[-1])
    choice = jnp.where(over, steps * steps, choice)
    choice = jnp.where(jnp.maximum(need[0], far) > WIDE, steps * steps + 1, choice)
    choice_ref[0] = choice


def capacities(most):
    return [(NEAR, a, b) for a in FAR for b in FAR] + [(WIDE,) * 3, (most,) * 3]


def make_plan(here, ids, owner):
    most = INNER * ids.shape[1]
    return pl.pallas_call(
        plan_body,
        in_specs=[smem()] * 3,
        out_specs=[smem()] * 2,
        out_shape=[
            jax.ShapeDtypeStruct((PLAN_ROWS, most + 1), jnp.int32),
            jax.ShapeDtypeStruct((1,), jnp.int32),
        ],
        scratch_shapes=[
            pltpu.SMEM((owner.shape[0] + 1,), jnp.int32),
            pltpu.SMEM(((PLANES + 1) * 2 * PLANES,), jnp.int32),
        ],
        compiler_params=params(),
    )(here, ids, owner)


def share_body(here_ref, beam_ref, *outs):
    pts, slots, tile, _ = beam_ref.shape
    share = outs[0].shape[1]
    rows = tile // INNER
    for j in range(INNER):
        start = pl.multiple_of((here_ref[0] ^ j) * rows + here_ref[1] * share, share)
        for p in range(pts):
            for s in range(slots):
                outs[j][p * slots + s] = beam_ref[p, s, pl.ds(start, share), :]


def beam_shares(here, beam, share):
    pts, slots, tile, _ = beam.shape
    return pl.pallas_call(
        share_body,
        in_specs=[smem(), vmem()],
        out_specs=[vmem()] * INNER,
        out_shape=[jax.ShapeDtypeStruct((pts * slots, share, tile), jnp.bfloat16)] * INNER,
        compiler_params=params(),
    )(here, beam)


def quarter_body(here_ref, exp_ref, images_ref, beam_ref, *outs):
    pts, slots, ch, tile, _ = images_ref.shape
    rows = tile // INNER
    for j in range(INNER):
        base = pl.multiple_of((here_ref[0] ^ j) * rows, rows)
        for p in range(pts):

            def step(s, carry):
                logs = jnp.log2(beam_ref[p, s, pl.ds(base, rows), :].astype(jnp.float32))
                for c in range(ch):
                    plane = images_ref[p, s, c, pl.ds(base, rows), :].astype(jnp.float32)
                    value = jnp.exp2(exp_ref[c] * logs) * plane
                    outs[c * INNER + j][p * slots + s] = value.astype(jnp.bfloat16)
                return carry

            lax.fori_loop(0, slots, step, 0)


def quarters(here, own_exp, images, beam):
    pts, slots, ch, tile, _ = images.shape
    shape = jax.ShapeDtypeStruct((pts * slots, tile // INNER, tile), jnp.bfloat16)
    res = pl.pallas_call(
        quarter_body,
        in_specs=[smem(), smem(), vmem(), vmem()],
        out_specs=[vmem()] * (ch * INNER),
        out_shape=[shape] * (ch * INNER),
        compiler_params=params(),
    )(here, own_exp, images, beam)
    return [res[c * INNER:(c + 1) * INNER] for c in range(ch)]


def pack_body(plan_ref, *refs):
    got, outs = refs[:INNER], refs[INNER:]
    for k, out in enumerate(outs, 1):
        start = jnp.int32(0)
        for j in range(INNER):
            count = plan_ref[COUNT, j * PLANES + k]

            def step(n, carry):
                out[start + n] = got[j][plan_ref[SEND + j * PLANES + k, n]]
                return carry

            lax.fori_loop(0, count, step, 0)
            start = start + count


def pack(plan, got, caps):
    _, rows, tile = got[0].shape
    return pl.pallas_call(
        pack_body,
        in_specs=[smem()] + [vmem()] * INNER,
        out_specs=[vmem()] * len(caps),
        out_shape=[jax.ShapeDtypeStruct((cap, rows, tile), jnp.bfloat16) for cap in caps],
        compiler_params=params(),
    )(plan, *got)


def each_tile(plan_ref, got, recv, add):
    for j in range(INNER):

        def own(n, carry):
            add(plan_ref[OWN + j, n], got[j][plan_ref[SEND + j * PLANES, n]])
            return carry

        lax.fori_loop(0, plan_ref[COUNT, j * PLANES], own, 0)
    for k, tiles in enumerate(recv, 1):

        def other(n, carry):
            add(plan_ref[RECV + k, n], tiles[n])
            return carry

        lax.fori_loop(0, plan_ref[COUNT + 1, k], other, 0)


def inverse_body(plan_ref, exp_ref, *refs):
    got, recv, out_ref, acc_ref = refs[:INNER], refs[INNER:-2], refs[-2], refs[-1]
    ch = exp_ref.shape[0]
    acc_ref[...] = jnp.zeros_like(acc_ref)

    def add(t, tile):
        logs = jnp.log2(tile.astype(jnp.float32))
        weight = jnp.zeros_like(logs)
        for c in range(ch):
            weight = weight + jnp.exp2((2.0 * exp_ref[c]) * logs)
        acc_ref[t] += weight * (1.0 / ch)

    each_tile(plan_ref, got, recv, add)
    out_ref[...] = (1.0 / jnp.maximum(acc_ref[...], weight_floor)).astype(out_ref.dtype)


def inverse_totals(plan, exponent, got, recv, per_plane):
    shape = (per_plane,) + got[0].shape[1:]
    return pl.pallas_call(
        inverse_body,
        in_specs=[smem()] * 2 + [vmem()] * (INNER + len(recv)),
        out_specs=vmem(),
        out_shape=jax.ShapeDtypeStruct(shape, jnp.bfloat16),
        scratch_shapes=[pltpu.VMEM(shape, jnp.float32)],
        compiler_params=params(),
    )(plan, exponent, *got, *recv)


def sum_body(nrecv, here_ref, plan_ref, *refs):
    got, recv = refs[:INNER], refs[INNER:INNER + nrecv]
    inverse, outs, acc_ref = refs[INNER + nrecv:-1 - INNER], refs[-1 - INNER:-1], refs[-1]
    inner, chan = here_ref[0], here_ref[1]
    share = inverse[0].shape[1]
    per = outs[0].shape[0]
    acc_ref[...] = jnp.zeros_like(acc_ref)

    def add(t, tile):
        acc_ref[t] += tile.astype(jnp.float32)

    each_tile(plan_ref, got, recv, add)
    for j in range(INNER):

        def emit(k, carry):
            t = (inner ^ j) * per + k
            for y, inv in enumerate(inverse):
                part = pl.ds(pl.multiple_of((chan ^ y) * share, share), share)
                value = acc_ref[t, part, :] * inv[t].astype(jnp.float32)
                outs[j][k, part, :] = value.astype(jnp.bfloat16)
            return carry

        lax.fori_loop(0, per, emit, 0)


def sum_normal(here, plan, got, recv, inverse, per_plane):
    _, rows, tile = got[0].shape
    return pl.pallas_call(
        functools.partial(sum_body, len(recv)),
        in_specs=[smem()] * 2 + [vmem()] * (INNER + len(recv) + len(inverse)),
        out_specs=[vmem()] * INNER,
        out_shape=[jax.ShapeDtypeStruct((per_plane // INNER, rows, tile), jnp.bfloat16)] * INNER,
        scratch_shapes=[pltpu.VMEM((per_plane, rows, tile), jnp.float32)],
        compiler_params=params(),
    )(here, plan, *got, *recv, *inverse)


def plane_conv_body(here_ref, psf_ref, *refs):
    quarter, out_ref, left_ref = refs[:INNER], refs[-2], refs[-1]
    per, rows, tile = quarter[0].shape
    inner = here_ref[0]
    for j in range(INNER):
        left = lax.dot_general(
            quarter[j][...].reshape(per * rows, tile),
            psf_ref[0, 1],
            (((1,), (1,)), ((), ())),
            preferred_element_type=jnp.float32,
        )
        part = pl.ds(pl.multiple_of((inner ^ j) * rows, rows), rows)
        left_ref[:, part, :] = left.astype(jnp.bfloat16).reshape(per, rows, tile)
    for t in range(per):
        out_ref[t, 0] = jnp.dot(
            psf_ref[0, 0], left_ref[t], preferred_element_type=jnp.float32
        ).astype(jnp.bfloat16)


def plane_convolve(here, psf, quarter, chan, before):
    per, rows, tile = quarter[0].shape
    ch = psf.shape[0]
    extra = [] if before is None else [before]
    block = per // 2
    return pl.pallas_call(
        plane_conv_body,
        grid=(per // block,),
        in_specs=[smem(), pl.BlockSpec((1, 2, tile, tile), lambda t: (chan, 0, 0, 0))]
        + [pl.BlockSpec((block, rows, tile), lambda t: (t, 0, 0))] * INNER
        + [pl.BlockSpec(memory_space=pl.ANY)] * len(extra),
        out_specs=pl.BlockSpec((block, 1, tile, tile), lambda t: (t, chan, 0, 0)),
        out_shape=jax.ShapeDtypeStruct((per, ch, tile, tile), jnp.bfloat16),
        scratch_shapes=[pltpu.VMEM((block, tile, tile), jnp.bfloat16)],
        input_output_aliases={2 + INNER: 0} if extra else {},
        compiler_params=params(),
    )(here, psf, *quarter, *extra)


def swap(value, axis, distance):
    n = lax.axis_size(axis)
    return lax.ppermute(value, axis, [(d, d ^ distance) for d in range(n)])


def inside(parts):
    near = swap(parts[1], "point", 1)
    across = swap(parts[2], "point", 2)
    last, near = lax.optimization_barrier((parts[3], near))
    return [parts[0], near, across, swap(last, "point", 3)]


def between(parts):
    return [swap(part, "point", (k + 1) * INNER) for k, part in enumerate(parts)]


def plane_shards(images, beam, exponent, intersection, counts, owner, psf):
    pts, slots, ch, tile, _ = images.shape
    npoint, nchan = lax.axis_size("point"), lax.axis_size("chan")
    s_dev = pts * slots
    nsky = owner.shape[0]
    per_plane = nsky // PLANES
    share = tile // INNER // nchan
    chan_pos, point_pos = lax.axis_index("chan"), lax.axis_index("point")
    here = jnp.stack([point_pos % INNER, chan_pos, point_pos // INNER]).astype(jnp.int32)
    own_exp = lax.dynamic_slice_in_dim(exponent, chan_pos * ch, ch)

    live = jnp.arange(slots)[None, :] < counts[:, None]
    own_ids = jnp.where(live, intersection, nsky).reshape(1, s_dev)
    ids = lax.all_to_all(
        jnp.broadcast_to(own_ids, (npoint, s_dev)), "point", split_axis=0, concat_axis=0, tiled=True
    )
    shares = beam_shares(here, beam, share)
    weighted = quarters(here, own_exp, images, beam)
    shares, weighted[0], ids = lax.optimization_barrier((shares, weighted[0], ids))
    beams = inside(shares)
    first = inside(weighted[0])
    plan, choice = make_plan(here, ids, owner)

    def branch(caps):
        def run(here, plan, beams, first, later, exponent, psf):
            beam_recv = between(pack(plan, beams, caps))
            got, packed, recv = [first], [pack(plan, first, caps)], []
            for c in range(1, ch):
                recv.append(between(packed[-1]))
                parts, _ = lax.optimization_barrier((later[c - 1], packed[-1]))
                got.append(inside(parts))
                packed.append(pack(plan, got[-1], caps))
                packed[-1], recv[-1] = lax.optimization_barrier((packed[-1], recv[-1]))
            recv.append(between(packed[-1]))
            inverse = inverse_totals(plan, exponent, beams, beam_recv, per_plane)
            inverses = [inverse] + [swap(inverse, "chan", y) for y in range(1, nchan)]
            normal = []
            for c in range(ch):
                if c:
                    recv[c], normal[-1] = lax.optimization_barrier((recv[c], normal[-1]))
                normal.append(inside(sum_normal(here, plan, got[c], recv[c], inverses, per_plane)))
            out = None
            for c in range(ch):
                out = plane_convolve(here, psf, normal[c], c, out)
            return out

        return run

    branches = [branch(caps) for caps in capacities(INNER * s_dev)]
    return lax.switch(choice[0], branches, here, plan, beams, first, weighted[1:], exponent, psf)


def shards(*args):
    if lax.axis_size("point") == PLANES * INNER:
        return plane_shards(*args)
    return row_split_shards(*args)


def solution(mesh):
    return jax.shard_map(
        shards,
        mesh=mesh,
        in_specs=(
            P("point", None, "chan", None, None),
            P("point", None, None, None),
            P(),
            P("point", None),
            P("point"),
            P(),
            P("chan", None, None, None),
        ),
        out_specs=P("point", "chan", None, None),
        check_vma=False,
    )
```

```python
import functools

import jax
import jax.numpy as jnp
from jax import lax
from jax.experimental import pallas as pl
from jax.experimental.pallas import tpu as pltpu
from jax.sharding import PartitionSpec as P

weight_floor = 0.05
VMEM_LIMIT = 48 * 1024 * 1024


def params():
    return pltpu.CompilerParams(vmem_limit_bytes=VMEM_LIMIT)


def put_rows(out_ref, at, value):
    group, rows = out_ref.shape[0], out_ref.shape[-2]
    for g in range(group):
        out_ref[(g,) + at] = value[g * rows:(g + 1) * rows].astype(jnp.bfloat16)


def row_block(tile, npoint):
    rows = tile // npoint
    block = max(rows, 16)
    return rows, block, block // rows


def weight_body(exp_ref, images_ref, beam_ref, out_ref):
    slots = images_ref.shape[1]
    for p in range(images_ref.shape[0]):
        for s in range(slots):
            logs = jnp.log(beam_ref[p, s].astype(jnp.float32))
            for c in range(images_ref.shape[2]):
                power = jnp.exp(exp_ref[c] * logs)
                plane = images_ref[p, s, c].astype(jnp.float32)
                put_rows(out_ref, (p * slots + s, c), power * plane)


def weigh(own_exp, images, beam, npoint):
    pts, slots, ch, tile, _ = images.shape
    rows, block, group = row_block(tile, npoint)
    return pl.pallas_call(
        weight_body,
        grid=(npoint // group,),
        in_specs=[
            pl.BlockSpec(memory_space=pltpu.SMEM),
            pl.BlockSpec((pts, slots, ch, block, tile), lambda i: (0, 0, 0, i, 0)),
            pl.BlockSpec((pts, slots, block, tile), lambda i: (0, 0, i, 0)),
        ],
        out_specs=pl.BlockSpec((group, pts * slots, ch, rows, tile), lambda i: (i, 0, 0, 0, 0)),
        out_shape=jax.ShapeDtypeStruct((npoint, pts * slots, ch, rows, tile), jnp.bfloat16),
        compiler_params=params(),
    )(own_exp, images, beam)


def split_body(beam_ref, out_ref):
    for s in range(beam_ref.shape[0]):
        put_rows(out_ref, (s,), beam_ref[s].astype(jnp.float32))


def split_rows(beam, npoint):
    s, tile, _ = beam.shape
    rows, block, group = row_block(tile, npoint)
    return pl.pallas_call(
        split_body,
        grid=(npoint // group,),
        in_specs=[pl.BlockSpec((s, block, tile), lambda i: (0, i, 0))],
        out_specs=pl.BlockSpec((group, s, rows, tile), lambda i: (i, 0, 0, 0)),
        out_shape=jax.ShapeDtypeStruct((npoint, s, rows, tile), jnp.bfloat16),
        compiler_params=params(),
    )(beam)


def total_body(s_dev, ids_ref, exp_ref, beam_ref, out_ref, acc_ref):
    nchan, npoint, part = beam_ref.shape[:3]
    nsky = out_ref.shape[0]
    ch = exp_ref.shape[0]
    acc_ref[...] = jnp.zeros_like(acc_ref)

    def step(d, carry):
        for share in range(nchan):
            for k in range(part):
                at = ids_ref[d, share * part + k]

                @pl.when(at < nsky)
                def _():
                    logs = jnp.log(beam_ref[share, d, k].astype(jnp.float32))
                    pw = jnp.zeros_like(logs)
                    for c in range(ch):
                        power = jnp.exp(exp_ref[c] * logs)
                        pw = pw + power * power
                    acc_ref[at] += pw * (1.0 / ch)

        return carry

    lax.fori_loop(0, npoint, step, 0)
    out_ref[...] = jnp.maximum(acc_ref[...], weight_floor)


def totals(ids, exponent, beams, nsky):
    rows, tile = beams.shape[3:]
    s_dev = ids.shape[1]
    return pl.pallas_call(
        functools.partial(total_body, s_dev),
        in_specs=[
            pl.BlockSpec(memory_space=pltpu.SMEM),
            pl.BlockSpec(memory_space=pltpu.SMEM),
            pl.BlockSpec(memory_space=pltpu.VMEM),
        ],
        out_specs=pl.BlockSpec(memory_space=pltpu.VMEM),
        out_shape=jax.ShapeDtypeStruct((nsky, rows, tile), jnp.float32),
        scratch_shapes=[pltpu.VMEM((nsky, rows, tile), jnp.float32)],
        compiler_params=params(),
    )(ids, exponent, beams)


def normal_body(ids_ref, owner_ref, tiles_ref, floor_ref, out_ref, acc_ref):
    npoint, s_dev, ch = tiles_ref.shape[:3]
    nsky = floor_ref.shape[0]
    acc_ref[...] = jnp.zeros_like(acc_ref)

    def step(d, carry):
        for s in range(s_dev):
            at = ids_ref[d, s]

            @pl.when(at < nsky)
            def _():
                acc_ref[at] += tiles_ref[d, s].astype(jnp.float32)

        return carry

    lax.fori_loop(0, npoint, step, 0)
    per = out_ref.shape[1]

    def emit(d, carry):
        for k in range(per):
            t = owner_ref[d * per + k]
            inv = floor_ref[t]
            for c in range(ch):
                out_ref[d, k, c] = (acc_ref[t, c] / inv).astype(jnp.bfloat16)
        return carry

    lax.fori_loop(0, npoint, emit, 0)


def normalise(ids, owner, tiles, floored):
    npoint, s_dev, ch, rows, tile = tiles.shape
    nsky = owner.shape[0]
    return pl.pallas_call(
        normal_body,
        in_specs=[
            pl.BlockSpec(memory_space=pltpu.SMEM),
            pl.BlockSpec(memory_space=pltpu.SMEM),
            pl.BlockSpec(memory_space=pltpu.VMEM),
            pl.BlockSpec(memory_space=pltpu.VMEM),
        ],
        out_specs=pl.BlockSpec(memory_space=pltpu.VMEM),
        out_shape=jax.ShapeDtypeStruct((npoint, nsky // npoint, ch, rows, tile), jnp.bfloat16),
        scratch_shapes=[pltpu.VMEM((nsky, ch, rows, tile), jnp.float32)],
        compiler_params=params(),
    )(ids, owner, tiles, floored)


def conv_body(tiles_ref, psf_ref, out_ref):
    tile = psf_ref.shape[-1]
    for c in range(tiles_ref.shape[2]):
        plane = tiles_ref[:, 0, c].reshape(tile, tile)
        left = lax.dot_general(
            plane, psf_ref[c, 1], (((1,), (1,)), ((), ())), preferred_element_type=jnp.float32
        ).astype(jnp.bfloat16)
        out_ref[0, c] = jnp.dot(
            psf_ref[c, 0], left, preferred_element_type=jnp.float32
        ).astype(jnp.bfloat16)


def convolve(tiles, psf):
    npoint, per, ch, rows, tile = tiles.shape
    return pl.pallas_call(
        conv_body,
        grid=(per,),
        in_specs=[
            pl.BlockSpec((npoint, 1, ch, rows, tile), lambda i: (0, i, 0, 0, 0)),
            pl.BlockSpec(psf.shape, lambda i: (0, 0, 0, 0)),
        ],
        out_specs=pl.BlockSpec((1, ch, tile, tile), lambda i: (i, 0, 0, 0)),
        out_shape=jax.ShapeDtypeStruct((per, ch, tile, tile), jnp.bfloat16),
        compiler_params=params(),
    )(tiles, psf)


def row_split_shards(images, beam, exponent, intersection, counts, owner, psf):
    pts, slots, ch, tile, _ = images.shape
    npoint = lax.axis_size("point")
    nchan = lax.axis_size("chan")
    s_dev = pts * slots
    part = s_dev // nchan
    nsky = owner.shape[0]
    chan_pos = lax.axis_index("chan")

    live = jnp.arange(slots)[None, :] < counts[:, None]
    own_ids = jnp.where(live, intersection, nsky).reshape(1, s_dev)
    ids = lax.all_to_all(
        jnp.broadcast_to(own_ids, (npoint, s_dev)), "point", split_axis=0, concat_axis=0, tiled=True
    )
    own_beam = lax.dynamic_slice_in_dim(
        beam.reshape(s_dev, tile, tile), chan_pos * part, part, axis=0
    )
    beam_rows = lax.all_to_all(
        split_rows(own_beam, npoint), "point", split_axis=0, concat_axis=0, tiled=True
    )
    own_exp = lax.dynamic_slice_in_dim(exponent, chan_pos * ch, ch)
    weighted = weigh(own_exp, images, beam, npoint)
    tiles = lax.all_to_all(weighted, "point", split_axis=0, concat_axis=0, tiled=True)
    beams = lax.all_gather(beam_rows, "chan", axis=0, tiled=False)
    floored = totals(ids, exponent, beams, nsky)
    ordered = normalise(ids, owner, tiles, floored)
    returned = lax.all_to_all(ordered, "point", split_axis=0, concat_axis=0, tiled=True)
    return convolve(returned, psf)


INNER = 4
PLANES = 4
SEND, OWN, RECV, COUNT = 0, 16, 20, 24
PLAN_ROWS = 32
NEAR = 12
FAR = (6, 8, 10)
WIDE = 14


def vmem():
    return pl.BlockSpec(memory_space=pltpu.VMEM)


def smem():
    return pl.BlockSpec(memory_space=pltpu.SMEM)


def plan_body(here_ref, *refs):
    ids, (owner_ref, plan_ref, choice_ref, row_ref, tally_ref) = refs[:INNER], refs[INNER:]
    s_dev = ids[0].shape[1]
    nsky = owner_ref.shape[0]
    per_plane = nsky // PLANES
    most = plan_ref.shape[1] - 1
    wide = 2 * PLANES
    local_tally = PLANES * wide
    plane = here_ref[2]
    row_ref[nsky] = nsky

    def place(r, carry):
        row_ref[owner_ref[r]] = r
        return carry

    lax.fori_loop(0, nsky, place, 0, unroll=8)
    for n in range(PLANES * wide):
        tally_ref[n] = 0
    for k0 in range(PLANES):
        source = plane ^ k0
        for a in range(INNER):
            if k0 == 0:
                for k in range(wide):
                    tally_ref[local_tally + k] = 0
            for s in range(s_dev):
                row = row_ref[ids[a][k0, s]]
                far = lax.div(row, per_plane) ^ source
                n = tally_ref[k0 * wide + far]
                tally_ref[k0 * wide + far] = n + 1
                local = row - plane * per_plane
                if k0 > 0:
                    plan_ref[RECV + k0, jnp.where(far == k0, n, most)] = local
                else:
                    m = tally_ref[local_tally + far]
                    tally_ref[local_tally + far] = m + 1
                    known = far < PLANES
                    line = SEND + a * PLANES + jnp.where(known, far, 0)
                    plan_ref[line, jnp.where(known, m, most)] = s
                    plan_ref[OWN + a, jnp.where(far == 0, m, most)] = local
            if k0 == 0:
                for k in range(PLANES):
                    plan_ref[COUNT, a * PLANES + k] = tally_ref[local_tally + k]
        plan_ref[COUNT + 1, k0] = tally_ref[k0 * wide + k0]
    need = []
    for k in range(1, PLANES):
        value = tally_ref[k]
        for k0 in range(1, PLANES):
            value = jnp.maximum(value, tally_ref[k0 * wide + k])
        need.append(value)
    steps = len(FAR)
    choice = jnp.int32(0)
    for cap in FAR[:-1]:
        choice = choice + jnp.where(need[1] > cap, steps, 0) + jnp.where(need[2] > cap, 1, 0)
    far = jnp.maximum(need[1], need[2])
    over = (need[0] > NEAR) | (far > FAR[-1])
    choice = jnp.where(over, steps * steps, choice)
    choice = jnp.where(jnp.maximum(need[0], far) > WIDE, steps * steps + 1, choice)
    choice_ref[0] = choice


def capacities(most):
    return [(NEAR, a, b) for a in FAR for b in FAR] + [(WIDE,) * 3, (most,) * 3]


def make_plan(here, ids, owner):
    most = INNER * ids[0].shape[1]
    return pl.pallas_call(
        plan_body,
        in_specs=[smem()] * (2 + INNER),
        out_specs=[smem()] * 2,
        out_shape=[
            jax.ShapeDtypeStruct((PLAN_ROWS, most + 1), jnp.int32),
            jax.ShapeDtypeStruct((1,), jnp.int32),
        ],
        scratch_shapes=[
            pltpu.SMEM((owner.shape[0] + 1,), jnp.int32),
            pltpu.SMEM(((PLANES + 1) * 2 * PLANES,), jnp.int32),
        ],
        compiler_params=params(),
    )(here, *ids, owner)


def quarter_body(chan, share, here_ref, exp_ref, images_ref, beam_ref, *outs):
    slots, tile = images_ref.shape[1], images_ref.shape[-1]
    rows = tile // INNER
    inner = here_ref[0]
    for j in range(INNER):
        base = pl.multiple_of((inner ^ j) * rows, rows)

        def step(s, carry):
            if share:
                half = pl.multiple_of(base + here_ref[1] * share, share)
                outs[j][s, :share] = beam_ref[0, s, pl.ds(half, share), :]
            logs = jnp.log2(beam_ref[0, s, pl.ds(base, rows), :].astype(jnp.float32))
            plane = images_ref[0, s, 0, pl.ds(base, rows), :].astype(jnp.float32)
            outs[j][s, share:] = (jnp.exp2(exp_ref[chan] * logs) * plane).astype(jnp.bfloat16)
            return carry

        lax.fori_loop(0, slots, step, 0)


def quarters(here, own_exp, images, beam, chan, share):
    pts, slots, ch, tile, _ = images.shape
    rows = tile // INNER + share
    return pl.pallas_call(
        functools.partial(quarter_body, chan, share),
        grid=(pts,),
        in_specs=[
            smem(),
            smem(),
            pl.BlockSpec((1, slots, 1, tile, tile), lambda p: (p, 0, chan, 0, 0)),
            pl.BlockSpec((1, slots, tile, tile), lambda p: (p, 0, 0, 0)),
        ],
        out_specs=[pl.BlockSpec((slots, rows, tile), lambda p: (p, 0, 0))] * INNER,
        out_shape=[jax.ShapeDtypeStruct((pts * slots, rows, tile), jnp.bfloat16)] * INNER,
        compiler_params=params(),
    )(here, own_exp, images, beam)


def pack_body(plan_ref, *refs):
    got, outs = refs[:INNER], refs[INNER:]
    for k, out in enumerate(outs, 1):
        start = jnp.int32(0)
        for j in range(INNER):
            count = plan_ref[COUNT, j * PLANES + k]

            def step(n, carry):
                out[start + n] = got[j][plan_ref[SEND + j * PLANES + k, n]]
                return carry

            lax.fori_loop(0, count, step, 0)
            start = start + count


def pack(plan, got, caps):
    _, rows, tile = got[0].shape
    return pl.pallas_call(
        pack_body,
        in_specs=[smem()] + [vmem()] * INNER,
        out_specs=[vmem()] * len(caps),
        out_shape=[jax.ShapeDtypeStruct((cap, rows, tile), jnp.bfloat16) for cap in caps],
        compiler_params=params(),
    )(plan, *got)


def each_tile(plan_ref, got, recv, lines, add):
    for j in range(INNER):

        def own(n, carry):
            add(plan_ref[OWN + j, n], got[j][plan_ref[SEND + j * PLANES, n], lines, :])
            return carry

        lax.fori_loop(0, plan_ref[COUNT, j * PLANES], own, 0)
    for k, tiles in enumerate(recv, 1):

        def other(n, carry):
            add(plan_ref[RECV + k, n], tiles[n, lines, :])
            return carry

        lax.fori_loop(0, plan_ref[COUNT + 1, k], other, 0)


def inverse_body(share, plan_ref, exp_ref, *refs):
    got, recv, out_ref, acc_ref = refs[:INNER], refs[INNER:-2], refs[-2], refs[-1]
    ch = exp_ref.shape[0]
    acc_ref[...] = jnp.zeros_like(acc_ref)

    def add(t, tile):
        logs = jnp.log2(tile.astype(jnp.float32))
        weight = jnp.zeros_like(logs)
        for c in range(ch):
            weight = weight + jnp.exp2((2.0 * exp_ref[c]) * logs)
        acc_ref[t] += weight * (1.0 / ch)

    each_tile(plan_ref, got, recv, slice(0, share), add)
    out_ref[...] = (1.0 / jnp.maximum(acc_ref[...], weight_floor)).astype(out_ref.dtype)


def inverse_totals(plan, exponent, got, recv, share, per_plane):
    shape = (per_plane, share, got[0].shape[-1])
    return pl.pallas_call(
        functools.partial(inverse_body, share),
        in_specs=[smem()] * 2 + [vmem()] * (INNER + len(recv)),
        out_specs=vmem(),
        out_shape=jax.ShapeDtypeStruct(shape, jnp.bfloat16),
        scratch_shapes=[pltpu.VMEM(shape, jnp.float32)],
        compiler_params=params(),
    )(plan, exponent, *got, *recv)


def sum_body(skip, nrecv, here_ref, plan_ref, *refs):
    got, recv = refs[:INNER], refs[INNER:INNER + nrecv]
    inverse, outs, acc_ref = refs[INNER + nrecv:-1 - INNER], refs[-1 - INNER:-1], refs[-1]
    inner, chan = here_ref[0], here_ref[1]
    share = inverse[0].shape[1]
    per, rows = outs[0].shape[:2]
    acc_ref[...] = jnp.zeros_like(acc_ref)

    def add(t, tile):
        acc_ref[t] += tile.astype(jnp.float32)

    each_tile(plan_ref, got, recv, slice(skip, skip + rows), add)
    for j in range(INNER):

        def emit(k, carry):
            t = (inner ^ j) * per + k
            for y, inv in enumerate(inverse):
                part = pl.ds(pl.multiple_of((chan ^ y) * share, share), share)
                value = acc_ref[t, part, :] * inv[t].astype(jnp.float32)
                outs[j][k, part, :] = value.astype(jnp.bfloat16)
            return carry

        lax.fori_loop(0, per, emit, 0)


def sum_normal(here, plan, got, recv, inverse, skip, per_plane):
    _, rows, tile = got[0].shape
    rows = rows - skip
    return pl.pallas_call(
        functools.partial(sum_body, skip, len(recv)),
        in_specs=[smem()] * 2 + [vmem()] * (INNER + len(recv) + len(inverse)),
        out_specs=[vmem()] * INNER,
        out_shape=[jax.ShapeDtypeStruct((per_plane // INNER, rows, tile), jnp.bfloat16)] * INNER,
        scratch_shapes=[pltpu.VMEM((per_plane, rows, tile), jnp.float32)],
        compiler_params=params(),
    )(here, plan, *got, *recv, *inverse)


def plane_conv_body(here_ref, psf_ref, *refs):
    quarter, out_ref, left_ref = refs[:INNER], refs[-2], refs[-1]
    per, rows, tile = quarter[0].shape
    inner = here_ref[0]
    for j in range(INNER):
        left = lax.dot_general(
            quarter[j][...].reshape(per * rows, tile),
            psf_ref[0, 1],
            (((1,), (1,)), ((), ())),
            preferred_element_type=jnp.float32,
        )
        part = pl.ds(pl.multiple_of((inner ^ j) * rows, rows), rows)
        left_ref[:, part, :] = left.astype(jnp.bfloat16).reshape(per, rows, tile)
    for t in range(per):
        out_ref[t, 0] = jnp.dot(
            psf_ref[0, 0], left_ref[t], preferred_element_type=jnp.float32
        ).astype(jnp.bfloat16)


def plane_convolve(here, psf, quarter, chan, before):
    per, rows, tile = quarter[0].shape
    ch = psf.shape[0]
    extra = [] if before is None else [before]
    block = per // 2
    return pl.pallas_call(
        plane_conv_body,
        grid=(per // block,),
        in_specs=[smem(), pl.BlockSpec((1, 2, tile, tile), lambda t: (chan, 0, 0, 0))]
        + [pl.BlockSpec((block, rows, tile), lambda t: (t, 0, 0))] * INNER
        + [pl.BlockSpec(memory_space=pl.ANY)] * len(extra),
        out_specs=pl.BlockSpec((block, 1, tile, tile), lambda t: (t, chan, 0, 0)),
        out_shape=jax.ShapeDtypeStruct((per, ch, tile, tile), jnp.bfloat16),
        scratch_shapes=[pltpu.VMEM((block, tile, tile), jnp.bfloat16)],
        input_output_aliases={2 + INNER: 0} if extra else {},
        compiler_params=params(),
    )(here, psf, *quarter, *extra)


def swap(value, axis, distance):
    n = lax.axis_size(axis)
    return lax.ppermute(value, axis, [(d, d ^ distance) for d in range(n)])


def inside(parts):
    near = swap(parts[1], "point", 1)
    across = swap(parts[2], "point", 2)
    last, near = lax.optimization_barrier((parts[3], near))
    return [parts[0], near, across, swap(last, "point", 3)]


def between(parts):
    return [swap(part, "point", (k + 1) * INNER) for k, part in enumerate(parts)]


def plane_shards(images, beam, exponent, intersection, counts, owner, psf):
    pts, slots, ch, tile, _ = images.shape
    npoint, nchan = lax.axis_size("point"), lax.axis_size("chan")
    s_dev = pts * slots
    nsky = owner.shape[0]
    per_plane = nsky // PLANES
    share = tile // INNER // nchan
    chan_pos, point_pos = lax.axis_index("chan"), lax.axis_index("point")
    here = jnp.stack([point_pos % INNER, chan_pos, point_pos // INNER]).astype(jnp.int32)
    own_exp = lax.dynamic_slice_in_dim(exponent, chan_pos * ch, ch)

    live = jnp.arange(slots)[None, :] < counts[:, None]
    own_ids = jnp.where(live, intersection, nsky).reshape(1, s_dev)
    column = [own_ids] + [swap(own_ids, "point", k * INNER) for k in range(1, PLANES)]
    column = jnp.concatenate(column, axis=0)
    ids = [column] + [swap(column, "point", j) for j in range(1, INNER)]
    first, ids = lax.optimization_barrier((quarters(here, own_exp, images, beam, 0, share), ids))
    first = inside(first)
    plan, choice = make_plan(here, ids, owner)
    later = [quarters(here, own_exp, images, beam, c, 0) for c in range(1, ch)]

    def branch(caps):
        def run(here, plan, first, later, exponent, psf):
            got, packed, recv = [first], [pack(plan, first, caps)], []
            for c in range(1, ch):
                recv.append(between(packed[-1]))
                parts, _ = lax.optimization_barrier((later[c - 1], packed[-1]))
                got.append(inside(parts))
                packed.append(pack(plan, got[-1], caps))
                packed[-1], recv[-1] = lax.optimization_barrier((packed[-1], recv[-1]))
            recv.append(between(packed[-1]))
            inverse = inverse_totals(plan, exponent, first, recv[0], share, per_plane)
            inverses = [inverse] + [swap(inverse, "chan", y) for y in range(1, nchan)]
            normal, out = [], None
            for c in range(ch):
                if c:
                    recv[c], normal[-1] = lax.optimization_barrier((recv[c], normal[-1]))
                scale = inverses
                if c + 1 < ch:
                    scale, early = lax.optimization_barrier((inverses, recv[c + 1][::2]))
                    recv[c + 1] = [early[0], recv[c + 1][1], early[1]]
                skip = 0 if c else share
                part = sum_normal(here, plan, got[c], recv[c], scale, skip, per_plane)
                normal.append(inside(part))
            for c in range(ch):
                out = plane_convolve(here, psf, normal[c], c, out)
            return out

        return run

    branches = [branch(caps) for caps in capacities(INNER * s_dev)]
    return lax.switch(choice[0], branches, here, plan, first, later, exponent, psf)


def shards(*args):
    if lax.axis_size("point") == PLANES * INNER:
        return plane_shards(*args)
    return row_split_shards(*args)


def solution(mesh):
    return jax.shard_map(
        shards,
        mesh=mesh,
        in_specs=(
            P("point", None, "chan", None, None),
            P("point", None, None, None),
            P(),
            P("point", None),
            P("point"),
            P(),
            P("chan", None, None, None),
        ),
        out_specs=P("point", "chan", None, None),
        check_vma=False,
    )
```

```python
import functools

import jax
import jax.numpy as jnp
from jax import lax
from jax.experimental import pallas as pl
from jax.experimental.pallas import tpu as pltpu
from jax.sharding import PartitionSpec as P

weight_floor = 0.05
VMEM_LIMIT = 48 * 1024 * 1024


def params():
    return pltpu.CompilerParams(vmem_limit_bytes=VMEM_LIMIT)


def put_rows(out_ref, at, value):
    group, rows = out_ref.shape[0], out_ref.shape[-2]
    for g in range(group):
        out_ref[(g,) + at] = value[g * rows:(g + 1) * rows].astype(jnp.bfloat16)


def row_block(tile, npoint):
    rows = tile // npoint
    block = max(rows, 16)
    return rows, block, block // rows


def weight_body(exp_ref, images_ref, beam_ref, out_ref):
    slots = images_ref.shape[1]
    for p in range(images_ref.shape[0]):
        for s in range(slots):
            logs = jnp.log(beam_ref[p, s].astype(jnp.float32))
            for c in range(images_ref.shape[2]):
                power = jnp.exp(exp_ref[c] * logs)
                plane = images_ref[p, s, c].astype(jnp.float32)
                put_rows(out_ref, (p * slots + s, c), power * plane)


def weigh(own_exp, images, beam, npoint):
    pts, slots, ch, tile, _ = images.shape
    rows, block, group = row_block(tile, npoint)
    return pl.pallas_call(
        weight_body,
        grid=(npoint // group,),
        in_specs=[
            pl.BlockSpec(memory_space=pltpu.SMEM),
            pl.BlockSpec((pts, slots, ch, block, tile), lambda i: (0, 0, 0, i, 0)),
            pl.BlockSpec((pts, slots, block, tile), lambda i: (0, 0, i, 0)),
        ],
        out_specs=pl.BlockSpec((group, pts * slots, ch, rows, tile), lambda i: (i, 0, 0, 0, 0)),
        out_shape=jax.ShapeDtypeStruct((npoint, pts * slots, ch, rows, tile), jnp.bfloat16),
        compiler_params=params(),
    )(own_exp, images, beam)


def split_body(beam_ref, out_ref):
    for s in range(beam_ref.shape[0]):
        put_rows(out_ref, (s,), beam_ref[s].astype(jnp.float32))


def split_rows(beam, npoint):
    s, tile, _ = beam.shape
    rows, block, group = row_block(tile, npoint)
    return pl.pallas_call(
        split_body,
        grid=(npoint // group,),
        in_specs=[pl.BlockSpec((s, block, tile), lambda i: (0, i, 0))],
        out_specs=pl.BlockSpec((group, s, rows, tile), lambda i: (i, 0, 0, 0)),
        out_shape=jax.ShapeDtypeStruct((npoint, s, rows, tile), jnp.bfloat16),
        compiler_params=params(),
    )(beam)


def total_body(s_dev, ids_ref, exp_ref, beam_ref, out_ref, acc_ref):
    nchan, npoint, part = beam_ref.shape[:3]
    nsky = out_ref.shape[0]
    ch = exp_ref.shape[0]
    acc_ref[...] = jnp.zeros_like(acc_ref)

    def step(d, carry):
        for share in range(nchan):
            for k in range(part):
                at = ids_ref[d, share * part + k]

                @pl.when(at < nsky)
                def _():
                    logs = jnp.log(beam_ref[share, d, k].astype(jnp.float32))
                    pw = jnp.zeros_like(logs)
                    for c in range(ch):
                        power = jnp.exp(exp_ref[c] * logs)
                        pw = pw + power * power
                    acc_ref[at] += pw * (1.0 / ch)

        return carry

    lax.fori_loop(0, npoint, step, 0)
    out_ref[...] = jnp.maximum(acc_ref[...], weight_floor)


def totals(ids, exponent, beams, nsky):
    rows, tile = beams.shape[3:]
    s_dev = ids.shape[1]
    return pl.pallas_call(
        functools.partial(total_body, s_dev),
        in_specs=[
            pl.BlockSpec(memory_space=pltpu.SMEM),
            pl.BlockSpec(memory_space=pltpu.SMEM),
            pl.BlockSpec(memory_space=pltpu.VMEM),
        ],
        out_specs=pl.BlockSpec(memory_space=pltpu.VMEM),
        out_shape=jax.ShapeDtypeStruct((nsky, rows, tile), jnp.float32),
        scratch_shapes=[pltpu.VMEM((nsky, rows, tile), jnp.float32)],
        compiler_params=params(),
    )(ids, exponent, beams)


def normal_body(ids_ref, owner_ref, tiles_ref, floor_ref, out_ref, acc_ref):
    npoint, s_dev, ch = tiles_ref.shape[:3]
    nsky = floor_ref.shape[0]
    acc_ref[...] = jnp.zeros_like(acc_ref)

    def step(d, carry):
        for s in range(s_dev):
            at = ids_ref[d, s]

            @pl.when(at < nsky)
            def _():
                acc_ref[at] += tiles_ref[d, s].astype(jnp.float32)

        return carry

    lax.fori_loop(0, npoint, step, 0)
    per = out_ref.shape[1]

    def emit(d, carry):
        for k in range(per):
            t = owner_ref[d * per + k]
            inv = floor_ref[t]
            for c in range(ch):
                out_ref[d, k, c] = (acc_ref[t, c] / inv).astype(jnp.bfloat16)
        return carry

    lax.fori_loop(0, npoint, emit, 0)


def normalise(ids, owner, tiles, floored):
    npoint, s_dev, ch, rows, tile = tiles.shape
    nsky = owner.shape[0]
    return pl.pallas_call(
        normal_body,
        in_specs=[
            pl.BlockSpec(memory_space=pltpu.SMEM),
            pl.BlockSpec(memory_space=pltpu.SMEM),
            pl.BlockSpec(memory_space=pltpu.VMEM),
            pl.BlockSpec(memory_space=pltpu.VMEM),
        ],
        out_specs=pl.BlockSpec(memory_space=pltpu.VMEM),
        out_shape=jax.ShapeDtypeStruct((npoint, nsky // npoint, ch, rows, tile), jnp.bfloat16),
        scratch_shapes=[pltpu.VMEM((nsky, ch, rows, tile), jnp.float32)],
        compiler_params=params(),
    )(ids, owner, tiles, floored)


def conv_body(tiles_ref, psf_ref, out_ref):
    tile = psf_ref.shape[-1]
    for c in range(tiles_ref.shape[2]):
        plane = tiles_ref[:, 0, c].reshape(tile, tile)
        left = lax.dot_general(
            plane, psf_ref[c, 1], (((1,), (1,)), ((), ())), preferred_element_type=jnp.float32
        ).astype(jnp.bfloat16)
        out_ref[0, c] = jnp.dot(
            psf_ref[c, 0], left, preferred_element_type=jnp.float32
        ).astype(jnp.bfloat16)


def convolve(tiles, psf):
    npoint, per, ch, rows, tile = tiles.shape
    return pl.pallas_call(
        conv_body,
        grid=(per,),
        in_specs=[
            pl.BlockSpec((npoint, 1, ch, rows, tile), lambda i: (0, i, 0, 0, 0)),
            pl.BlockSpec(psf.shape, lambda i: (0, 0, 0, 0)),
        ],
        out_specs=pl.BlockSpec((1, ch, tile, tile), lambda i: (i, 0, 0, 0)),
        out_shape=jax.ShapeDtypeStruct((per, ch, tile, tile), jnp.bfloat16),
        compiler_params=params(),
    )(tiles, psf)


def row_split_shards(images, beam, exponent, intersection, counts, owner, psf):
    pts, slots, ch, tile, _ = images.shape
    npoint = lax.axis_size("point")
    nchan = lax.axis_size("chan")
    s_dev = pts * slots
    part = s_dev // nchan
    nsky = owner.shape[0]
    chan_pos = lax.axis_index("chan")

    live = jnp.arange(slots)[None, :] < counts[:, None]
    own_ids = jnp.where(live, intersection, nsky).reshape(1, s_dev)
    ids = lax.all_to_all(
        jnp.broadcast_to(own_ids, (npoint, s_dev)), "point", split_axis=0, concat_axis=0, tiled=True
    )
    own_beam = lax.dynamic_slice_in_dim(
        beam.reshape(s_dev, tile, tile), chan_pos * part, part, axis=0
    )
    beam_rows = lax.all_to_all(
        split_rows(own_beam, npoint), "point", split_axis=0, concat_axis=0, tiled=True
    )
    own_exp = lax.dynamic_slice_in_dim(exponent, chan_pos * ch, ch)
    weighted = weigh(own_exp, images, beam, npoint)
    tiles = lax.all_to_all(weighted, "point", split_axis=0, concat_axis=0, tiled=True)
    beams = lax.all_gather(beam_rows, "chan", axis=0, tiled=False)
    floored = totals(ids, exponent, beams, nsky)
    ordered = normalise(ids, owner, tiles, floored)
    returned = lax.all_to_all(ordered, "point", split_axis=0, concat_axis=0, tiled=True)
    return convolve(returned, psf)


INNER = 4
PLANES = 4
SEND, OWN, RECV, COUNT = 0, 16, 20, 24
PLAN_ROWS = 32
CAPS = (7, 8, 9, 10, 12)


def vmem():
    return pl.BlockSpec(memory_space=pltpu.VMEM)


def smem():
    return pl.BlockSpec(memory_space=pltpu.SMEM)


def plan_body(here_ref, *refs):
    ids, (owner_ref, plan_ref, choice_ref, row_ref, tally_ref) = refs[:INNER], refs[INNER:]
    s_dev = ids[0].shape[1]
    nsky = owner_ref.shape[0]
    per_plane = nsky // PLANES
    most = plan_ref.shape[1] - 1
    wide = 2 * PLANES
    local_tally = PLANES * wide
    plane = here_ref[2]
    row_ref[nsky] = nsky

    def place(r, carry):
        row_ref[owner_ref[r]] = r
        return carry

    lax.fori_loop(0, nsky, place, 0, unroll=8)
    for n in range(PLANES * wide):
        tally_ref[n] = 0
    for k0 in range(PLANES):
        source = plane ^ k0
        for a in range(INNER):
            if k0 == 0:
                for k in range(wide):
                    tally_ref[local_tally + k] = 0
            for s in range(s_dev):
                row = row_ref[ids[a][k0, s]]
                far = lax.div(row, per_plane) ^ source
                n = tally_ref[k0 * wide + far]
                tally_ref[k0 * wide + far] = n + 1
                local = row - plane * per_plane
                if k0 > 0:
                    plan_ref[RECV + k0, jnp.where(far == k0, n, most)] = local
                else:
                    m = tally_ref[local_tally + far]
                    tally_ref[local_tally + far] = m + 1
                    known = far < PLANES
                    line = SEND + a * PLANES + jnp.where(known, far, 0)
                    plan_ref[line, jnp.where(known, m, most)] = s
                    plan_ref[OWN + a, jnp.where(far == 0, m, most)] = local
            if k0 == 0:
                for k in range(PLANES):
                    plan_ref[COUNT, a * PLANES + k] = tally_ref[local_tally + k]
        plan_ref[COUNT + 1, k0] = tally_ref[k0 * wide + k0]
    need = tally_ref[1]
    for k0 in range(PLANES):
        for k in range(1, PLANES):
            need = jnp.maximum(need, tally_ref[k0 * wide + k])
    choice = jnp.int32(0)
    for cap in CAPS:
        choice = choice + (need > cap).astype(jnp.int32)
    choice_ref[0] = choice


def make_plan(here, ids, owner):
    most = INNER * ids[0].shape[1]
    return pl.pallas_call(
        plan_body,
        in_specs=[smem()] * (2 + INNER),
        out_specs=[smem()] * 2,
        out_shape=[
            jax.ShapeDtypeStruct((PLAN_ROWS, most + 1), jnp.int32),
            jax.ShapeDtypeStruct((1,), jnp.int32),
        ],
        scratch_shapes=[
            pltpu.SMEM((owner.shape[0] + 1,), jnp.int32),
            pltpu.SMEM(((PLANES + 1) * 2 * PLANES,), jnp.int32),
        ],
        compiler_params=params(),
    )(here, *ids, owner)


def quarter_body(chan, share, here_ref, exp_ref, images_ref, beam_ref, *outs):
    slots, tile = images_ref.shape[1], images_ref.shape[-1]
    rows = tile // INNER
    inner = here_ref[0]
    for j in range(INNER):
        base = pl.multiple_of((inner ^ j) * rows, rows)

        def step(s, carry):
            if share:
                half = pl.multiple_of(base + here_ref[1] * share, share)
                outs[j][s, :share] = beam_ref[0, s, pl.ds(half, share), :]
            logs = jnp.log2(beam_ref[0, s, pl.ds(base, rows), :].astype(jnp.float32))
            plane = images_ref[0, s, 0, pl.ds(base, rows), :].astype(jnp.float32)
            outs[j][s, share:] = (jnp.exp2(exp_ref[chan] * logs) * plane).astype(jnp.bfloat16)
            return carry

        lax.fori_loop(0, slots, step, 0)


def quarters(here, own_exp, images, beam, chan, share):
    pts, slots, ch, tile, _ = images.shape
    rows = tile // INNER + share
    return pl.pallas_call(
        functools.partial(quarter_body, chan, share),
        grid=(pts,),
        in_specs=[
            smem(),
            smem(),
            pl.BlockSpec((1, slots, 1, tile, tile), lambda p: (p, 0, chan, 0, 0)),
            pl.BlockSpec((1, slots, tile, tile), lambda p: (p, 0, 0, 0)),
        ],
        out_specs=[pl.BlockSpec((slots, rows, tile), lambda p: (p, 0, 0))] * INNER,
        out_shape=[jax.ShapeDtypeStruct((pts * slots, rows, tile), jnp.bfloat16)] * INNER,
        compiler_params=params(),
    )(here, own_exp, images, beam)


def pack_body(here_ref, plan_ref, *refs):
    got, out = refs[:INNER], refs[INNER]
    for k in range(1, PLANES):
        start = jnp.int32(0)
        for j in range(INNER):
            count = plan_ref[COUNT, j * PLANES + k]

            def step(n, carry):
                tile = got[j][plan_ref[SEND + j * PLANES + k, n]]
                out[here_ref[2] ^ k, start + n] = tile
                return carry

            lax.fori_loop(0, count, step, 0)
            start = start + count


def pack(here, plan, got, cap):
    _, rows, tile = got[0].shape
    return pl.pallas_call(
        pack_body,
        in_specs=[smem()] * 2 + [vmem()] * INNER,
        out_specs=vmem(),
        out_shape=jax.ShapeDtypeStruct((PLANES, cap, rows, tile), jnp.bfloat16),
        compiler_params=params(),
    )(here, plan, *got)


def each_tile(here_ref, plan_ref, got, recv, lines, add):
    for j in range(INNER):

        def own(n, carry):
            add(plan_ref[OWN + j, n], got[j][plan_ref[SEND + j * PLANES, n], lines, :])
            return carry

        lax.fori_loop(0, plan_ref[COUNT, j * PLANES], own, 0)
    for k in range(1, PLANES):

        def other(n, carry):
            add(plan_ref[RECV + k, n], recv[here_ref[2] ^ k, n, lines, :])
            return carry

        lax.fori_loop(0, plan_ref[COUNT + 1, k], other, 0)


def inverse_body(share, here_ref, plan_ref, exp_ref, *refs):
    got, (recv, out_ref, acc_ref) = refs[:INNER], refs[INNER:]
    ch = exp_ref.shape[0]
    acc_ref[...] = jnp.zeros_like(acc_ref)

    def add(t, tile):
        logs = jnp.log2(tile.astype(jnp.float32))
        weight = jnp.zeros_like(logs)
        for c in range(ch):
            weight = weight + jnp.exp2((2.0 * exp_ref[c]) * logs)
        acc_ref[t] += weight * (1.0 / ch)

    each_tile(here_ref, plan_ref, got, recv, slice(0, share), add)
    out_ref[...] = (1.0 / jnp.maximum(acc_ref[...], weight_floor)).astype(out_ref.dtype)


def inverse_totals(here, plan, exponent, got, recv, share, per_plane):
    shape = (per_plane, share, got[0].shape[-1])
    return pl.pallas_call(
        functools.partial(inverse_body, share),
        in_specs=[smem()] * 3 + [vmem()] * (INNER + 1),
        out_specs=vmem(),
        out_shape=jax.ShapeDtypeStruct(shape, jnp.bfloat16),
        scratch_shapes=[pltpu.VMEM(shape, jnp.float32)],
        compiler_params=params(),
    )(here, plan, exponent, *got, recv)


def sum_body(skip, here_ref, plan_ref, *refs):
    got, recv = refs[:INNER], refs[INNER]
    inverse, outs, acc_ref = refs[INNER + 1:-1 - INNER], refs[-1 - INNER:-1], refs[-1]
    inner, chan = here_ref[0], here_ref[1]
    share = inverse[0].shape[1]
    per, rows = outs[0].shape[:2]
    acc_ref[...] = jnp.zeros_like(acc_ref)

    def add(t, tile):
        acc_ref[t] += tile.astype(jnp.float32)

    each_tile(here_ref, plan_ref, got, recv, slice(skip, skip + rows), add)
    for j in range(INNER):

        def emit(k, carry):
            t = (inner ^ j) * per + k
            for y, inv in enumerate(inverse):
                part = pl.ds(pl.multiple_of((chan ^ y) * share, share), share)
                value = acc_ref[t, part, :] * inv[t].astype(jnp.float32)
                outs[j][k, part, :] = value.astype(jnp.bfloat16)
            return carry

        lax.fori_loop(0, per, emit, 0)


def sum_normal(here, plan, got, recv, inverse, skip, per_plane):
    _, rows, tile = got[0].shape
    rows = rows - skip
    return pl.pallas_call(
        functools.partial(sum_body, skip),
        in_specs=[smem()] * 2 + [vmem()] * (INNER + 1 + len(inverse)),
        out_specs=[vmem()] * INNER,
        out_shape=[jax.ShapeDtypeStruct((per_plane // INNER, rows, tile), jnp.bfloat16)] * INNER,
        scratch_shapes=[pltpu.VMEM((per_plane, rows, tile), jnp.float32)],
        compiler_params=params(),
    )(here, plan, *got, recv, *inverse)


def plane_conv_body(here_ref, psf_ref, *refs):
    quarter, out_ref, left_ref = refs[:INNER], refs[-2], refs[-1]
    per, rows, tile = quarter[0].shape
    inner = here_ref[0]
    for j in range(INNER):
        left = lax.dot_general(
            quarter[j][...].reshape(per * rows, tile),
            psf_ref[0, 1],
            (((1,), (1,)), ((), ())),
            preferred_element_type=jnp.float32,
        )
        part = pl.ds(pl.multiple_of((inner ^ j) * rows, rows), rows)
        left_ref[:, part, :] = left.astype(jnp.bfloat16).reshape(per, rows, tile)
    for t in range(per):
        out_ref[t, 0] = jnp.dot(
            psf_ref[0, 0], left_ref[t], preferred_element_type=jnp.float32
        ).astype(jnp.bfloat16)


def plane_convolve(here, psf, quarter, chan, before):
    per, rows, tile = quarter[0].shape
    ch = psf.shape[0]
    extra = [] if before is None else [before]
    block = per // 2
    return pl.pallas_call(
        plane_conv_body,
        grid=(per // block,),
        in_specs=[smem(), pl.BlockSpec((1, 2, tile, tile), lambda t: (chan, 0, 0, 0))]
        + [pl.BlockSpec((block, rows, tile), lambda t: (t, 0, 0))] * INNER
        + [pl.BlockSpec(memory_space=pl.ANY)] * len(extra),
        out_specs=pl.BlockSpec((block, 1, tile, tile), lambda t: (t, chan, 0, 0)),
        out_shape=jax.ShapeDtypeStruct((per, ch, tile, tile), jnp.bfloat16),
        scratch_shapes=[pltpu.VMEM((block, tile, tile), jnp.bfloat16)],
        input_output_aliases={2 + INNER: 0} if extra else {},
        compiler_params=params(),
    )(here, psf, *quarter, *extra)


def swap(value, axis, distance):
    n = lax.axis_size(axis)
    return lax.ppermute(value, axis, [(d, d ^ distance) for d in range(n)])


def inside(parts):
    near = swap(parts[1], "point", 1)
    across = swap(parts[2], "point", 2)
    last, near = lax.optimization_barrier((parts[3], near))
    return [parts[0], near, across, swap(last, "point", 3)]


def between(parts):
    groups = [[p * INNER + a for p in range(PLANES)] for a in range(INNER)]
    return lax.all_to_all(
        parts, "point", split_axis=0, concat_axis=0, axis_index_groups=groups, tiled=True
    )


def plane_shards(images, beam, exponent, intersection, counts, owner, psf):
    pts, slots, ch, tile, _ = images.shape
    npoint, nchan = lax.axis_size("point"), lax.axis_size("chan")
    s_dev = pts * slots
    nsky = owner.shape[0]
    per_plane = nsky // PLANES
    share = tile // INNER // nchan
    chan_pos, point_pos = lax.axis_index("chan"), lax.axis_index("point")
    here = jnp.stack([point_pos % INNER, chan_pos, point_pos // INNER]).astype(jnp.int32)
    own_exp = lax.dynamic_slice_in_dim(exponent, chan_pos * ch, ch)

    live = jnp.arange(slots)[None, :] < counts[:, None]
    own_ids = jnp.where(live, intersection, nsky).reshape(1, s_dev)
    column = [own_ids] + [swap(own_ids, "point", k * INNER) for k in range(1, PLANES)]
    column = jnp.concatenate(column, axis=0)
    ids = [column] + [swap(column, "point", j) for j in range(1, INNER)]
    first, ids = lax.optimization_barrier((quarters(here, own_exp, images, beam, 0, share), ids))
    first = inside(first)
    plan, choice = make_plan(here, ids, owner)
    later = [quarters(here, own_exp, images, beam, c, 0) for c in range(1, ch)]

    def branch(cap):
        def run(here, plan, first, later, exponent, psf):
            got, packed, recv = [first], [pack(here, plan, first, cap)], []
            for c in range(1, ch):
                recv.append(between(packed[-1]))
                parts, _ = lax.optimization_barrier((later[c - 1], packed[-1]))
                got.append(inside(parts))
                packed.append(pack(here, plan, got[-1], cap))
                packed[-1], recv[-1] = lax.optimization_barrier((packed[-1], recv[-1]))
            recv.append(between(packed[-1]))
            inverse = inverse_totals(here, plan, exponent, first, recv[0], share, per_plane)
            inverses = [inverse] + [swap(inverse, "chan", y) for y in range(1, nchan)]
            normal, out = [], None
            for c in range(ch):
                if c:
                    recv[c], normal[-1] = lax.optimization_barrier((recv[c], normal[-1]))
                skip = 0 if c else share
                part = sum_normal(here, plan, got[c], recv[c], inverses, skip, per_plane)
                normal.append(inside(part))
            for c in range(ch):
                out = plane_convolve(here, psf, normal[c], c, out)
            return out

        return run

    branches = [branch(cap) for cap in CAPS + (INNER * s_dev,)]
    return lax.switch(choice[0], branches, here, plan, first, later, exponent, psf)


def shards(*args):
    if lax.axis_size("point") == PLANES * INNER:
        return plane_shards(*args)
    return row_split_shards(*args)


def solution(mesh):
    return jax.shard_map(
        shards,
        mesh=mesh,
        in_specs=(
            P("point", None, "chan", None, None),
            P("point", None, None, None),
            P(),
            P("point", None),
            P("point"),
            P(),
            P("chan", None, None, None),
        ),
        out_specs=P("point", "chan", None, None),
        check_vma=False,
    )
```

```python
import functools

import jax
import jax.numpy as jnp
from jax import lax
from jax.experimental import pallas as pl
from jax.experimental.pallas import tpu as pltpu
from jax.sharding import PartitionSpec as P

weight_floor = 0.05
VMEM_LIMIT = 48 * 1024 * 1024


def params():
    return pltpu.CompilerParams(vmem_limit_bytes=VMEM_LIMIT)


def put_rows(out_ref, at, value):
    group, rows = out_ref.shape[0], out_ref.shape[-2]
    for g in range(group):
        out_ref[(g,) + at] = value[g * rows:(g + 1) * rows].astype(jnp.bfloat16)


def row_block(tile, npoint):
    rows = tile // npoint
    block = max(rows, 16)
    return rows, block, block // rows


def weight_body(exp_ref, images_ref, beam_ref, out_ref):
    slots = images_ref.shape[1]
    for p in range(images_ref.shape[0]):
        for s in range(slots):
            logs = jnp.log(beam_ref[p, s].astype(jnp.float32))
            for c in range(images_ref.shape[2]):
                power = jnp.exp(exp_ref[c] * logs)
                plane = images_ref[p, s, c].astype(jnp.float32)
                put_rows(out_ref, (p * slots + s, c), power * plane)


def weigh(own_exp, images, beam, npoint):
    pts, slots, ch, tile, _ = images.shape
    rows, block, group = row_block(tile, npoint)
    return pl.pallas_call(
        weight_body,
        grid=(npoint // group,),
        in_specs=[
            pl.BlockSpec(memory_space=pltpu.SMEM),
            pl.BlockSpec((pts, slots, ch, block, tile), lambda i: (0, 0, 0, i, 0)),
            pl.BlockSpec((pts, slots, block, tile), lambda i: (0, 0, i, 0)),
        ],
        out_specs=pl.BlockSpec((group, pts * slots, ch, rows, tile), lambda i: (i, 0, 0, 0, 0)),
        out_shape=jax.ShapeDtypeStruct((npoint, pts * slots, ch, rows, tile), jnp.bfloat16),
        compiler_params=params(),
    )(own_exp, images, beam)


def split_body(beam_ref, out_ref):
    for s in range(beam_ref.shape[0]):
        put_rows(out_ref, (s,), beam_ref[s].astype(jnp.float32))


def split_rows(beam, npoint):
    s, tile, _ = beam.shape
    rows, block, group = row_block(tile, npoint)
    return pl.pallas_call(
        split_body,
        grid=(npoint // group,),
        in_specs=[pl.BlockSpec((s, block, tile), lambda i: (0, i, 0))],
        out_specs=pl.BlockSpec((group, s, rows, tile), lambda i: (i, 0, 0, 0)),
        out_shape=jax.ShapeDtypeStruct((npoint, s, rows, tile), jnp.bfloat16),
        compiler_params=params(),
    )(beam)


def total_body(s_dev, ids_ref, exp_ref, beam_ref, out_ref, acc_ref):
    nchan, npoint, part = beam_ref.shape[:3]
    nsky = out_ref.shape[0]
    ch = exp_ref.shape[0]
    acc_ref[...] = jnp.zeros_like(acc_ref)

    def step(d, carry):
        for share in range(nchan):
            for k in range(part):
                at = ids_ref[d, share * part + k]

                @pl.when(at < nsky)
                def _():
                    logs = jnp.log(beam_ref[share, d, k].astype(jnp.float32))
                    pw = jnp.zeros_like(logs)
                    for c in range(ch):
                        power = jnp.exp(exp_ref[c] * logs)
                        pw = pw + power * power
                    acc_ref[at] += pw * (1.0 / ch)

        return carry

    lax.fori_loop(0, npoint, step, 0)
    out_ref[...] = jnp.maximum(acc_ref[...], weight_floor)


def totals(ids, exponent, beams, nsky):
    rows, tile = beams.shape[3:]
    s_dev = ids.shape[1]
    return pl.pallas_call(
        functools.partial(total_body, s_dev),
        in_specs=[
            pl.BlockSpec(memory_space=pltpu.SMEM),
            pl.BlockSpec(memory_space=pltpu.SMEM),
            pl.BlockSpec(memory_space=pltpu.VMEM),
        ],
        out_specs=pl.BlockSpec(memory_space=pltpu.VMEM),
        out_shape=jax.ShapeDtypeStruct((nsky, rows, tile), jnp.float32),
        scratch_shapes=[pltpu.VMEM((nsky, rows, tile), jnp.float32)],
        compiler_params=params(),
    )(ids, exponent, beams)


def normal_body(ids_ref, owner_ref, tiles_ref, floor_ref, out_ref, acc_ref):
    npoint, s_dev, ch = tiles_ref.shape[:3]
    nsky = floor_ref.shape[0]
    acc_ref[...] = jnp.zeros_like(acc_ref)

    def step(d, carry):
        for s in range(s_dev):
            at = ids_ref[d, s]

            @pl.when(at < nsky)
            def _():
                acc_ref[at] += tiles_ref[d, s].astype(jnp.float32)

        return carry

    lax.fori_loop(0, npoint, step, 0)
    per = out_ref.shape[1]

    def emit(d, carry):
        for k in range(per):
            t = owner_ref[d * per + k]
            inv = floor_ref[t]
            for c in range(ch):
                out_ref[d, k, c] = (acc_ref[t, c] / inv).astype(jnp.bfloat16)
        return carry

    lax.fori_loop(0, npoint, emit, 0)


def normalise(ids, owner, tiles, floored):
    npoint, s_dev, ch, rows, tile = tiles.shape
    nsky = owner.shape[0]
    return pl.pallas_call(
        normal_body,
        in_specs=[
            pl.BlockSpec(memory_space=pltpu.SMEM),
            pl.BlockSpec(memory_space=pltpu.SMEM),
            pl.BlockSpec(memory_space=pltpu.VMEM),
            pl.BlockSpec(memory_space=pltpu.VMEM),
        ],
        out_specs=pl.BlockSpec(memory_space=pltpu.VMEM),
        out_shape=jax.ShapeDtypeStruct((npoint, nsky // npoint, ch, rows, tile), jnp.bfloat16),
        scratch_shapes=[pltpu.VMEM((nsky, ch, rows, tile), jnp.float32)],
        compiler_params=params(),
    )(ids, owner, tiles, floored)


def conv_body(tiles_ref, psf_ref, out_ref):
    tile = psf_ref.shape[-1]
    for c in range(tiles_ref.shape[2]):
        plane = tiles_ref[:, 0, c].reshape(tile, tile)
        left = lax.dot_general(
            plane, psf_ref[c, 1], (((1,), (1,)), ((), ())), preferred_element_type=jnp.float32
        ).astype(jnp.bfloat16)
        out_ref[0, c] = jnp.dot(
            psf_ref[c, 0], left, preferred_element_type=jnp.float32
        ).astype(jnp.bfloat16)


def convolve(tiles, psf):
    npoint, per, ch, rows, tile = tiles.shape
    return pl.pallas_call(
        conv_body,
        grid=(per,),
        in_specs=[
            pl.BlockSpec((npoint, 1, ch, rows, tile), lambda i: (0, i, 0, 0, 0)),
            pl.BlockSpec(psf.shape, lambda i: (0, 0, 0, 0)),
        ],
        out_specs=pl.BlockSpec((1, ch, tile, tile), lambda i: (i, 0, 0, 0)),
        out_shape=jax.ShapeDtypeStruct((per, ch, tile, tile), jnp.bfloat16),
        compiler_params=params(),
    )(tiles, psf)


def row_split_shards(images, beam, exponent, intersection, counts, owner, psf):
    pts, slots, ch, tile, _ = images.shape
    npoint = lax.axis_size("point")
    nchan = lax.axis_size("chan")
    s_dev = pts * slots
    part = s_dev // nchan
    nsky = owner.shape[0]
    chan_pos = lax.axis_index("chan")

    live = jnp.arange(slots)[None, :] < counts[:, None]
    own_ids = jnp.where(live, intersection, nsky).reshape(1, s_dev)
    ids = lax.all_to_all(
        jnp.broadcast_to(own_ids, (npoint, s_dev)), "point", split_axis=0, concat_axis=0, tiled=True
    )
    own_beam = lax.dynamic_slice_in_dim(
        beam.reshape(s_dev, tile, tile), chan_pos * part, part, axis=0
    )
    beam_rows = lax.all_to_all(
        split_rows(own_beam, npoint), "point", split_axis=0, concat_axis=0, tiled=True
    )
    own_exp = lax.dynamic_slice_in_dim(exponent, chan_pos * ch, ch)
    weighted = weigh(own_exp, images, beam, npoint)
    tiles = lax.all_to_all(weighted, "point", split_axis=0, concat_axis=0, tiled=True)
    beams = lax.all_gather(beam_rows, "chan", axis=0, tiled=False)
    floored = totals(ids, exponent, beams, nsky)
    ordered = normalise(ids, owner, tiles, floored)
    returned = lax.all_to_all(ordered, "point", split_axis=0, concat_axis=0, tiled=True)
    return convolve(returned, psf)


INNER = 4
PLANES = 4
SEND, OWN, RECV, COUNT = 0, 16, 20, 24
PLAN_ROWS = 32
NEAR = 10
FAR = (6, 8, 10)
WIDE = 14


def vmem():
    return pl.BlockSpec(memory_space=pltpu.VMEM)


def smem():
    return pl.BlockSpec(memory_space=pltpu.SMEM)


def plan_body(here_ref, *refs):
    ids, (owner_ref, plan_ref, choice_ref, row_ref, tally_ref) = refs[:INNER], refs[INNER:]
    s_dev = ids[0].shape[1]
    nsky = owner_ref.shape[0]
    per_plane = nsky // PLANES
    most = plan_ref.shape[1] - 1
    wide = 2 * PLANES
    local_tally = PLANES * wide
    plane = here_ref[2]
    row_ref[nsky] = nsky

    def place(r, carry):
        row_ref[owner_ref[r]] = r
        return carry

    lax.fori_loop(0, nsky, place, 0, unroll=8)
    for n in range(PLANES * wide):
        tally_ref[n] = 0
    for k0 in range(PLANES):
        source = plane ^ k0
        for a in range(INNER):
            if k0 == 0:
                for k in range(wide):
                    tally_ref[local_tally + k] = 0
            for s in range(s_dev):
                row = row_ref[ids[a][k0, s]]
                far = lax.div(row, per_plane) ^ source
                n = tally_ref[k0 * wide + far]
                tally_ref[k0 * wide + far] = n + 1
                local = row - plane * per_plane
                if k0 > 0:
                    plan_ref[RECV + k0, jnp.where(far == k0, n, most)] = local
                else:
                    m = tally_ref[local_tally + far]
                    tally_ref[local_tally + far] = m + 1
                    known = far < PLANES
                    line = SEND + a * PLANES + jnp.where(known, far, 0)
                    plan_ref[line, jnp.where(known, m, most)] = s
                    plan_ref[OWN + a, jnp.where(far == 0, m, most)] = local
            if k0 == 0:
                for k in range(PLANES):
                    plan_ref[COUNT, a * PLANES + k] = tally_ref[local_tally + k]
        plan_ref[COUNT + 1, k0] = tally_ref[k0 * wide + k0]
    need = []
    for k in range(1, PLANES):
        value = tally_ref[k]
        for k0 in range(1, PLANES):
            value = jnp.maximum(value, tally_ref[k0 * wide + k])
        need.append(value)
    steps = len(FAR)
    choice = jnp.int32(0)
    for cap in FAR[:-1]:
        choice = choice + jnp.where(need[1] > cap, steps, 0) + jnp.where(need[2] > cap, 1, 0)
    far = jnp.maximum(need[1], need[2])
    over = (need[0] > NEAR) | (far > FAR[-1])
    choice = jnp.where(over, steps * steps, choice)
    choice = jnp.where(jnp.maximum(need[0], far) > WIDE, steps * steps + 1, choice)
    choice_ref[0] = choice


def capacities(most):
    return [(NEAR, a, b) for a in FAR for b in FAR] + [(WIDE,) * 3, (most,) * 3]


def make_plan(here, ids, owner):
    most = INNER * ids[0].shape[1]
    return pl.pallas_call(
        plan_body,
        in_specs=[smem()] * (2 + INNER),
        out_specs=[smem()] * 2,
        out_shape=[
            jax.ShapeDtypeStruct((PLAN_ROWS, most + 1), jnp.int32),
            jax.ShapeDtypeStruct((1,), jnp.int32),
        ],
        scratch_shapes=[
            pltpu.SMEM((owner.shape[0] + 1,), jnp.int32),
            pltpu.SMEM(((PLANES + 1) * 2 * PLANES,), jnp.int32),
        ],
        compiler_params=params(),
    )(here, *ids, owner)


def quarter_body(chan, share, here_ref, exp_ref, images_ref, beam_ref, *outs):
    slots, tile = images_ref.shape[1], images_ref.shape[-1]
    rows = tile // INNER
    inner = here_ref[0]
    for j in range(INNER):
        base = pl.multiple_of((inner ^ j) * rows, rows)

        def step(s, carry):
            if share:
                half = pl.multiple_of(base + here_ref[1] * share, share)
                outs[j][s, :share] = beam_ref[0, s, pl.ds(half, share), :]
            logs = jnp.log2(beam_ref[0, s, pl.ds(base, rows), :].astype(jnp.float32))
            plane = images_ref[0, s, 0, pl.ds(base, rows), :].astype(jnp.float32)
            outs[j][s, share:] = (jnp.exp2(exp_ref[chan] * logs) * plane).astype(jnp.bfloat16)
            return carry

        lax.fori_loop(0, slots, step, 0)


def quarters(here, own_exp, images, beam, chan, share):
    pts, slots, ch, tile, _ = images.shape
    rows = tile // INNER + share
    return pl.pallas_call(
        functools.partial(quarter_body, chan, share),
        grid=(pts,),
        in_specs=[
            smem(),
            smem(),
            pl.BlockSpec((1, slots, 1, tile, tile), lambda p: (p, 0, chan, 0, 0)),
            pl.BlockSpec((1, slots, tile, tile), lambda p: (p, 0, 0, 0)),
        ],
        out_specs=[pl.BlockSpec((slots, rows, tile), lambda p: (p, 0, 0))] * INNER,
        out_shape=[jax.ShapeDtypeStruct((pts * slots, rows, tile), jnp.bfloat16)] * INNER,
        compiler_params=params(),
    )(here, own_exp, images, beam)


def pack_body(plan_ref, *refs):
    got, outs = refs[:INNER], refs[INNER:]
    for k, out in enumerate(outs, 1):
        start = jnp.int32(0)
        for j in range(INNER):
            count = plan_ref[COUNT, j * PLANES + k]

            def step(n, carry):
                out[start + n] = got[j][plan_ref[SEND + j * PLANES + k, n]]
                return carry

            lax.fori_loop(0, count, step, 0)
            start = start + count


def pack(plan, got, caps):
    _, rows, tile = got[0].shape
    return pl.pallas_call(
        pack_body,
        in_specs=[smem()] + [vmem()] * INNER,
        out_specs=[vmem()] * len(caps),
        out_shape=[jax.ShapeDtypeStruct((cap, rows, tile), jnp.bfloat16) for cap in caps],
        compiler_params=params(),
    )(plan, *got)


def each_tile(plan_ref, got, recv, lines, add):
    for j in range(INNER):

        def own(n, carry):
            add(plan_ref[OWN + j, n], got[j][plan_ref[SEND + j * PLANES, n], lines, :])
            return carry

        lax.fori_loop(0, plan_ref[COUNT, j * PLANES], own, 0)
    for k, tiles in enumerate(recv, 1):

        def other(n, carry):
            add(plan_ref[RECV + k, n], tiles[n, lines, :])
            return carry

        lax.fori_loop(0, plan_ref[COUNT + 1, k], other, 0)


def inverse_body(share, here_ref, plan_ref, exp_ref, *refs):
    got, recv, outs, acc_ref = refs[:INNER], refs[INNER:-1 - INNER], refs[-1 - INNER:-1], refs[-1]
    ch = exp_ref.shape[0]
    per = outs[0].shape[0]
    acc_ref[...] = jnp.zeros_like(acc_ref)

    def add(t, tile):
        logs = jnp.log2(tile.astype(jnp.float32))
        weight = jnp.zeros_like(logs)
        for c in range(ch):
            weight = weight + jnp.exp2((2.0 * exp_ref[c]) * logs)
        acc_ref[t] += weight * (1.0 / ch)

    each_tile(plan_ref, got, recv, slice(0, share), add)
    for j in range(INNER):
        part = acc_ref[pl.ds((here_ref[0] ^ j) * per, per)]
        outs[j][...] = (1.0 / jnp.maximum(part, weight_floor)).astype(jnp.bfloat16)


def inverse_totals(here, plan, exponent, got, recv, share, per_plane):
    shape = (per_plane, share, got[0].shape[-1])
    out = jax.ShapeDtypeStruct((per_plane // INNER,) + shape[1:], jnp.bfloat16)
    return pl.pallas_call(
        functools.partial(inverse_body, share),
        in_specs=[smem()] * 3 + [vmem()] * (INNER + len(recv)),
        out_specs=[vmem()] * INNER,
        out_shape=[out] * INNER,
        scratch_shapes=[pltpu.VMEM(shape, jnp.float32)],
        compiler_params=params(),
    )(here, plan, exponent, *got, *recv)


def sum_body(skip, here_ref, plan_ref, *refs):
    got, recv, outs, acc_ref = refs[:INNER], refs[INNER:-1 - INNER], refs[-1 - INNER:-1], refs[-1]
    per, rows = outs[0].shape[:2]
    acc_ref[...] = jnp.zeros_like(acc_ref)

    def add(t, tile):
        acc_ref[t] += tile.astype(jnp.float32)

    each_tile(plan_ref, got, recv, slice(skip, skip + rows), add)
    for j in range(INNER):

        def emit(k, carry):
            outs[j][k] = acc_ref[(here_ref[0] ^ j) * per + k].astype(jnp.bfloat16)
            return carry

        lax.fori_loop(0, per, emit, 0)


def sum_tiles(here, plan, got, recv, skip, per_plane):
    _, rows, tile = got[0].shape
    rows = rows - skip
    return pl.pallas_call(
        functools.partial(sum_body, skip),
        in_specs=[smem()] * 2 + [vmem()] * (INNER + len(recv)),
        out_specs=[vmem()] * INNER,
        out_shape=[jax.ShapeDtypeStruct((per_plane // INNER, rows, tile), jnp.bfloat16)] * INNER,
        scratch_shapes=[pltpu.VMEM((per_plane, rows, tile), jnp.float32)],
        compiler_params=params(),
    )(here, plan, *got, *recv)


def plane_conv_body(nchan, here_ref, psf_ref, *refs):
    quarter, inverse, out_ref, left_ref = refs[:INNER], refs[INNER:INNER + nchan], refs[-2], refs[-1]
    per, rows, tile = quarter[0].shape
    share = inverse[0].shape[2]
    inner, chan = here_ref[0], here_ref[1]
    for j in range(INNER):
        for y in range(nchan):
            part = pl.ds(pl.multiple_of((chan ^ y) * share, share), share)
            value = quarter[j][:, part, :].astype(jnp.float32) * inverse[y][j].astype(jnp.float32)
            left = lax.dot_general(
                value.astype(jnp.bfloat16).reshape(per * share, tile),
                psf_ref[0, 1],
                (((1,), (1,)), ((), ())),
                preferred_element_type=jnp.float32,
            )
            start = pl.multiple_of((inner ^ j) * rows + (chan ^ y) * share, share)
            left = left.astype(jnp.bfloat16).reshape(per, share, tile)
            left_ref[:, pl.ds(start, share), :] = left
    for t in range(per):
        out_ref[t, 0] = jnp.dot(
            psf_ref[0, 0], left_ref[t], preferred_element_type=jnp.float32
        ).astype(jnp.bfloat16)


def plane_convolve(here, psf, quarter, inverses, chan, before):
    per, rows, tile = quarter[0].shape
    ch, share = psf.shape[0], inverses[0].shape[2]
    extra = [] if before is None else [before]
    block = per // 2
    return pl.pallas_call(
        functools.partial(plane_conv_body, len(inverses)),
        grid=(per // block,),
        in_specs=[smem(), pl.BlockSpec((1, 2, tile, tile), lambda t: (chan, 0, 0, 0))]
        + [pl.BlockSpec((block, rows, tile), lambda t: (t, 0, 0))] * INNER
        + [pl.BlockSpec((INNER, block, share, tile), lambda t: (0, t, 0, 0))] * len(inverses)
        + [pl.BlockSpec(memory_space=pl.ANY)] * len(extra),
        out_specs=pl.BlockSpec((block, 1, tile, tile), lambda t: (t, chan, 0, 0)),
        out_shape=jax.ShapeDtypeStruct((per, ch, tile, tile), jnp.bfloat16),
        scratch_shapes=[pltpu.VMEM((block, tile, tile), jnp.bfloat16)],
        input_output_aliases={2 + INNER + len(inverses): 0} if extra else {},
        compiler_params=params(),
    )(here, psf, *quarter, *inverses, *extra)


def swap(value, axis, distance):
    n = lax.axis_size(axis)
    return lax.ppermute(value, axis, [(d, d ^ distance) for d in range(n)])


def inside(parts):
    near = swap(parts[1], "point", 1)
    across = swap(parts[2], "point", 2)
    last, near = lax.optimization_barrier((parts[3], near))
    return [parts[0], near, across, swap(last, "point", 3)]


def between(parts):
    return [swap(part, "point", (k + 1) * INNER) for k, part in enumerate(parts)]


def plane_shards(images, beam, exponent, intersection, counts, owner, psf):
    pts, slots, ch, tile, _ = images.shape
    npoint, nchan = lax.axis_size("point"), lax.axis_size("chan")
    s_dev = pts * slots
    nsky = owner.shape[0]
    per_plane = nsky // PLANES
    share = tile // INNER // nchan
    chan_pos, point_pos = lax.axis_index("chan"), lax.axis_index("point")
    here = jnp.stack([point_pos % INNER, chan_pos, point_pos // INNER]).astype(jnp.int32)
    own_exp = lax.dynamic_slice_in_dim(exponent, chan_pos * ch, ch)

    live = jnp.arange(slots)[None, :] < counts[:, None]
    own_ids = jnp.where(live, intersection, nsky).reshape(1, s_dev)
    column = [own_ids] + [swap(own_ids, "point", k * INNER) for k in range(1, PLANES)]
    column = jnp.concatenate(column, axis=0)
    ids = [column] + [swap(column, "point", j) for j in range(1, INNER)]
    first, ids = lax.optimization_barrier((quarters(here, own_exp, images, beam, 0, share), ids))
    first = inside(first)
    plan, choice = make_plan(here, ids, owner)
    later = [quarters(here, own_exp, images, beam, c, 0) for c in range(1, ch)]

    def branch(caps):
        def run(here, plan, first, later, exponent, psf):
            got, packed, recv = [first], [pack(plan, first, caps)], []
            for c in range(1, ch):
                recv.append(between(packed[-1]))
                parts, _ = lax.optimization_barrier((later[c - 1], packed[-1]))
                got.append(inside(parts))
                packed.append(pack(plan, got[-1], caps))
                packed[-1], recv[-1] = lax.optimization_barrier((packed[-1], recv[-1]))
            recv.append(between(packed[-1]))
            inverse = inverse_totals(here, plan, exponent, first, recv[0], share, per_plane)
            inverse = inside(inverse)
            numer = []
            for c in range(ch):
                if c:
                    recv[c], numer[-1], inverse = lax.optimization_barrier((recv[c], numer[-1], inverse))
                part = sum_tiles(here, plan, got[c], recv[c], 0 if c else share, per_plane)
                numer.append(inside(part))
            inverse = jnp.stack(inverse)
            inverses = [inverse] + [swap(inverse, "chan", y) for y in range(1, nchan)]
            out = None
            for c in range(ch):
                out = plane_convolve(here, psf, numer[c], inverses, c, out)
            return out

        return run

    branches = [branch(caps) for caps in capacities(INNER * s_dev)]
    return lax.switch(choice[0], branches, here, plan, first, later, exponent, psf)


def shards(*args):
    if lax.axis_size("point") == PLANES * INNER:
        return plane_shards(*args)
    return row_split_shards(*args)


def solution(mesh):
    return jax.shard_map(
        shards,
        mesh=mesh,
        in_specs=(
            P("point", None, "chan", None, None),
            P("point", None, None, None),
            P(),
            P("point", None),
            P("point"),
            P(),
            P("chan", None, None, None),
        ),
        out_specs=P("point", "chan", None, None),
        check_vma=False,
    )
```

```python
import functools

import jax
import jax.numpy as jnp
from jax import lax
from jax.experimental import pallas as pl
from jax.experimental.pallas import tpu as pltpu
from jax.sharding import PartitionSpec as P

weight_floor = 0.05
VMEM_LIMIT = 48 * 1024 * 1024


def params():
    return pltpu.CompilerParams(vmem_limit_bytes=VMEM_LIMIT)


def put_rows(out_ref, at, value):
    group, rows = out_ref.shape[0], out_ref.shape[-2]
    for g in range(group):
        out_ref[(g,) + at] = value[g * rows:(g + 1) * rows].astype(jnp.bfloat16)


def row_block(tile, npoint):
    rows = tile // npoint
    block = max(rows, 16)
    return rows, block, block // rows


def weight_body(exp_ref, images_ref, beam_ref, out_ref):
    slots = images_ref.shape[1]
    for p in range(images_ref.shape[0]):
        for s in range(slots):
            logs = jnp.log(beam_ref[p, s].astype(jnp.float32))
            for c in range(images_ref.shape[2]):
                power = jnp.exp(exp_ref[c] * logs)
                plane = images_ref[p, s, c].astype(jnp.float32)
                put_rows(out_ref, (p * slots + s, c), power * plane)


def weigh(own_exp, images, beam, npoint):
    pts, slots, ch, tile, _ = images.shape
    rows, block, group = row_block(tile, npoint)
    return pl.pallas_call(
        weight_body,
        grid=(npoint // group,),
        in_specs=[
            pl.BlockSpec(memory_space=pltpu.SMEM),
            pl.BlockSpec((pts, slots, ch, block, tile), lambda i: (0, 0, 0, i, 0)),
            pl.BlockSpec((pts, slots, block, tile), lambda i: (0, 0, i, 0)),
        ],
        out_specs=pl.BlockSpec((group, pts * slots, ch, rows, tile), lambda i: (i, 0, 0, 0, 0)),
        out_shape=jax.ShapeDtypeStruct((npoint, pts * slots, ch, rows, tile), jnp.bfloat16),
        compiler_params=params(),
    )(own_exp, images, beam)


def split_body(beam_ref, out_ref):
    for s in range(beam_ref.shape[0]):
        put_rows(out_ref, (s,), beam_ref[s].astype(jnp.float32))


def split_rows(beam, npoint):
    s, tile, _ = beam.shape
    rows, block, group = row_block(tile, npoint)
    return pl.pallas_call(
        split_body,
        grid=(npoint // group,),
        in_specs=[pl.BlockSpec((s, block, tile), lambda i: (0, i, 0))],
        out_specs=pl.BlockSpec((group, s, rows, tile), lambda i: (i, 0, 0, 0)),
        out_shape=jax.ShapeDtypeStruct((npoint, s, rows, tile), jnp.bfloat16),
        compiler_params=params(),
    )(beam)


def total_body(s_dev, ids_ref, exp_ref, beam_ref, out_ref, acc_ref):
    nchan, npoint, part = beam_ref.shape[:3]
    nsky = out_ref.shape[0]
    ch = exp_ref.shape[0]
    acc_ref[...] = jnp.zeros_like(acc_ref)

    def step(d, carry):
        for share in range(nchan):
            for k in range(part):
                at = ids_ref[d, share * part + k]

                @pl.when(at < nsky)
                def _():
                    logs = jnp.log(beam_ref[share, d, k].astype(jnp.float32))
                    pw = jnp.zeros_like(logs)
                    for c in range(ch):
                        power = jnp.exp(exp_ref[c] * logs)
                        pw = pw + power * power
                    acc_ref[at] += pw * (1.0 / ch)

        return carry

    lax.fori_loop(0, npoint, step, 0)
    out_ref[...] = jnp.maximum(acc_ref[...], weight_floor)


def totals(ids, exponent, beams, nsky):
    rows, tile = beams.shape[3:]
    s_dev = ids.shape[1]
    return pl.pallas_call(
        functools.partial(total_body, s_dev),
        in_specs=[
            pl.BlockSpec(memory_space=pltpu.SMEM),
            pl.BlockSpec(memory_space=pltpu.SMEM),
            pl.BlockSpec(memory_space=pltpu.VMEM),
        ],
        out_specs=pl.BlockSpec(memory_space=pltpu.VMEM),
        out_shape=jax.ShapeDtypeStruct((nsky, rows, tile), jnp.float32),
        scratch_shapes=[pltpu.VMEM((nsky, rows, tile), jnp.float32)],
        compiler_params=params(),
    )(ids, exponent, beams)


def normal_body(ids_ref, owner_ref, tiles_ref, floor_ref, out_ref, acc_ref):
    npoint, s_dev, ch = tiles_ref.shape[:3]
    nsky = floor_ref.shape[0]
    acc_ref[...] = jnp.zeros_like(acc_ref)

    def step(d, carry):
        for s in range(s_dev):
            at = ids_ref[d, s]

            @pl.when(at < nsky)
            def _():
                acc_ref[at] += tiles_ref[d, s].astype(jnp.float32)

        return carry

    lax.fori_loop(0, npoint, step, 0)
    per = out_ref.shape[1]

    def emit(d, carry):
        for k in range(per):
            t = owner_ref[d * per + k]
            inv = floor_ref[t]
            for c in range(ch):
                out_ref[d, k, c] = (acc_ref[t, c] / inv).astype(jnp.bfloat16)
        return carry

    lax.fori_loop(0, npoint, emit, 0)


def normalise(ids, owner, tiles, floored):
    npoint, s_dev, ch, rows, tile = tiles.shape
    nsky = owner.shape[0]
    return pl.pallas_call(
        normal_body,
        in_specs=[
            pl.BlockSpec(memory_space=pltpu.SMEM),
            pl.BlockSpec(memory_space=pltpu.SMEM),
            pl.BlockSpec(memory_space=pltpu.VMEM),
            pl.BlockSpec(memory_space=pltpu.VMEM),
        ],
        out_specs=pl.BlockSpec(memory_space=pltpu.VMEM),
        out_shape=jax.ShapeDtypeStruct((npoint, nsky // npoint, ch, rows, tile), jnp.bfloat16),
        scratch_shapes=[pltpu.VMEM((nsky, ch, rows, tile), jnp.float32)],
        compiler_params=params(),
    )(ids, owner, tiles, floored)


def conv_body(tiles_ref, psf_ref, out_ref):
    tile = psf_ref.shape[-1]
    for c in range(tiles_ref.shape[2]):
        plane = tiles_ref[:, 0, c].reshape(tile, tile)
        left = lax.dot_general(
            plane, psf_ref[c, 1], (((1,), (1,)), ((), ())), preferred_element_type=jnp.float32
        ).astype(jnp.bfloat16)
        out_ref[0, c] = jnp.dot(
            psf_ref[c, 0], left, preferred_element_type=jnp.float32
        ).astype(jnp.bfloat16)


def convolve(tiles, psf):
    npoint, per, ch, rows, tile = tiles.shape
    return pl.pallas_call(
        conv_body,
        grid=(per,),
        in_specs=[
            pl.BlockSpec((npoint, 1, ch, rows, tile), lambda i: (0, i, 0, 0, 0)),
            pl.BlockSpec(psf.shape, lambda i: (0, 0, 0, 0)),
        ],
        out_specs=pl.BlockSpec((1, ch, tile, tile), lambda i: (i, 0, 0, 0)),
        out_shape=jax.ShapeDtypeStruct((per, ch, tile, tile), jnp.bfloat16),
        compiler_params=params(),
    )(tiles, psf)


def row_split_shards(images, beam, exponent, intersection, counts, owner, psf):
    pts, slots, ch, tile, _ = images.shape
    npoint = lax.axis_size("point")
    nchan = lax.axis_size("chan")
    s_dev = pts * slots
    part = s_dev // nchan
    nsky = owner.shape[0]
    chan_pos = lax.axis_index("chan")

    live = jnp.arange(slots)[None, :] < counts[:, None]
    own_ids = jnp.where(live, intersection, nsky).reshape(1, s_dev)
    ids = lax.all_to_all(
        jnp.broadcast_to(own_ids, (npoint, s_dev)), "point", split_axis=0, concat_axis=0, tiled=True
    )
    own_beam = lax.dynamic_slice_in_dim(
        beam.reshape(s_dev, tile, tile), chan_pos * part, part, axis=0
    )
    beam_rows = lax.all_to_all(
        split_rows(own_beam, npoint), "point", split_axis=0, concat_axis=0, tiled=True
    )
    own_exp = lax.dynamic_slice_in_dim(exponent, chan_pos * ch, ch)
    weighted = weigh(own_exp, images, beam, npoint)
    tiles = lax.all_to_all(weighted, "point", split_axis=0, concat_axis=0, tiled=True)
    beams = lax.all_gather(beam_rows, "chan", axis=0, tiled=False)
    floored = totals(ids, exponent, beams, nsky)
    ordered = normalise(ids, owner, tiles, floored)
    returned = lax.all_to_all(ordered, "point", split_axis=0, concat_axis=0, tiled=True)
    return convolve(returned, psf)


INNER = 4
PLANES = 4
SEND, OWN, RECV, COUNT = 0, 16, 20, 24
PLAN_ROWS = 32
FAR = (7, 9)
NEAR = 10
WIDE = (11, 14)


def vmem():
    return pl.BlockSpec(memory_space=pltpu.VMEM)


def smem():
    return pl.BlockSpec(memory_space=pltpu.SMEM)


def plan_body(here_ref, *refs):
    ids, (owner_ref, plan_ref, choice_ref, row_ref, tally_ref) = refs[:INNER], refs[INNER:]
    s_dev = ids[0].shape[1]
    nsky = owner_ref.shape[0]
    per_plane = nsky // PLANES
    most = plan_ref.shape[1] - 1
    wide = 2 * PLANES
    local_tally = PLANES * wide
    plane = here_ref[2]
    row_ref[nsky] = nsky

    def place(r, carry):
        row_ref[owner_ref[r]] = r
        return carry

    lax.fori_loop(0, nsky, place, 0, unroll=8)
    for n in range(PLANES * wide):
        tally_ref[n] = 0
    for k0 in range(PLANES):
        source = plane ^ k0
        for a in range(INNER):
            if k0 == 0:
                for k in range(wide):
                    tally_ref[local_tally + k] = 0
            for s in range(s_dev):
                row = row_ref[ids[a][k0, s]]
                far = lax.div(row, per_plane) ^ source
                n = tally_ref[k0 * wide + far]
                tally_ref[k0 * wide + far] = n + 1
                local = row - plane * per_plane
                if k0 > 0:
                    plan_ref[RECV + k0, jnp.where(far == k0, n, most)] = local
                else:
                    m = tally_ref[local_tally + far]
                    tally_ref[local_tally + far] = m + 1
                    known = far < PLANES
                    line = SEND + a * PLANES + jnp.where(known, far, 0)
                    plan_ref[line, jnp.where(known, m, most)] = s
                    plan_ref[OWN + a, jnp.where(far == 0, m, most)] = local
            if k0 == 0:
                for k in range(PLANES):
                    plan_ref[COUNT, a * PLANES + k] = tally_ref[local_tally + k]
        plan_ref[COUNT + 1, k0] = tally_ref[k0 * wide + k0]
    need = []
    for k in range(1, PLANES):
        value = tally_ref[k]
        for k0 in range(1, PLANES):
            value = jnp.maximum(value, tally_ref[k0 * wide + k])
        need.append(value)
    steps = len(FAR)
    choice = jnp.int32(0)
    for cap in FAR[:-1]:
        choice = choice + jnp.where(need[1] > cap, steps, 0) + jnp.where(need[2] > cap, 1, 0)
    most_needed = jnp.maximum(need[0], jnp.maximum(need[1], need[2]))
    over = (need[0] > NEAR) | (jnp.maximum(need[1], need[2]) > FAR[-1])
    wide = jnp.int32(steps * steps)
    for cap in WIDE:
        wide = wide + (most_needed > cap).astype(jnp.int32)
    choice_ref[0] = jnp.where(over, wide, choice)


def capacities(most):
    return [(NEAR, a, b) for a in FAR for b in FAR] + [(cap,) * 3 for cap in WIDE + (most,)]


def make_plan(here, ids, owner):
    most = INNER * ids[0].shape[1]
    return pl.pallas_call(
        plan_body,
        in_specs=[smem()] * (2 + INNER),
        out_specs=[smem()] * 2,
        out_shape=[
            jax.ShapeDtypeStruct((PLAN_ROWS, most + 1), jnp.int32),
            jax.ShapeDtypeStruct((1,), jnp.int32),
        ],
        scratch_shapes=[
            pltpu.SMEM((owner.shape[0] + 1,), jnp.int32),
            pltpu.SMEM(((PLANES + 1) * 2 * PLANES,), jnp.int32),
        ],
        compiler_params=params(),
    )(here, *ids, owner)


def quarter_body(chan, share, channels, here_ref, exp_ref, images_ref, beam_ref, *outs):
    slots, tile = images_ref.shape[1], images_ref.shape[-1]
    rows = tile // INNER
    inner = here_ref[0]
    for j in range(INNER):
        base = pl.multiple_of((inner ^ j) * rows, rows)

        def step(s, carry):
            if share:
                half = pl.multiple_of(base + here_ref[1] * share, share)
                outs[j][s, :share] = beam_ref[0, s, pl.ds(half, share), :]
            logs = jnp.log2(beam_ref[0, s, pl.ds(base, rows), :].astype(jnp.float32))
            plane = images_ref[0, s, 0, pl.ds(base, rows), :].astype(jnp.float32)
            outs[j][s, share:] = (jnp.exp2(exp_ref[here_ref[1] * channels + chan] * logs) * plane).astype(jnp.bfloat16)
            return carry

        lax.fori_loop(0, slots, step, 0)


def quarters(here, exponent, images, beam, chan, share):
    pts, slots, ch, tile, _ = images.shape
    rows = tile // INNER + share
    return pl.pallas_call(
        functools.partial(quarter_body, chan, share, ch),
        grid=(pts,),
        in_specs=[
            smem(),
            smem(),
            pl.BlockSpec((1, slots, 1, tile, tile), lambda p: (p, 0, chan, 0, 0)),
            pl.BlockSpec((1, slots, tile, tile), lambda p: (p, 0, 0, 0)),
        ],
        out_specs=[pl.BlockSpec((slots, rows, tile), lambda p: (p, 0, 0))] * INNER,
        out_shape=[jax.ShapeDtypeStruct((pts * slots, rows, tile), jnp.bfloat16)] * INNER,
        compiler_params=params(),
    )(here, exponent, images, beam)


def pack_body(plan_ref, *refs):
    got, outs = refs[:INNER], refs[INNER:]
    for k, out in enumerate(outs, 1):
        start = jnp.int32(0)
        for j in range(INNER):
            count = plan_ref[COUNT, j * PLANES + k]

            def step(n, carry):
                out[start + n] = got[j][plan_ref[SEND + j * PLANES + k, n]]
                return carry

            lax.fori_loop(0, count, step, 0)
            start = start + count


def pack(plan, got, caps):
    _, rows, tile = got[0].shape
    return pl.pallas_call(
        pack_body,
        in_specs=[smem()] + [vmem()] * INNER,
        out_specs=[vmem()] * len(caps),
        out_shape=[jax.ShapeDtypeStruct((cap, rows, tile), jnp.bfloat16) for cap in caps],
        compiler_params=params(),
    )(plan, *got)


def each_tile(plan_ref, got, recv, add):
    for j in range(INNER):

        def own(n, carry):
            add(plan_ref[OWN + j, n], got[j][plan_ref[SEND + j * PLANES, n]])
            return carry

        lax.fori_loop(0, plan_ref[COUNT, j * PLANES], own, 0)
    for k, tiles in enumerate(recv, 1):

        def other(n, carry):
            add(plan_ref[RECV + k, n], tiles[n])
            return carry

        lax.fori_loop(0, plan_ref[COUNT + 1, k], other, 0)


def sum_body(share, here_ref, plan_ref, exp_ref, *refs):
    got, recv, outs = refs[:INNER], refs[INNER:2 * INNER - 1], refs[2 * INNER - 1:3 * INNER - 1]
    acc_ref = refs[3 * INNER - 1]
    ch = exp_ref.shape[0]
    per, rows = outs[0].shape[:2]
    acc_ref[...] = jnp.zeros_like(acc_ref)

    def add(t, tile):
        acc_ref[t, share:] += tile[share:].astype(jnp.float32)
        if share:
            logs = jnp.log2(tile[:share].astype(jnp.float32))
            weight = jnp.zeros_like(logs)
            for c in range(ch):
                weight = weight + jnp.exp2((2.0 * exp_ref[c]) * logs)
            acc_ref[t, :share] += weight * (1.0 / ch)

    each_tile(plan_ref, got, recv, add)
    for j in range(INNER):

        def emit(k, carry):
            t = (here_ref[0] ^ j) * per + k
            outs[j][k, share:] = acc_ref[t, share:].astype(jnp.bfloat16)
            if share:
                total = jnp.maximum(acc_ref[t, :share], weight_floor)
                outs[j][k, :share] = (1.0 / total).astype(jnp.bfloat16)
            return carry

        lax.fori_loop(0, per, emit, 0)


def sum_tiles(here, plan, exponent, got, recv, share, per_plane):
    _, rows, tile = got[0].shape
    return pl.pallas_call(
        functools.partial(sum_body, share),
        in_specs=[smem()] * 3 + [vmem()] * (INNER + len(recv)),
        out_specs=[vmem()] * INNER,
        out_shape=[jax.ShapeDtypeStruct((per_plane // INNER, rows, tile), jnp.bfloat16)] * INNER,
        scratch_shapes=[pltpu.VMEM((per_plane, rows, tile), jnp.float32)],
        compiler_params=params(),
    )(here, plan, exponent, *got, *recv)


def plane_conv_body(nchan, skip, here_ref, psf_ref, *refs):
    quarter, inverse, out_ref, left_ref = refs[:INNER], refs[INNER:INNER + nchan], refs[-2], refs[-1]
    per, rows, tile = quarter[0].shape
    rows = rows - skip
    share = inverse[0].shape[2]
    inner, chan = here_ref[0], here_ref[1]
    for j in range(INNER):
        for y in range(nchan):
            part = pl.ds(pl.multiple_of(skip + (chan ^ y) * share, share), share)
            value = quarter[j][:, part, :].astype(jnp.float32) * inverse[y][j].astype(jnp.float32)
            left = lax.dot_general(
                value.astype(jnp.bfloat16).reshape(per * share, tile),
                psf_ref[0, 1],
                (((1,), (1,)), ((), ())),
                preferred_element_type=jnp.float32,
            )
            start = pl.multiple_of((inner ^ j) * rows + (chan ^ y) * share, share)
            left = left.astype(jnp.bfloat16).reshape(per, share, tile)
            left_ref[:, pl.ds(start, share), :] = left
    for t in range(per):
        out_ref[t, 0] = jnp.dot(
            psf_ref[0, 0], left_ref[t], preferred_element_type=jnp.float32
        ).astype(jnp.bfloat16)


def plane_convolve(here, psf, quarter, inverses, chan, before):
    per, rows, tile = quarter[0].shape
    ch, share = psf.shape[0], inverses[0].shape[2]
    extra = [] if before is None else [before]
    block = per // 2
    return pl.pallas_call(
        functools.partial(plane_conv_body, len(inverses), rows - tile // INNER),
        grid=(per // block,),
        in_specs=[smem(), pl.BlockSpec((1, 2, tile, tile), lambda t: (chan, 0, 0, 0))]
        + [pl.BlockSpec((block, rows, tile), lambda t: (t, 0, 0))] * INNER
        + [pl.BlockSpec((INNER, block, share, tile), lambda t: (0, t, 0, 0))] * len(inverses)
        + [pl.BlockSpec(memory_space=pl.ANY)] * len(extra),
        out_specs=pl.BlockSpec((block, 1, tile, tile), lambda t: (t, chan, 0, 0)),
        out_shape=jax.ShapeDtypeStruct((per, ch, tile, tile), jnp.bfloat16),
        scratch_shapes=[pltpu.VMEM((block, tile, tile), jnp.bfloat16)],
        input_output_aliases={2 + INNER + len(inverses): 0} if extra else {},
        compiler_params=params(),
    )(here, psf, *quarter, *inverses, *extra)


def swap(value, axis, distance):
    n = lax.axis_size(axis)
    return lax.ppermute(value, axis, [(d, d ^ distance) for d in range(n)])


def inside(parts):
    near = swap(parts[1], "point", 1)
    across = swap(parts[2], "point", 2)
    last, near = lax.optimization_barrier((parts[3], near))
    return [parts[0], near, across, swap(last, "point", 3)]


def between(parts):
    return [swap(part, "point", (k + 1) * INNER) for k, part in enumerate(parts)]


def plane_shards(images, beam, exponent, intersection, counts, owner, psf):
    pts, slots, ch, tile, _ = images.shape
    npoint, nchan = lax.axis_size("point"), lax.axis_size("chan")
    s_dev = pts * slots
    nsky = owner.shape[0]
    per_plane = nsky // PLANES
    share = tile // INNER // nchan
    chan_pos, point_pos = lax.axis_index("chan"), lax.axis_index("point")
    here = jnp.stack([point_pos % INNER, chan_pos, point_pos // INNER]).astype(jnp.int32)

    live = jnp.arange(slots)[None, :] < counts[:, None]
    own_ids = jnp.where(live, intersection, nsky).reshape(1, s_dev)
    column = [own_ids] + [swap(own_ids, "point", k * INNER) for k in range(1, PLANES)]
    column = jnp.concatenate(column, axis=0)
    ids = [column] + [swap(column, "point", j) for j in range(1, INNER)]
    first, ids = lax.optimization_barrier((quarters(here, exponent, images, beam, 0, share), ids))
    first = inside(first)
    plan, choice = make_plan(here, ids, owner)
    later = [quarters(here, exponent, images, beam, c, 0) for c in range(1, ch)]

    def branch(caps):
        def run(here, plan, first, later, exponent, psf):
            got, packed, recv = [first], [pack(plan, first, caps)], []
            for c in range(1, ch):
                recv.append(between(packed[-1]))
                parts, _ = lax.optimization_barrier((later[c - 1], packed[-1]))
                got.append([parts[0]] + [swap(parts[j], "point", j) for j in range(1, INNER)])
                packed.append(pack(plan, got[-1], caps))
                recv[-1], _ = lax.optimization_barrier((recv[-1], packed[-1]))
            recv.append(between(packed[-1]))
            numer = []
            for c in range(ch):
                if c == 1:
                    inverse = jnp.stack([part[:, :share] for part in numer[0]])
                    recv[c], inverse = lax.optimization_barrier((recv[c], inverse))
                if c + 1 < ch:
                    recv[c], recv[c + 1][0] = lax.optimization_barrier((recv[c], recv[c + 1][0]))
                part = sum_tiles(here, plan, exponent, got[c], recv[c], 0 if c else share, per_plane)
                numer.append(inside(part))
            inverses = [inverse] + [swap(inverse, "chan", y) for y in range(1, nchan)]
            out = None
            for c in range(ch - 1):
                out = plane_convolve(here, psf, numer[c], inverses, c, out)
            return numer[-1], inverses, out

        return run

    branches = [branch(caps) for caps in capacities(INNER * s_dev)]
    numer, inverses, out = lax.switch(
        choice[0], branches, here, plan, first, later, exponent, psf
    )
    return plane_convolve(here, psf, numer, inverses, ch - 1, out)


def shards(*args):
    if lax.axis_size("point") == PLANES * INNER:
        return plane_shards(*args)
    return row_split_shards(*args)


def solution(mesh):
    return jax.shard_map(
        shards,
        mesh=mesh,
        in_specs=(
            P("point", None, "chan", None, None),
            P("point", None, None, None),
            P(),
            P("point", None),
            P("point"),
            P(),
            P("chan", None, None, None),
        ),
        out_specs=P("point", "chan", None, None),
        check_vma=False,
    )
```

```python
import functools

import jax
import jax.numpy as jnp
from jax import lax
from jax.experimental import pallas as pl
from jax.experimental.pallas import tpu as pltpu
from jax.sharding import PartitionSpec as P

weight_floor = 0.05
VMEM_LIMIT = 48 * 1024 * 1024


def params():
    return pltpu.CompilerParams(vmem_limit_bytes=VMEM_LIMIT)


def put_rows(out_ref, at, value):
    group, rows = out_ref.shape[0], out_ref.shape[-2]
    for g in range(group):
        out_ref[(g,) + at] = value[g * rows:(g + 1) * rows].astype(jnp.bfloat16)


def row_block(tile, npoint):
    rows = tile // npoint
    block = max(rows, 16)
    return rows, block, block // rows


def weight_body(exp_ref, images_ref, beam_ref, out_ref):
    slots = images_ref.shape[1]
    for p in range(images_ref.shape[0]):
        for s in range(slots):
            logs = jnp.log(beam_ref[p, s].astype(jnp.float32))
            for c in range(images_ref.shape[2]):
                power = jnp.exp(exp_ref[c] * logs)
                plane = images_ref[p, s, c].astype(jnp.float32)
                put_rows(out_ref, (p * slots + s, c), power * plane)


def weigh(own_exp, images, beam, npoint):
    pts, slots, ch, tile, _ = images.shape
    rows, block, group = row_block(tile, npoint)
    return pl.pallas_call(
        weight_body,
        grid=(npoint // group,),
        in_specs=[
            pl.BlockSpec(memory_space=pltpu.SMEM),
            pl.BlockSpec((pts, slots, ch, block, tile), lambda i: (0, 0, 0, i, 0)),
            pl.BlockSpec((pts, slots, block, tile), lambda i: (0, 0, i, 0)),
        ],
        out_specs=pl.BlockSpec((group, pts * slots, ch, rows, tile), lambda i: (i, 0, 0, 0, 0)),
        out_shape=jax.ShapeDtypeStruct((npoint, pts * slots, ch, rows, tile), jnp.bfloat16),
        compiler_params=params(),
    )(own_exp, images, beam)


def split_body(beam_ref, out_ref):
    for s in range(beam_ref.shape[0]):
        put_rows(out_ref, (s,), beam_ref[s].astype(jnp.float32))


def split_rows(beam, npoint):
    s, tile, _ = beam.shape
    rows, block, group = row_block(tile, npoint)
    return pl.pallas_call(
        split_body,
        grid=(npoint // group,),
        in_specs=[pl.BlockSpec((s, block, tile), lambda i: (0, i, 0))],
        out_specs=pl.BlockSpec((group, s, rows, tile), lambda i: (i, 0, 0, 0)),
        out_shape=jax.ShapeDtypeStruct((npoint, s, rows, tile), jnp.bfloat16),
        compiler_params=params(),
    )(beam)


def total_body(s_dev, ids_ref, exp_ref, beam_ref, out_ref, acc_ref):
    nchan, npoint, part = beam_ref.shape[:3]
    nsky = out_ref.shape[0]
    ch = exp_ref.shape[0]
    acc_ref[...] = jnp.zeros_like(acc_ref)

    def step(d, carry):
        for share in range(nchan):
            for k in range(part):
                at = ids_ref[d, share * part + k]

                @pl.when(at < nsky)
                def _():
                    logs = jnp.log(beam_ref[share, d, k].astype(jnp.float32))
                    pw = jnp.zeros_like(logs)
                    for c in range(ch):
                        power = jnp.exp(exp_ref[c] * logs)
                        pw = pw + power * power
                    acc_ref[at] += pw * (1.0 / ch)

        return carry

    lax.fori_loop(0, npoint, step, 0)
    out_ref[...] = jnp.maximum(acc_ref[...], weight_floor)


def totals(ids, exponent, beams, nsky):
    rows, tile = beams.shape[3:]
    s_dev = ids.shape[1]
    return pl.pallas_call(
        functools.partial(total_body, s_dev),
        in_specs=[
            pl.BlockSpec(memory_space=pltpu.SMEM),
            pl.BlockSpec(memory_space=pltpu.SMEM),
            pl.BlockSpec(memory_space=pltpu.VMEM),
        ],
        out_specs=pl.BlockSpec(memory_space=pltpu.VMEM),
        out_shape=jax.ShapeDtypeStruct((nsky, rows, tile), jnp.float32),
        scratch_shapes=[pltpu.VMEM((nsky, rows, tile), jnp.float32)],
        compiler_params=params(),
    )(ids, exponent, beams)


def normal_body(ids_ref, owner_ref, tiles_ref, floor_ref, out_ref, acc_ref):
    npoint, s_dev, ch = tiles_ref.shape[:3]
    nsky = floor_ref.shape[0]
    acc_ref[...] = jnp.zeros_like(acc_ref)

    def step(d, carry):
        for s in range(s_dev):
            at = ids_ref[d, s]

            @pl.when(at < nsky)
            def _():
                acc_ref[at] += tiles_ref[d, s].astype(jnp.float32)

        return carry

    lax.fori_loop(0, npoint, step, 0)
    per = out_ref.shape[1]

    def emit(d, carry):
        for k in range(per):
            t = owner_ref[d * per + k]
            inv = floor_ref[t]
            for c in range(ch):
                out_ref[d, k, c] = (acc_ref[t, c] / inv).astype(jnp.bfloat16)
        return carry

    lax.fori_loop(0, npoint, emit, 0)


def normalise(ids, owner, tiles, floored):
    npoint, s_dev, ch, rows, tile = tiles.shape
    nsky = owner.shape[0]
    return pl.pallas_call(
        normal_body,
        in_specs=[
            pl.BlockSpec(memory_space=pltpu.SMEM),
            pl.BlockSpec(memory_space=pltpu.SMEM),
            pl.BlockSpec(memory_space=pltpu.VMEM),
            pl.BlockSpec(memory_space=pltpu.VMEM),
        ],
        out_specs=pl.BlockSpec(memory_space=pltpu.VMEM),
        out_shape=jax.ShapeDtypeStruct((npoint, nsky // npoint, ch, rows, tile), jnp.bfloat16),
        scratch_shapes=[pltpu.VMEM((nsky, ch, rows, tile), jnp.float32)],
        compiler_params=params(),
    )(ids, owner, tiles, floored)


def conv_body(tiles_ref, psf_ref, out_ref):
    tile = psf_ref.shape[-1]
    for c in range(tiles_ref.shape[2]):
        plane = tiles_ref[:, 0, c].reshape(tile, tile)
        left = lax.dot_general(
            plane, psf_ref[c, 1], (((1,), (1,)), ((), ())), preferred_element_type=jnp.float32
        ).astype(jnp.bfloat16)
        out_ref[0, c] = jnp.dot(
            psf_ref[c, 0], left, preferred_element_type=jnp.float32
        ).astype(jnp.bfloat16)


def convolve(tiles, psf):
    npoint, per, ch, rows, tile = tiles.shape
    return pl.pallas_call(
        conv_body,
        grid=(per,),
        in_specs=[
            pl.BlockSpec((npoint, 1, ch, rows, tile), lambda i: (0, i, 0, 0, 0)),
            pl.BlockSpec(psf.shape, lambda i: (0, 0, 0, 0)),
        ],
        out_specs=pl.BlockSpec((1, ch, tile, tile), lambda i: (i, 0, 0, 0)),
        out_shape=jax.ShapeDtypeStruct((per, ch, tile, tile), jnp.bfloat16),
        compiler_params=params(),
    )(tiles, psf)


def row_split_shards(images, beam, exponent, intersection, counts, owner, psf):
    pts, slots, ch, tile, _ = images.shape
    npoint = lax.axis_size("point")
    nchan = lax.axis_size("chan")
    s_dev = pts * slots
    part = s_dev // nchan
    nsky = owner.shape[0]
    chan_pos = lax.axis_index("chan")

    live = jnp.arange(slots)[None, :] < counts[:, None]
    own_ids = jnp.where(live, intersection, nsky).reshape(1, s_dev)
    ids = lax.all_to_all(
        jnp.broadcast_to(own_ids, (npoint, s_dev)), "point", split_axis=0, concat_axis=0, tiled=True
    )
    own_beam = lax.dynamic_slice_in_dim(
        beam.reshape(s_dev, tile, tile), chan_pos * part, part, axis=0
    )
    beam_rows = lax.all_to_all(
        split_rows(own_beam, npoint), "point", split_axis=0, concat_axis=0, tiled=True
    )
    own_exp = lax.dynamic_slice_in_dim(exponent, chan_pos * ch, ch)
    weighted = weigh(own_exp, images, beam, npoint)
    tiles = lax.all_to_all(weighted, "point", split_axis=0, concat_axis=0, tiled=True)
    beams = lax.all_gather(beam_rows, "chan", axis=0, tiled=False)
    floored = totals(ids, exponent, beams, nsky)
    ordered = normalise(ids, owner, tiles, floored)
    returned = lax.all_to_all(ordered, "point", split_axis=0, concat_axis=0, tiled=True)
    return convolve(returned, psf)


INNER = 4
PLANES = 4
SEND, OWN, RECV, COUNT = 0, 16, 20, 24
PLAN_ROWS = 32
FAR = (7, 9)
NEAR = 10
WIDE = (11, 14)


def vmem():
    return pl.BlockSpec(memory_space=pltpu.VMEM)


def smem():
    return pl.BlockSpec(memory_space=pltpu.SMEM)


def plan_body(here_ref, *refs):
    ids, (owner_ref, plan_ref, choice_ref, row_ref, tally_ref) = refs[:INNER], refs[INNER:]
    s_dev = ids[0].shape[1]
    nsky = owner_ref.shape[0]
    per_plane = nsky // PLANES
    most = plan_ref.shape[1] - 1
    wide = 2 * PLANES
    local_tally = PLANES * wide
    plane = here_ref[2]
    row_ref[nsky] = nsky

    def place(r, carry):
        row_ref[owner_ref[r]] = r
        return carry

    lax.fori_loop(0, nsky, place, 0, unroll=8)
    for n in range(PLANES * wide):
        tally_ref[n] = 0
    for k0 in range(PLANES):
        source = plane ^ k0
        for a in range(INNER):
            if k0 == 0:
                for k in range(wide):
                    tally_ref[local_tally + k] = 0
            for s in range(s_dev):
                row = row_ref[ids[a][k0, s]]
                far = lax.div(row, per_plane) ^ source
                n = tally_ref[k0 * wide + far]
                tally_ref[k0 * wide + far] = n + 1
                local = row - plane * per_plane
                if k0 > 0:
                    plan_ref[RECV + k0, jnp.where(far == k0, n, most)] = local
                else:
                    m = tally_ref[local_tally + far]
                    tally_ref[local_tally + far] = m + 1
                    known = far < PLANES
                    line = SEND + a * PLANES + jnp.where(known, far, 0)
                    plan_ref[line, jnp.where(known, m, most)] = s
                    plan_ref[OWN + a, jnp.where(far == 0, m, most)] = local
            if k0 == 0:
                for k in range(PLANES):
                    plan_ref[COUNT, a * PLANES + k] = tally_ref[local_tally + k]
        plan_ref[COUNT + 1, k0] = tally_ref[k0 * wide + k0]
    need = []
    for k in range(1, PLANES):
        value = tally_ref[k]
        for k0 in range(1, PLANES):
            value = jnp.maximum(value, tally_ref[k0 * wide + k])
        need.append(value)
    steps = len(FAR)
    choice = jnp.int32(0)
    for cap in FAR[:-1]:
        choice = choice + jnp.where(need[1] > cap, steps, 0) + jnp.where(need[2] > cap, 1, 0)
    most_needed = jnp.maximum(need[0], jnp.maximum(need[1], need[2]))
    over = (need[0] > NEAR) | (jnp.maximum(need[1], need[2]) > FAR[-1])
    wide = jnp.int32(steps * steps)
    for cap in WIDE:
        wide = wide + (most_needed > cap).astype(jnp.int32)
    choice_ref[0] = jnp.where(over, wide, choice)


def capacities(most):
    return [(NEAR, a, b) for a in FAR for b in FAR] + [(cap,) * 3 for cap in WIDE + (most,)]


def make_plan(here, ids, owner):
    most = INNER * ids[0].shape[1]
    return pl.pallas_call(
        plan_body,
        in_specs=[smem()] * (2 + INNER),
        out_specs=[smem()] * 2,
        out_shape=[
            jax.ShapeDtypeStruct((PLAN_ROWS, most + 1), jnp.int32),
            jax.ShapeDtypeStruct((1,), jnp.int32),
        ],
        scratch_shapes=[
            pltpu.SMEM((owner.shape[0] + 1,), jnp.int32),
            pltpu.SMEM(((PLANES + 1) * 2 * PLANES,), jnp.int32),
        ],
        compiler_params=params(),
    )(here, *ids, owner)


def quarter_body(chan, share, channels, here_ref, exp_ref, images_ref, beam_ref, *outs):
    slots, tile = images_ref.shape[1], images_ref.shape[-1]
    rows = tile // INNER
    inner = here_ref[0]
    for j in range(INNER):
        base = pl.multiple_of((inner ^ j) * rows, rows)

        def step(s, carry):
            if share:
                half = pl.multiple_of(base + here_ref[1] * share, share)
                outs[j][s, :share] = beam_ref[0, s, pl.ds(half, share), :]
            logs = jnp.log2(beam_ref[0, s, pl.ds(base, rows), :].astype(jnp.float32))
            plane = images_ref[0, s, 0, pl.ds(base, rows), :].astype(jnp.float32)
            outs[j][s, share:] = (jnp.exp2(exp_ref[here_ref[1] * channels + chan] * logs) * plane).astype(jnp.bfloat16)
            return carry

        lax.fori_loop(0, slots, step, 0)


def quarters(here, exponent, images, beam, chan, share):
    pts, slots, ch, tile, _ = images.shape
    rows = tile // INNER + share
    return pl.pallas_call(
        functools.partial(quarter_body, chan, share, ch),
        grid=(pts,),
        in_specs=[
            smem(),
            smem(),
            pl.BlockSpec((1, slots, 1, tile, tile), lambda p: (p, 0, chan, 0, 0)),
            pl.BlockSpec((1, slots, tile, tile), lambda p: (p, 0, 0, 0)),
        ],
        out_specs=[pl.BlockSpec((slots, rows, tile), lambda p: (p, 0, 0))] * INNER,
        out_shape=[jax.ShapeDtypeStruct((pts * slots, rows, tile), jnp.bfloat16)] * INNER,
        compiler_params=params(),
    )(here, exponent, images, beam)


def pack_body(plan_ref, *refs):
    got, outs = refs[:INNER], refs[INNER:]
    for k, out in enumerate(outs, 1):
        start = jnp.int32(0)
        for j in range(INNER):
            count = plan_ref[COUNT, j * PLANES + k]

            def step(n, carry):
                out[start + n] = got[j][plan_ref[SEND + j * PLANES + k, n]]
                return carry

            lax.fori_loop(0, count, step, 0)
            start = start + count


def pack(plan, got, caps):
    _, rows, tile = got[0].shape
    return pl.pallas_call(
        pack_body,
        in_specs=[smem()] + [vmem()] * INNER,
        out_specs=[vmem()] * len(caps),
        out_shape=[jax.ShapeDtypeStruct((cap, rows, tile), jnp.bfloat16) for cap in caps],
        compiler_params=params(),
    )(plan, *got)


def each_tile(plan_ref, got, recv, lines, add):
    for j in range(INNER):

        def own(n, carry):
            add(plan_ref[OWN + j, n], got[j][plan_ref[SEND + j * PLANES, n], lines, :])
            return carry

        lax.fori_loop(0, plan_ref[COUNT, j * PLANES], own, 0)
    for k, tiles in enumerate(recv, 1):

        def other(n, carry):
            add(plan_ref[RECV + k, n], tiles[n, lines, :])
            return carry

        lax.fori_loop(0, plan_ref[COUNT + 1, k], other, 0)


def inverse_body(share, here_ref, plan_ref, exp_ref, *refs):
    got, recv, outs, acc_ref = refs[:INNER], refs[INNER:-1 - INNER], refs[-1 - INNER:-1], refs[-1]
    ch = exp_ref.shape[0]
    per = outs[0].shape[0]
    acc_ref[...] = jnp.zeros_like(acc_ref)

    def add(t, tile):
        logs = jnp.log2(tile.astype(jnp.float32))
        weight = jnp.zeros_like(logs)
        for c in range(ch):
            weight = weight + jnp.exp2((2.0 * exp_ref[c]) * logs)
        acc_ref[t] += weight * (1.0 / ch)

    each_tile(plan_ref, got, recv, slice(0, share), add)
    for j in range(INNER):
        part = acc_ref[pl.ds((here_ref[0] ^ j) * per, per)]
        outs[j][...] = (1.0 / jnp.maximum(part, weight_floor)).astype(jnp.bfloat16)


def inverse_totals(here, plan, exponent, got, recv, share, per_plane):
    shape = (per_plane, share, got[0].shape[-1])
    out = jax.ShapeDtypeStruct((per_plane // INNER,) + shape[1:], jnp.bfloat16)
    return pl.pallas_call(
        functools.partial(inverse_body, share),
        in_specs=[smem()] * 3 + [vmem()] * (INNER + len(recv)),
        out_specs=[vmem()] * INNER,
        out_shape=[out] * INNER,
        scratch_shapes=[pltpu.VMEM(shape, jnp.float32)],
        compiler_params=params(),
    )(here, plan, exponent, *got, *recv)


def sum_body(skip, here_ref, plan_ref, *refs):
    got, recv, outs, acc_ref = refs[:INNER], refs[INNER:-1 - INNER], refs[-1 - INNER:-1], refs[-1]
    per, rows = outs[0].shape[:2]
    acc_ref[...] = jnp.zeros_like(acc_ref)

    def add(t, tile):
        acc_ref[t] += tile.astype(jnp.float32)

    each_tile(plan_ref, got, recv, slice(skip, skip + rows), add)
    for j in range(INNER):

        def emit(k, carry):
            outs[j][k] = acc_ref[(here_ref[0] ^ j) * per + k].astype(jnp.bfloat16)
            return carry

        lax.fori_loop(0, per, emit, 0)


def sum_tiles(here, plan, got, recv, skip, per_plane):
    _, rows, tile = got[0].shape
    rows = rows - skip
    return pl.pallas_call(
        functools.partial(sum_body, skip),
        in_specs=[smem()] * 2 + [vmem()] * (INNER + len(recv)),
        out_specs=[vmem()] * INNER,
        out_shape=[jax.ShapeDtypeStruct((per_plane // INNER, rows, tile), jnp.bfloat16)] * INNER,
        scratch_shapes=[pltpu.VMEM((per_plane, rows, tile), jnp.float32)],
        compiler_params=params(),
    )(here, plan, *got, *recv)


def plane_conv_body(nchan, here_ref, psf_ref, *refs):
    quarter, inverse, out_ref, left_ref = refs[:INNER], refs[INNER:INNER + nchan], refs[-2], refs[-1]
    per, rows, tile = quarter[0].shape
    share = inverse[0].shape[2]
    inner, chan = here_ref[0], here_ref[1]
    for j in range(INNER):
        for y in range(nchan):
            part = pl.ds(pl.multiple_of((chan ^ y) * share, share), share)
            value = quarter[j][:, part, :].astype(jnp.float32) * inverse[y][j].astype(jnp.float32)
            left = lax.dot_general(
                value.astype(jnp.bfloat16).reshape(per * share, tile),
                psf_ref[0, 1],
                (((1,), (1,)), ((), ())),
                preferred_element_type=jnp.float32,
            )
            start = pl.multiple_of((inner ^ j) * rows + (chan ^ y) * share, share)
            left = left.astype(jnp.bfloat16).reshape(per, share, tile)
            left_ref[:, pl.ds(start, share), :] = left
    for t in range(per):
        out_ref[t, 0] = jnp.dot(
            psf_ref[0, 0], left_ref[t], preferred_element_type=jnp.float32
        ).astype(jnp.bfloat16)


def plane_convolve(here, psf, quarter, inverses, chan, before):
    per, rows, tile = quarter[0].shape
    ch, share = psf.shape[0], inverses[0].shape[2]
    extra = [] if before is None else [before]
    block = per // 2
    return pl.pallas_call(
        functools.partial(plane_conv_body, len(inverses)),
        grid=(per // block,),
        in_specs=[smem(), pl.BlockSpec((1, 2, tile, tile), lambda t: (chan, 0, 0, 0))]
        + [pl.BlockSpec((block, rows, tile), lambda t: (t, 0, 0))] * INNER
        + [pl.BlockSpec((INNER, block, share, tile), lambda t: (0, t, 0, 0))] * len(inverses)
        + [pl.BlockSpec(memory_space=pl.ANY)] * len(extra),
        out_specs=pl.BlockSpec((block, 1, tile, tile), lambda t: (t, chan, 0, 0)),
        out_shape=jax.ShapeDtypeStruct((per, ch, tile, tile), jnp.bfloat16),
        scratch_shapes=[pltpu.VMEM((block, tile, tile), jnp.bfloat16)],
        input_output_aliases={2 + INNER + len(inverses): 0} if extra else {},
        compiler_params=params(),
    )(here, psf, *quarter, *inverses, *extra)


def swap(value, axis, distance):
    n = lax.axis_size(axis)
    return lax.ppermute(value, axis, [(d, d ^ distance) for d in range(n)])


def inside(parts):
    near = swap(parts[1], "point", 1)
    across = swap(parts[2], "point", 2)
    last, near = lax.optimization_barrier((parts[3], near))
    return [parts[0], near, across, swap(last, "point", 3)]


def exchange(parts):
    return [parts[0]] + [swap(parts[j], "point", j) for j in range(1, INNER)]


def between(parts):
    return [swap(part, "point", (k + 1) * INNER) for k, part in enumerate(parts)]


def plane_shards(images, beam, exponent, intersection, counts, owner, psf):
    pts, slots, ch, tile, _ = images.shape
    npoint, nchan = lax.axis_size("point"), lax.axis_size("chan")
    s_dev = pts * slots
    nsky = owner.shape[0]
    per_plane = nsky // PLANES
    share = tile // INNER // nchan
    chan_pos, point_pos = lax.axis_index("chan"), lax.axis_index("point")
    here = jnp.stack([point_pos % INNER, chan_pos, point_pos // INNER]).astype(jnp.int32)

    live = jnp.arange(slots)[None, :] < counts[:, None]
    own_ids = jnp.where(live, intersection, nsky).reshape(1, s_dev)
    column = [own_ids] + [swap(own_ids, "point", k * INNER) for k in range(1, PLANES)]
    column = jnp.concatenate(column, axis=0)
    ids = [column] + [swap(column, "point", j) for j in range(1, INNER)]
    first, ids = lax.optimization_barrier((quarters(here, exponent, images, beam, 0, share), ids))
    first = inside(first)
    plan, choice = make_plan(here, ids, owner)
    later = [quarters(here, exponent, images, beam, c, 0) for c in range(1, ch)]

    def branch(caps):
        def run(here, plan, first, later, exponent, psf):
            got, packed, recv = [first], [pack(plan, first, caps)], []
            for c in range(1, ch):
                recv.append(between(packed[-1]))
                parts, _ = lax.optimization_barrier((later[c - 1], packed[-1]))
                got.append(exchange(parts))
                packed.append(pack(plan, got[-1], caps))
                recv[-1], _ = lax.optimization_barrier((recv[-1], packed[-1]))
            recv.append(between(packed[-1]))
            inverse = inverse_totals(here, plan, exponent, first, recv[0], share, per_plane)
            inverse = exchange(inverse)
            if ch > 1:
                inverse, recv[1][1] = lax.optimization_barrier((inverse, recv[1][1]))
            inverse = jnp.stack(inverse)
            inverses = [inverse] + [swap(inverse, "chan", y) for y in range(1, nchan)]
            numer = []
            for c in range(ch):
                if c == 1:
                    recv[c], numer = lax.optimization_barrier((recv[c], numer))
                if c + 1 < ch:
                    recv[c], recv[c + 1][0] = lax.optimization_barrier((recv[c], recv[c + 1][0]))
                part = sum_tiles(here, plan, got[c], recv[c], 0 if c else share, per_plane)
                numer.append(inside(part))
            out = None
            for c in range(ch):
                out = plane_convolve(here, psf, numer[c], inverses, c, out)
            return out

        return run

    branches = [branch(caps) for caps in capacities(INNER * s_dev)]
    return lax.switch(choice[0], branches, here, plan, first, later, exponent, psf)


def shards(*args):
    if lax.axis_size("point") == PLANES * INNER:
        return plane_shards(*args)
    return row_split_shards(*args)


def solution(mesh):
    return jax.shard_map(
        shards,
        mesh=mesh,
        in_specs=(
            P("point", None, "chan", None, None),
            P("point", None, None, None),
            P(),
            P("point", None),
            P("point"),
            P(),
            P("chan", None, None, None),
        ),
        out_specs=P("point", "chan", None, None),
        check_vma=False,
    )
```

```python
import functools

import jax
import jax.numpy as jnp
from jax import lax
from jax.experimental import pallas as pl
from jax.experimental.pallas import tpu as pltpu
from jax.sharding import PartitionSpec as P

weight_floor = 0.05
VMEM_LIMIT = 48 * 1024 * 1024


def params():
    return pltpu.CompilerParams(vmem_limit_bytes=VMEM_LIMIT)


def put_rows(out_ref, at, value):
    group, rows = out_ref.shape[0], out_ref.shape[-2]
    for g in range(group):
        out_ref[(g,) + at] = value[g * rows:(g + 1) * rows].astype(jnp.bfloat16)


def row_block(tile, npoint):
    rows = tile // npoint
    block = max(rows, 16)
    return rows, block, block // rows


def weight_body(exp_ref, images_ref, beam_ref, out_ref):
    slots = images_ref.shape[1]
    for p in range(images_ref.shape[0]):
        for s in range(slots):
            logs = jnp.log(beam_ref[p, s].astype(jnp.float32))
            for c in range(images_ref.shape[2]):
                power = jnp.exp(exp_ref[c] * logs)
                plane = images_ref[p, s, c].astype(jnp.float32)
                put_rows(out_ref, (p * slots + s, c), power * plane)


def weigh(own_exp, images, beam, npoint):
    pts, slots, ch, tile, _ = images.shape
    rows, block, group = row_block(tile, npoint)
    return pl.pallas_call(
        weight_body,
        grid=(npoint // group,),
        in_specs=[
            pl.BlockSpec(memory_space=pltpu.SMEM),
            pl.BlockSpec((pts, slots, ch, block, tile), lambda i: (0, 0, 0, i, 0)),
            pl.BlockSpec((pts, slots, block, tile), lambda i: (0, 0, i, 0)),
        ],
        out_specs=pl.BlockSpec((group, pts * slots, ch, rows, tile), lambda i: (i, 0, 0, 0, 0)),
        out_shape=jax.ShapeDtypeStruct((npoint, pts * slots, ch, rows, tile), jnp.bfloat16),
        compiler_params=params(),
    )(own_exp, images, beam)


def split_body(beam_ref, out_ref):
    for s in range(beam_ref.shape[0]):
        put_rows(out_ref, (s,), beam_ref[s].astype(jnp.float32))


def split_rows(beam, npoint):
    s, tile, _ = beam.shape
    rows, block, group = row_block(tile, npoint)
    return pl.pallas_call(
        split_body,
        grid=(npoint // group,),
        in_specs=[pl.BlockSpec((s, block, tile), lambda i: (0, i, 0))],
        out_specs=pl.BlockSpec((group, s, rows, tile), lambda i: (i, 0, 0, 0)),
        out_shape=jax.ShapeDtypeStruct((npoint, s, rows, tile), jnp.bfloat16),
        compiler_params=params(),
    )(beam)


def total_body(s_dev, ids_ref, exp_ref, beam_ref, out_ref, acc_ref):
    nchan, npoint, part = beam_ref.shape[:3]
    nsky = out_ref.shape[0]
    ch = exp_ref.shape[0]
    acc_ref[...] = jnp.zeros_like(acc_ref)

    def step(d, carry):
        for share in range(nchan):
            for k in range(part):
                at = ids_ref[d, share * part + k]

                @pl.when(at < nsky)
                def _():
                    logs = jnp.log(beam_ref[share, d, k].astype(jnp.float32))
                    pw = jnp.zeros_like(logs)
                    for c in range(ch):
                        power = jnp.exp(exp_ref[c] * logs)
                        pw = pw + power * power
                    acc_ref[at] += pw * (1.0 / ch)

        return carry

    lax.fori_loop(0, npoint, step, 0)
    out_ref[...] = jnp.maximum(acc_ref[...], weight_floor)


def totals(ids, exponent, beams, nsky):
    rows, tile = beams.shape[3:]
    s_dev = ids.shape[1]
    return pl.pallas_call(
        functools.partial(total_body, s_dev),
        in_specs=[
            pl.BlockSpec(memory_space=pltpu.SMEM),
            pl.BlockSpec(memory_space=pltpu.SMEM),
            pl.BlockSpec(memory_space=pltpu.VMEM),
        ],
        out_specs=pl.BlockSpec(memory_space=pltpu.VMEM),
        out_shape=jax.ShapeDtypeStruct((nsky, rows, tile), jnp.float32),
        scratch_shapes=[pltpu.VMEM((nsky, rows, tile), jnp.float32)],
        compiler_params=params(),
    )(ids, exponent, beams)


def normal_body(ids_ref, owner_ref, tiles_ref, floor_ref, out_ref, acc_ref):
    npoint, s_dev, ch = tiles_ref.shape[:3]
    nsky = floor_ref.shape[0]
    acc_ref[...] = jnp.zeros_like(acc_ref)

    def step(d, carry):
        for s in range(s_dev):
            at = ids_ref[d, s]

            @pl.when(at < nsky)
            def _():
                acc_ref[at] += tiles_ref[d, s].astype(jnp.float32)

        return carry

    lax.fori_loop(0, npoint, step, 0)
    per = out_ref.shape[1]

    def emit(d, carry):
        for k in range(per):
            t = owner_ref[d * per + k]
            inv = floor_ref[t]
            for c in range(ch):
                out_ref[d, k, c] = (acc_ref[t, c] / inv).astype(jnp.bfloat16)
        return carry

    lax.fori_loop(0, npoint, emit, 0)


def normalise(ids, owner, tiles, floored):
    npoint, s_dev, ch, rows, tile = tiles.shape
    nsky = owner.shape[0]
    return pl.pallas_call(
        normal_body,
        in_specs=[
            pl.BlockSpec(memory_space=pltpu.SMEM),
            pl.BlockSpec(memory_space=pltpu.SMEM),
            pl.BlockSpec(memory_space=pltpu.VMEM),
            pl.BlockSpec(memory_space=pltpu.VMEM),
        ],
        out_specs=pl.BlockSpec(memory_space=pltpu.VMEM),
        out_shape=jax.ShapeDtypeStruct((npoint, nsky // npoint, ch, rows, tile), jnp.bfloat16),
        scratch_shapes=[pltpu.VMEM((nsky, ch, rows, tile), jnp.float32)],
        compiler_params=params(),
    )(ids, owner, tiles, floored)


def conv_body(tiles_ref, psf_ref, out_ref):
    tile = psf_ref.shape[-1]
    for c in range(tiles_ref.shape[2]):
        plane = tiles_ref[:, 0, c].reshape(tile, tile)
        left = lax.dot_general(
            plane, psf_ref[c, 1], (((1,), (1,)), ((), ())), preferred_element_type=jnp.float32
        ).astype(jnp.bfloat16)
        out_ref[0, c] = jnp.dot(
            psf_ref[c, 0], left, preferred_element_type=jnp.float32
        ).astype(jnp.bfloat16)


def convolve(tiles, psf):
    npoint, per, ch, rows, tile = tiles.shape
    return pl.pallas_call(
        conv_body,
        grid=(per,),
        in_specs=[
            pl.BlockSpec((npoint, 1, ch, rows, tile), lambda i: (0, i, 0, 0, 0)),
            pl.BlockSpec(psf.shape, lambda i: (0, 0, 0, 0)),
        ],
        out_specs=pl.BlockSpec((1, ch, tile, tile), lambda i: (i, 0, 0, 0)),
        out_shape=jax.ShapeDtypeStruct((per, ch, tile, tile), jnp.bfloat16),
        compiler_params=params(),
    )(tiles, psf)


def row_split_shards(images, beam, exponent, intersection, counts, owner, psf):
    pts, slots, ch, tile, _ = images.shape
    npoint = lax.axis_size("point")
    nchan = lax.axis_size("chan")
    s_dev = pts * slots
    part = s_dev // nchan
    nsky = owner.shape[0]
    chan_pos = lax.axis_index("chan")

    live = jnp.arange(slots)[None, :] < counts[:, None]
    own_ids = jnp.where(live, intersection, nsky).reshape(1, s_dev)
    ids = lax.all_to_all(
        jnp.broadcast_to(own_ids, (npoint, s_dev)), "point", split_axis=0, concat_axis=0, tiled=True
    )
    own_beam = lax.dynamic_slice_in_dim(
        beam.reshape(s_dev, tile, tile), chan_pos * part, part, axis=0
    )
    beam_rows = lax.all_to_all(
        split_rows(own_beam, npoint), "point", split_axis=0, concat_axis=0, tiled=True
    )
    own_exp = lax.dynamic_slice_in_dim(exponent, chan_pos * ch, ch)
    weighted = weigh(own_exp, images, beam, npoint)
    tiles = lax.all_to_all(weighted, "point", split_axis=0, concat_axis=0, tiled=True)
    beams = lax.all_gather(beam_rows, "chan", axis=0, tiled=False)
    floored = totals(ids, exponent, beams, nsky)
    ordered = normalise(ids, owner, tiles, floored)
    returned = lax.all_to_all(ordered, "point", split_axis=0, concat_axis=0, tiled=True)
    return convolve(returned, psf)


INNER = 4
PLANES = 4
SEND, OWN, RECV, COUNT = 0, 16, 20, 24
PLAN_ROWS = 32
ORDER = (0, 2, 3, 1)
NEAR = 12
FAR = (6, 8, 10)
WIDE = 14


def vmem():
    return pl.BlockSpec(memory_space=pltpu.VMEM)


def smem():
    return pl.BlockSpec(memory_space=pltpu.SMEM)


def plan_body(here_ref, *refs):
    ids, (owner_ref, plan_ref, choice_ref, row_ref, tally_ref) = refs[:INNER], refs[INNER:]
    s_dev = ids[0].shape[1]
    nsky = owner_ref.shape[0]
    per_plane = nsky // PLANES
    most = plan_ref.shape[1] - 1
    wide = 2 * PLANES
    local_tally = PLANES * wide
    plane = here_ref[2]
    row_ref[nsky] = nsky

    def place(r, carry):
        row_ref[owner_ref[r]] = r
        return carry

    lax.fori_loop(0, nsky, place, 0, unroll=8)
    for n in range(PLANES * wide):
        tally_ref[n] = 0
    for k0 in range(PLANES):
        source = plane ^ k0
        for a in range(INNER):
            if k0 == 0:
                for k in range(wide):
                    tally_ref[local_tally + k] = 0
            for s in range(s_dev):
                row = row_ref[ids[a][k0, s]]
                far = lax.div(row, per_plane) ^ source
                n = tally_ref[k0 * wide + far]
                tally_ref[k0 * wide + far] = n + 1
                local = row - plane * per_plane
                if k0 > 0:
                    plan_ref[RECV + k0, jnp.where(far == k0, n, most)] = local
                else:
                    m = tally_ref[local_tally + far]
                    tally_ref[local_tally + far] = m + 1
                    known = far < PLANES
                    line = SEND + a * PLANES + jnp.where(known, far, 0)
                    plan_ref[line, jnp.where(known, m, most)] = s
                    plan_ref[OWN + a, jnp.where(far == 0, m, most)] = local
            if k0 == 0:
                for k in range(PLANES):
                    plan_ref[COUNT, a * PLANES + k] = tally_ref[local_tally + k]
        plan_ref[COUNT + 1, k0] = tally_ref[k0 * wide + k0]
    need = []
    for k in range(1, PLANES):
        value = tally_ref[k]
        for k0 in range(1, PLANES):
            value = jnp.maximum(value, tally_ref[k0 * wide + k])
        need.append(value)
    steps = len(FAR)
    choice = jnp.int32(0)
    for cap in FAR[:-1]:
        choice = choice + jnp.where(need[1] > cap, steps, 0) + jnp.where(need[2] > cap, 1, 0)
    far = jnp.maximum(need[1], need[2])
    over = (need[0] > NEAR) | (far > FAR[-1])
    choice = jnp.where(over, steps * steps, choice)
    choice = jnp.where(jnp.maximum(need[0], far) > WIDE, steps * steps + 1, choice)
    choice_ref[0] = choice


def capacities(most):
    return [(NEAR, a, b) for a in FAR for b in FAR] + [(WIDE,) * 3, (most,) * 3]


def make_plan(here, ids, owner):
    most = INNER * ids[0].shape[1]
    return pl.pallas_call(
        plan_body,
        in_specs=[smem()] * (2 + INNER),
        out_specs=[smem()] * 2,
        out_shape=[
            jax.ShapeDtypeStruct((PLAN_ROWS, most + 1), jnp.int32),
            jax.ShapeDtypeStruct((1,), jnp.int32),
        ],
        scratch_shapes=[
            pltpu.SMEM((owner.shape[0] + 1,), jnp.int32),
            pltpu.SMEM(((PLANES + 1) * 2 * PLANES,), jnp.int32),
        ],
        compiler_params=params(),
    )(here, *ids, owner)


def quarter_body(chan, share, channels, here_ref, exp_ref, images_ref, beam_ref, *outs):
    slots, tile = images_ref.shape[1], images_ref.shape[-1]
    rows = tile // INNER
    inner = here_ref[0]
    for j in range(INNER):
        base = pl.multiple_of((inner ^ j) * rows, rows)

        def step(s, carry):
            if share:
                half = pl.multiple_of(base + here_ref[1] * share, share)
                outs[j][s, :share] = beam_ref[0, s, pl.ds(half, share), :]
            logs = jnp.log2(beam_ref[0, s, pl.ds(base, rows), :].astype(jnp.float32))
            plane = images_ref[0, s, 0, pl.ds(base, rows), :].astype(jnp.float32)
            outs[j][s, share:] = (jnp.exp2(exp_ref[here_ref[1] * channels + chan] * logs) * plane).astype(jnp.bfloat16)
            return carry

        lax.fori_loop(0, slots, step, 0)


def quarters(here, exponent, images, beam, chan, share):
    pts, slots, ch, tile, _ = images.shape
    rows = tile // INNER + share
    return pl.pallas_call(
        functools.partial(quarter_body, chan, share, ch),
        grid=(pts,),
        in_specs=[
            smem(),
            smem(),
            pl.BlockSpec((1, slots, 1, tile, tile), lambda p: (p, 0, chan, 0, 0)),
            pl.BlockSpec((1, slots, tile, tile), lambda p: (p, 0, 0, 0)),
        ],
        out_specs=[pl.BlockSpec((slots, rows, tile), lambda p: (p, 0, 0))] * INNER,
        out_shape=[jax.ShapeDtypeStruct((pts * slots, rows, tile), jnp.bfloat16)] * INNER,
        compiler_params=params(),
    )(here, exponent, images, beam)


def pack_body(plan_ref, *refs):
    got, outs = refs[:INNER], refs[INNER:]
    for k, out in enumerate(outs, 1):
        start = jnp.int32(0)
        for j in range(INNER):
            count = plan_ref[COUNT, j * PLANES + k]

            def step(n, carry):
                out[start + n] = got[j][plan_ref[SEND + j * PLANES + k, n]]
                return carry

            lax.fori_loop(0, count, step, 0)
            start = start + count


def pack(plan, got, caps):
    _, rows, tile = got[0].shape
    return pl.pallas_call(
        pack_body,
        in_specs=[smem()] + [vmem()] * INNER,
        out_specs=[vmem()] * len(caps),
        out_shape=[jax.ShapeDtypeStruct((cap, rows, tile), jnp.bfloat16) for cap in caps],
        compiler_params=params(),
    )(plan, *got)


def each_tile(plan_ref, got, recv, lines, add):
    for j in range(INNER):

        def own(n, carry):
            add(plan_ref[OWN + j, n], got[j][plan_ref[SEND + j * PLANES, n], lines, :])
            return carry

        lax.fori_loop(0, plan_ref[COUNT, j * PLANES], own, 0)
    for k, tiles in enumerate(recv, 1):

        def other(n, carry):
            add(plan_ref[RECV + k, n], tiles[n, lines, :])
            return carry

        lax.fori_loop(0, plan_ref[COUNT + 1, k], other, 0)


def inverse_body(share, plan_ref, exp_ref, *refs):
    got, recv, out_ref, acc_ref = refs[:INNER], refs[INNER:-2], refs[-2], refs[-1]
    ch = exp_ref.shape[0]
    acc_ref[...] = jnp.zeros_like(acc_ref)

    def add(t, tile):
        logs = jnp.log2(tile.astype(jnp.float32))
        weight = jnp.zeros_like(logs)
        for c in range(ch):
            weight = weight + jnp.exp2((2.0 * exp_ref[c]) * logs)
        acc_ref[t] += weight * (1.0 / ch)

    each_tile(plan_ref, got, recv, slice(0, share), add)
    out_ref[...] = (1.0 / jnp.maximum(acc_ref[...], weight_floor)).astype(out_ref.dtype)


def inverse_totals(plan, exponent, got, recv, share, per_plane):
    shape = (per_plane, share, got[0].shape[-1])
    return pl.pallas_call(
        functools.partial(inverse_body, share),
        in_specs=[smem()] * 2 + [vmem()] * (INNER + len(recv)),
        out_specs=vmem(),
        out_shape=jax.ShapeDtypeStruct(shape, jnp.bfloat16),
        scratch_shapes=[pltpu.VMEM(shape, jnp.float32)],
        compiler_params=params(),
    )(plan, exponent, *got, *recv)


def sum_body(skip, nrecv, here_ref, plan_ref, *refs):
    got, recv = refs[:INNER], refs[INNER:INNER + nrecv]
    inverse, outs, acc_ref = refs[INNER + nrecv:-1 - INNER], refs[-1 - INNER:-1], refs[-1]
    inner, chan = here_ref[0], here_ref[1]
    share = inverse[0].shape[1]
    per, rows = outs[0].shape[:2]
    acc_ref[...] = jnp.zeros_like(acc_ref)

    def add(t, tile):
        acc_ref[t] += tile.astype(jnp.float32)

    each_tile(plan_ref, got, recv, slice(skip, skip + rows), add)
    for j in range(INNER):

        def emit(k, carry):
            t = (inner ^ j) * per + k
            for y, inv in enumerate(inverse):
                part = pl.ds(pl.multiple_of((chan ^ y) * share, share), share)
                value = acc_ref[t, part, :] * inv[t].astype(jnp.float32)
                outs[j][k, part, :] = value.astype(jnp.bfloat16)
            return carry

        lax.fori_loop(0, per, emit, 0)


def sum_normal(here, plan, got, recv, inverse, skip, per_plane):
    _, rows, tile = got[0].shape
    rows = rows - skip
    return pl.pallas_call(
        functools.partial(sum_body, skip, len(recv)),
        in_specs=[smem()] * 2 + [vmem()] * (INNER + len(recv) + len(inverse)),
        out_specs=[vmem()] * INNER,
        out_shape=[jax.ShapeDtypeStruct((per_plane // INNER, rows, tile), jnp.bfloat16)] * INNER,
        scratch_shapes=[pltpu.VMEM((per_plane, rows, tile), jnp.float32)],
        compiler_params=params(),
    )(here, plan, *got, *recv, *inverse)


def plane_conv_body(here_ref, psf_ref, *refs):
    quarter, out_ref, left_ref = refs[:INNER], refs[-2], refs[-1]
    per, rows, tile = quarter[0].shape
    inner = here_ref[0]
    for j, part in zip(ORDER, quarter):
        left = lax.dot_general(
            part[...].reshape(per * rows, tile),
            psf_ref[0, 1],
            (((1,), (1,)), ((), ())),
            preferred_element_type=jnp.float32,
        )
        at = pl.ds(pl.multiple_of((inner ^ j) * rows, rows), rows)
        left_ref[:, at, :] = left.astype(jnp.bfloat16).reshape(per, rows, tile)
    for t in range(per):
        out_ref[t, 0] = jnp.dot(
            psf_ref[0, 0], left_ref[t], preferred_element_type=jnp.float32
        ).astype(jnp.bfloat16)


def plane_convolve(here, psf, quarter, chan, before):
    per, rows, tile = quarter[0].shape
    ch = psf.shape[0]
    extra = [] if before is None else [before]
    block = per // 2
    return pl.pallas_call(
        plane_conv_body,
        grid=(per // block,),
        in_specs=[smem(), pl.BlockSpec((1, 2, tile, tile), lambda t: (chan, 0, 0, 0))]
        + [pl.BlockSpec((block, rows, tile), lambda t: (t, 0, 0))] * INNER
        + [pl.BlockSpec(memory_space=pl.ANY)] * len(extra),
        out_specs=pl.BlockSpec((block, 1, tile, tile), lambda t: (t, chan, 0, 0)),
        out_shape=jax.ShapeDtypeStruct((per, ch, tile, tile), jnp.bfloat16),
        scratch_shapes=[pltpu.VMEM((block, tile, tile), jnp.bfloat16)],
        input_output_aliases={2 + INNER: 0} if extra else {},
        compiler_params=params(),
    )(here, psf, *[quarter[j] for j in ORDER], *extra)


def swap(value, axis, distance):
    n = lax.axis_size(axis)
    return lax.ppermute(value, axis, [(d, d ^ distance) for d in range(n)])


def inside(parts):
    near = swap(parts[1], "point", 1)
    across = swap(parts[2], "point", 2)
    last, near = lax.optimization_barrier((parts[3], near))
    return [parts[0], near, across, swap(last, "point", 3)]


def exchange(parts):
    return [parts[0]] + [swap(parts[j], "point", j) for j in range(1, INNER)]


def between(parts):
    return [swap(part, "point", (k + 1) * INNER) for k, part in enumerate(parts)]


def plane_shards(images, beam, exponent, intersection, counts, owner, psf):
    pts, slots, ch, tile, _ = images.shape
    npoint, nchan = lax.axis_size("point"), lax.axis_size("chan")
    s_dev = pts * slots
    nsky = owner.shape[0]
    per_plane = nsky // PLANES
    share = tile // INNER // nchan
    chan_pos, point_pos = lax.axis_index("chan"), lax.axis_index("point")
    here = jnp.stack([point_pos % INNER, chan_pos, point_pos // INNER]).astype(jnp.int32)

    live = jnp.arange(slots)[None, :] < counts[:, None]
    own_ids = jnp.where(live, intersection, nsky).reshape(1, s_dev)
    column = [own_ids] + [swap(own_ids, "point", k * INNER) for k in range(1, PLANES)]
    column = jnp.concatenate(column, axis=0)
    ids = [column] + [swap(column, "point", j) for j in range(1, INNER)]
    first, ids = lax.optimization_barrier((quarters(here, exponent, images, beam, 0, share), ids))
    first = inside(first)
    plan, choice = make_plan(here, ids, owner)
    later = [quarters(here, exponent, images, beam, c, 0) for c in range(1, ch)]

    def branch(caps):
        def run(here, plan, first, later, exponent, psf):
            got, packed, recv = [first], [pack(plan, first, caps)], []
            for c in range(1, ch):
                recv.append(between(packed[-1]))
                parts, _ = lax.optimization_barrier((later[c - 1], packed[-1]))
                got.append(exchange(parts))
                packed.append(pack(plan, got[-1], caps))
                packed[-1], recv[-1] = lax.optimization_barrier((packed[-1], recv[-1]))
            recv.append(between(packed[-1]))
            inverse = inverse_totals(plan, exponent, first, recv[0], share, per_plane)
            inverses = [inverse] + [swap(inverse, "chan", y) for y in range(1, nchan)]
            out = None
            for c in range(ch):
                skip = 0 if c else share
                part = sum_normal(here, plan, got[c], recv[c], inverses, skip, per_plane)
                normal = exchange(part)
                out = plane_convolve(here, psf, normal, c, out)
            return out

        return run

    branches = [branch(caps) for caps in capacities(INNER * s_dev)]
    return lax.switch(choice[0], branches, here, plan, first, later, exponent, psf)


def shards(*args):
    if lax.axis_size("point") == PLANES * INNER:
        return plane_shards(*args)
    return row_split_shards(*args)


def solution(mesh):
    return jax.shard_map(
        shards,
        mesh=mesh,
        in_specs=(
            P("point", None, "chan", None, None),
            P("point", None, None, None),
            P(),
            P("point", None),
            P("point"),
            P(),
            P("chan", None, None, None),
        ),
        out_specs=P("point", "chan", None, None),
        check_vma=False,
    )
```

```python
import functools

import jax
import jax.numpy as jnp
from jax import lax
from jax.experimental import pallas as pl
from jax.experimental.pallas import tpu as pltpu
from jax.sharding import PartitionSpec as P

weight_floor = 0.05
VMEM_LIMIT = 48 * 1024 * 1024


def params():
    return pltpu.CompilerParams(vmem_limit_bytes=VMEM_LIMIT)


def put_rows(out_ref, at, value):
    group, rows = out_ref.shape[0], out_ref.shape[-2]
    for g in range(group):
        out_ref[(g,) + at] = value[g * rows:(g + 1) * rows].astype(jnp.bfloat16)


def row_block(tile, npoint):
    rows = tile // npoint
    block = max(rows, 16)
    return rows, block, block // rows


def weight_body(exp_ref, images_ref, beam_ref, out_ref):
    slots = images_ref.shape[1]
    for p in range(images_ref.shape[0]):
        for s in range(slots):
            logs = jnp.log(beam_ref[p, s].astype(jnp.float32))
            for c in range(images_ref.shape[2]):
                power = jnp.exp(exp_ref[c] * logs)
                plane = images_ref[p, s, c].astype(jnp.float32)
                put_rows(out_ref, (p * slots + s, c), power * plane)


def weigh(own_exp, images, beam, npoint):
    pts, slots, ch, tile, _ = images.shape
    rows, block, group = row_block(tile, npoint)
    return pl.pallas_call(
        weight_body,
        grid=(npoint // group,),
        in_specs=[
            pl.BlockSpec(memory_space=pltpu.SMEM),
            pl.BlockSpec((pts, slots, ch, block, tile), lambda i: (0, 0, 0, i, 0)),
            pl.BlockSpec((pts, slots, block, tile), lambda i: (0, 0, i, 0)),
        ],
        out_specs=pl.BlockSpec((group, pts * slots, ch, rows, tile), lambda i: (i, 0, 0, 0, 0)),
        out_shape=jax.ShapeDtypeStruct((npoint, pts * slots, ch, rows, tile), jnp.bfloat16),
        compiler_params=params(),
    )(own_exp, images, beam)


def split_body(beam_ref, out_ref):
    for s in range(beam_ref.shape[0]):
        put_rows(out_ref, (s,), beam_ref[s].astype(jnp.float32))


def split_rows(beam, npoint):
    s, tile, _ = beam.shape
    rows, block, group = row_block(tile, npoint)
    return pl.pallas_call(
        split_body,
        grid=(npoint // group,),
        in_specs=[pl.BlockSpec((s, block, tile), lambda i: (0, i, 0))],
        out_specs=pl.BlockSpec((group, s, rows, tile), lambda i: (i, 0, 0, 0)),
        out_shape=jax.ShapeDtypeStruct((npoint, s, rows, tile), jnp.bfloat16),
        compiler_params=params(),
    )(beam)


def total_body(s_dev, ids_ref, exp_ref, beam_ref, out_ref, acc_ref):
    nchan, npoint, part = beam_ref.shape[:3]
    nsky = out_ref.shape[0]
    ch = exp_ref.shape[0]
    acc_ref[...] = jnp.zeros_like(acc_ref)

    def step(d, carry):
        for share in range(nchan):
            for k in range(part):
                at = ids_ref[d, share * part + k]

                @pl.when(at < nsky)
                def _():
                    logs = jnp.log(beam_ref[share, d, k].astype(jnp.float32))
                    pw = jnp.zeros_like(logs)
                    for c in range(ch):
                        power = jnp.exp(exp_ref[c] * logs)
                        pw = pw + power * power
                    acc_ref[at] += pw * (1.0 / ch)

        return carry

    lax.fori_loop(0, npoint, step, 0)
    out_ref[...] = jnp.maximum(acc_ref[...], weight_floor)


def totals(ids, exponent, beams, nsky):
    rows, tile = beams.shape[3:]
    s_dev = ids.shape[1]
    return pl.pallas_call(
        functools.partial(total_body, s_dev),
        in_specs=[
            pl.BlockSpec(memory_space=pltpu.SMEM),
            pl.BlockSpec(memory_space=pltpu.SMEM),
            pl.BlockSpec(memory_space=pltpu.VMEM),
        ],
        out_specs=pl.BlockSpec(memory_space=pltpu.VMEM),
        out_shape=jax.ShapeDtypeStruct((nsky, rows, tile), jnp.float32),
        scratch_shapes=[pltpu.VMEM((nsky, rows, tile), jnp.float32)],
        compiler_params=params(),
    )(ids, exponent, beams)


def normal_body(ids_ref, owner_ref, tiles_ref, floor_ref, out_ref, acc_ref):
    npoint, s_dev, ch = tiles_ref.shape[:3]
    nsky = floor_ref.shape[0]
    acc_ref[...] = jnp.zeros_like(acc_ref)

    def step(d, carry):
        for s in range(s_dev):
            at = ids_ref[d, s]

            @pl.when(at < nsky)
            def _():
                acc_ref[at] += tiles_ref[d, s].astype(jnp.float32)

        return carry

    lax.fori_loop(0, npoint, step, 0)
    per = out_ref.shape[1]

    def emit(d, carry):
        for k in range(per):
            t = owner_ref[d * per + k]
            inv = floor_ref[t]
            for c in range(ch):
                out_ref[d, k, c] = (acc_ref[t, c] / inv).astype(jnp.bfloat16)
        return carry

    lax.fori_loop(0, npoint, emit, 0)


def normalise(ids, owner, tiles, floored):
    npoint, s_dev, ch, rows, tile = tiles.shape
    nsky = owner.shape[0]
    return pl.pallas_call(
        normal_body,
        in_specs=[
            pl.BlockSpec(memory_space=pltpu.SMEM),
            pl.BlockSpec(memory_space=pltpu.SMEM),
            pl.BlockSpec(memory_space=pltpu.VMEM),
            pl.BlockSpec(memory_space=pltpu.VMEM),
        ],
        out_specs=pl.BlockSpec(memory_space=pltpu.VMEM),
        out_shape=jax.ShapeDtypeStruct((npoint, nsky // npoint, ch, rows, tile), jnp.bfloat16),
        scratch_shapes=[pltpu.VMEM((nsky, ch, rows, tile), jnp.float32)],
        compiler_params=params(),
    )(ids, owner, tiles, floored)


def conv_body(tiles_ref, psf_ref, out_ref):
    tile = psf_ref.shape[-1]
    for c in range(tiles_ref.shape[2]):
        plane = tiles_ref[:, 0, c].reshape(tile, tile)
        left = lax.dot_general(
            plane, psf_ref[c, 1], (((1,), (1,)), ((), ())), preferred_element_type=jnp.float32
        ).astype(jnp.bfloat16)
        out_ref[0, c] = jnp.dot(
            psf_ref[c, 0], left, preferred_element_type=jnp.float32
        ).astype(jnp.bfloat16)


def convolve(tiles, psf):
    npoint, per, ch, rows, tile = tiles.shape
    return pl.pallas_call(
        conv_body,
        grid=(per,),
        in_specs=[
            pl.BlockSpec((npoint, 1, ch, rows, tile), lambda i: (0, i, 0, 0, 0)),
            pl.BlockSpec(psf.shape, lambda i: (0, 0, 0, 0)),
        ],
        out_specs=pl.BlockSpec((1, ch, tile, tile), lambda i: (i, 0, 0, 0)),
        out_shape=jax.ShapeDtypeStruct((per, ch, tile, tile), jnp.bfloat16),
        compiler_params=params(),
    )(tiles, psf)


def row_split_shards(images, beam, exponent, intersection, counts, owner, psf):
    pts, slots, ch, tile, _ = images.shape
    npoint = lax.axis_size("point")
    nchan = lax.axis_size("chan")
    s_dev = pts * slots
    part = s_dev // nchan
    nsky = owner.shape[0]
    chan_pos = lax.axis_index("chan")

    live = jnp.arange(slots)[None, :] < counts[:, None]
    own_ids = jnp.where(live, intersection, nsky).reshape(1, s_dev)
    ids = lax.all_to_all(
        jnp.broadcast_to(own_ids, (npoint, s_dev)), "point", split_axis=0, concat_axis=0, tiled=True
    )
    own_beam = lax.dynamic_slice_in_dim(
        beam.reshape(s_dev, tile, tile), chan_pos * part, part, axis=0
    )
    beam_rows = lax.all_to_all(
        split_rows(own_beam, npoint), "point", split_axis=0, concat_axis=0, tiled=True
    )
    own_exp = lax.dynamic_slice_in_dim(exponent, chan_pos * ch, ch)
    weighted = weigh(own_exp, images, beam, npoint)
    tiles = lax.all_to_all(weighted, "point", split_axis=0, concat_axis=0, tiled=True)
    beams = lax.all_gather(beam_rows, "chan", axis=0, tiled=False)
    floored = totals(ids, exponent, beams, nsky)
    ordered = normalise(ids, owner, tiles, floored)
    returned = lax.all_to_all(ordered, "point", split_axis=0, concat_axis=0, tiled=True)
    return convolve(returned, psf)


INNER = 4
PLANES = 4
SEND, OWN, RECV, COUNT = 0, 16, 20, 24
PLAN_ROWS = 32
ORDER = (0, 2, 3, 1)
NEAR = 12
FAR = (6, 8, 10)
WIDE = 14


def vmem():
    return pl.BlockSpec(memory_space=pltpu.VMEM)


def smem():
    return pl.BlockSpec(memory_space=pltpu.SMEM)


def plan_body(here_ref, *refs):
    ids, (owner_ref, plan_ref, choice_ref, row_ref, tally_ref) = refs[:INNER], refs[INNER:]
    s_dev = ids[0].shape[1]
    nsky = owner_ref.shape[0]
    per_plane = nsky // PLANES
    most = plan_ref.shape[1] - 1
    wide = 2 * PLANES
    local_tally = PLANES * wide
    plane = here_ref[2]
    row_ref[nsky] = nsky

    def place(r, carry):
        row_ref[owner_ref[r]] = r
        return carry

    lax.fori_loop(0, nsky, place, 0, unroll=8)
    for n in range(PLANES * wide):
        tally_ref[n] = 0
    for k0 in range(PLANES):
        source = plane ^ k0
        for a in range(INNER):
            if k0 == 0:
                for k in range(wide):
                    tally_ref[local_tally + k] = 0
            for s in range(s_dev):
                row = row_ref[ids[a][k0, s]]
                far = lax.div(row, per_plane) ^ source
                n = tally_ref[k0 * wide + far]
                tally_ref[k0 * wide + far] = n + 1
                local = row - plane * per_plane
                if k0 > 0:
                    plan_ref[RECV + k0, jnp.where(far == k0, n, most)] = local
                else:
                    m = tally_ref[local_tally + far]
                    tally_ref[local_tally + far] = m + 1
                    known = far < PLANES
                    line = SEND + a * PLANES + jnp.where(known, far, 0)
                    plan_ref[line, jnp.where(known, m, most)] = s
                    plan_ref[OWN + a, jnp.where(far == 0, m, most)] = local
            if k0 == 0:
                for k in range(PLANES):
                    plan_ref[COUNT, a * PLANES + k] = tally_ref[local_tally + k]
        plan_ref[COUNT + 1, k0] = tally_ref[k0 * wide + k0]
    need = []
    for k in range(1, PLANES):
        value = tally_ref[k]
        for k0 in range(1, PLANES):
            value = jnp.maximum(value, tally_ref[k0 * wide + k])
        need.append(value)
    steps = len(FAR)
    choice = jnp.int32(0)
    for cap in FAR[:-1]:
        choice = choice + jnp.where(need[1] > cap, steps, 0) + jnp.where(need[2] > cap, 1, 0)
    far = jnp.maximum(need[1], need[2])
    over = (need[0] > NEAR) | (far > FAR[-1])
    choice = jnp.where(over, steps * steps, choice)
    choice = jnp.where(jnp.maximum(need[0], far) > WIDE, steps * steps + 1, choice)
    choice_ref[0] = choice


def capacities(most):
    return [(NEAR, a, b) for a in FAR for b in FAR] + [(WIDE,) * 3, (most,) * 3]


def make_plan(here, ids, owner):
    most = INNER * ids[0].shape[1]
    return pl.pallas_call(
        plan_body,
        in_specs=[smem()] * (2 + INNER),
        out_specs=[smem()] * 2,
        out_shape=[
            jax.ShapeDtypeStruct((PLAN_ROWS, most + 1), jnp.int32),
            jax.ShapeDtypeStruct((1,), jnp.int32),
        ],
        scratch_shapes=[
            pltpu.SMEM((owner.shape[0] + 1,), jnp.int32),
            pltpu.SMEM(((PLANES + 1) * 2 * PLANES,), jnp.int32),
        ],
        compiler_params=params(),
    )(here, *ids, owner)


def quarter_body(chan, share, channels, here_ref, exp_ref, images_ref, beam_ref, *outs):
    slots, tile = images_ref.shape[1], images_ref.shape[-1]
    rows = tile // INNER
    inner = here_ref[0]
    for j in range(INNER):
        base = pl.multiple_of((inner ^ j) * rows, rows)

        def step(s, carry):
            if share:
                half = pl.multiple_of(base + here_ref[1] * share, share)
                outs[j][s, :share] = beam_ref[0, s, pl.ds(half, share), :]
            logs = jnp.log2(beam_ref[0, s, pl.ds(base, rows), :].astype(jnp.float32))
            plane = images_ref[0, s, 0, pl.ds(base, rows), :].astype(jnp.float32)
            outs[j][s, share:] = (jnp.exp2(exp_ref[here_ref[1] * channels + chan] * logs) * plane).astype(jnp.bfloat16)
            return carry

        lax.fori_loop(0, slots, step, 0)


def quarters(here, exponent, images, beam, chan, share):
    pts, slots, ch, tile, _ = images.shape
    rows = tile // INNER + share
    return pl.pallas_call(
        functools.partial(quarter_body, chan, share, ch),
        grid=(pts,),
        in_specs=[
            smem(),
            smem(),
            pl.BlockSpec((1, slots, 1, tile, tile), lambda p: (p, 0, chan, 0, 0)),
            pl.BlockSpec((1, slots, tile, tile), lambda p: (p, 0, 0, 0)),
        ],
        out_specs=[pl.BlockSpec((slots, rows, tile), lambda p: (p, 0, 0))] * INNER,
        out_shape=[jax.ShapeDtypeStruct((pts * slots, rows, tile), jnp.bfloat16)] * INNER,
        compiler_params=params(),
    )(here, exponent, images, beam)


def pack_body(plan_ref, *refs):
    got, outs = refs[:INNER], refs[INNER:]
    for k, out in enumerate(outs, 1):
        start = jnp.int32(0)
        for j in range(INNER):
            count = plan_ref[COUNT, j * PLANES + k]

            def step(n, carry):
                out[start + n] = got[j][plan_ref[SEND + j * PLANES + k, n]]
                return carry

            lax.fori_loop(0, count, step, 0)
            start = start + count


def pack(plan, got, caps):
    _, rows, tile = got[0].shape
    return pl.pallas_call(
        pack_body,
        in_specs=[smem()] + [vmem()] * INNER,
        out_specs=[vmem()] * len(caps),
        out_shape=[jax.ShapeDtypeStruct((cap, rows, tile), jnp.bfloat16) for cap in caps],
        compiler_params=params(),
    )(plan, *got)


def each_tile(plan_ref, got, recv, lines, add):
    for j in range(INNER):

        def own(n, carry):
            add(plan_ref[OWN + j, n], got[j][plan_ref[SEND + j * PLANES, n], lines, :])
            return carry

        lax.fori_loop(0, plan_ref[COUNT, j * PLANES], own, 0)
    for k, tiles in enumerate(recv, 1):

        def other(n, carry):
            add(plan_ref[RECV + k, n], tiles[n, lines, :])
            return carry

        lax.fori_loop(0, plan_ref[COUNT + 1, k], other, 0)


def inverse_body(share, plan_ref, exp_ref, *refs):
    got, recv, out_ref, acc_ref = refs[:INNER], refs[INNER:-2], refs[-2], refs[-1]
    ch = exp_ref.shape[0]
    acc_ref[...] = jnp.zeros_like(acc_ref)

    def add(t, tile):
        logs = jnp.log2(tile.astype(jnp.float32))
        weight = jnp.zeros_like(logs)
        for c in range(ch):
            weight = weight + jnp.exp2((2.0 * exp_ref[c]) * logs)
        acc_ref[t] += weight * (1.0 / ch)

    each_tile(plan_ref, got, recv, slice(0, share), add)
    out_ref[...] = (1.0 / jnp.maximum(acc_ref[...], weight_floor)).astype(out_ref.dtype)


def inverse_totals(plan, exponent, got, recv, share, per_plane):
    shape = (per_plane, share, got[0].shape[-1])
    return pl.pallas_call(
        functools.partial(inverse_body, share),
        in_specs=[smem()] * 2 + [vmem()] * (INNER + len(recv)),
        out_specs=vmem(),
        out_shape=jax.ShapeDtypeStruct(shape, jnp.bfloat16),
        scratch_shapes=[pltpu.VMEM(shape, jnp.float32)],
        compiler_params=params(),
    )(plan, exponent, *got, *recv)


def sum_body(skip, nrecv, here_ref, plan_ref, *refs):
    got, recv = refs[:INNER], refs[INNER:INNER + nrecv]
    inverse, outs, acc_ref = refs[INNER + nrecv:-1 - INNER], refs[-1 - INNER:-1], refs[-1]
    inner, chan = here_ref[0], here_ref[1]
    share = inverse[0].shape[1]
    per, rows = outs[0].shape[:2]
    acc_ref[...] = jnp.zeros_like(acc_ref)

    def add(t, tile):
        acc_ref[t] += tile.astype(jnp.float32)

    each_tile(plan_ref, got, recv, slice(skip, skip + rows), add)
    for j in range(INNER):

        def emit(k, carry):
            t = (inner ^ j) * per + k
            for y, inv in enumerate(inverse):
                part = pl.ds(pl.multiple_of((chan ^ y) * share, share), share)
                value = acc_ref[t, part, :] * inv[t].astype(jnp.float32)
                outs[j][k, part, :] = value.astype(jnp.bfloat16)
            return carry

        lax.fori_loop(0, per, emit, 0)


def sum_normal(here, plan, got, recv, inverse, skip, per_plane):
    _, rows, tile = got[0].shape
    rows = rows - skip
    return pl.pallas_call(
        functools.partial(sum_body, skip, len(recv)),
        in_specs=[smem()] * 2 + [vmem()] * (INNER + len(recv) + len(inverse)),
        out_specs=[vmem()] * INNER,
        out_shape=[jax.ShapeDtypeStruct((per_plane // INNER, rows, tile), jnp.bfloat16)] * INNER,
        scratch_shapes=[pltpu.VMEM((per_plane, rows, tile), jnp.float32)],
        compiler_params=params(),
    )(here, plan, *got, *recv, *inverse)


def plane_conv_body(here_ref, psf_ref, *refs):
    quarter, out_ref, left_ref = refs[:INNER], refs[-2], refs[-1]
    per, rows, tile = quarter[0].shape
    inner = here_ref[0]
    for j, part in zip(ORDER, quarter):
        left = lax.dot_general(
            part[...].reshape(per * rows, tile),
            psf_ref[0, 1],
            (((1,), (1,)), ((), ())),
            preferred_element_type=jnp.float32,
        )
        at = pl.ds(pl.multiple_of((inner ^ j) * rows, rows), rows)
        left_ref[:, at, :] = left.astype(jnp.bfloat16).reshape(per, rows, tile)
    for t in range(per):
        out_ref[t, 0] = jnp.dot(
            psf_ref[0, 0], left_ref[t], preferred_element_type=jnp.float32
        ).astype(jnp.bfloat16)


def plane_convolve(here, psf, quarter, chan, before):
    per, rows, tile = quarter[0].shape
    ch = psf.shape[0]
    extra = [] if before is None else [before]
    block = per // 2
    return pl.pallas_call(
        plane_conv_body,
        grid=(per // block,),
        in_specs=[smem(), pl.BlockSpec((1, 2, tile, tile), lambda t: (chan, 0, 0, 0))]
        + [pl.BlockSpec((block, rows, tile), lambda t: (t, 0, 0))] * INNER
        + [pl.BlockSpec(memory_space=pl.ANY)] * len(extra),
        out_specs=pl.BlockSpec((block, 1, tile, tile), lambda t: (t, chan, 0, 0)),
        out_shape=jax.ShapeDtypeStruct((per, ch, tile, tile), jnp.bfloat16),
        scratch_shapes=[pltpu.VMEM((block, tile, tile), jnp.bfloat16)],
        input_output_aliases={2 + INNER: 0} if extra else {},
        compiler_params=params(),
    )(here, psf, *[quarter[j] for j in ORDER], *extra)


def swap(value, axis, distance):
    n = lax.axis_size(axis)
    return lax.ppermute(value, axis, [(d, d ^ distance) for d in range(n)])


def inside(parts):
    near = swap(parts[1], "point", 1)
    across = swap(parts[2], "point", 2)
    last, near = lax.optimization_barrier((parts[3], near))
    return [parts[0], near, across, swap(last, "point", 3)]


def exchange(parts):
    return [parts[0]] + [swap(parts[j], "point", j) for j in range(1, INNER)]


def between(parts):
    return [swap(part, "point", (k + 1) * INNER) for k, part in enumerate(parts)]


def plane_shards(images, beam, exponent, intersection, counts, owner, psf):
    pts, slots, ch, tile, _ = images.shape
    npoint, nchan = lax.axis_size("point"), lax.axis_size("chan")
    s_dev = pts * slots
    nsky = owner.shape[0]
    per_plane = nsky // PLANES
    share = tile // INNER // nchan
    chan_pos, point_pos = lax.axis_index("chan"), lax.axis_index("point")
    here = jnp.stack([point_pos % INNER, chan_pos, point_pos // INNER]).astype(jnp.int32)

    live = jnp.arange(slots)[None, :] < counts[:, None]
    own_ids = jnp.where(live, intersection, nsky).reshape(1, s_dev)
    column = [own_ids] + [swap(own_ids, "point", k * INNER) for k in range(1, PLANES)]
    column = jnp.concatenate(column, axis=0)
    ids = [column] + [swap(column, "point", j) for j in range(1, INNER)]
    first, ids = lax.optimization_barrier((quarters(here, exponent, images, beam, 0, share), ids))
    first = inside(first)
    plan, choice = make_plan(here, ids, owner)
    later = [quarters(here, exponent, images, beam, c, 0) for c in range(1, ch)]

    def branch(caps):
        def run(here, plan, first, later, exponent, psf):
            got, packed, recv = [first], [pack(plan, first, caps)], []
            for c in range(1, ch):
                recv.append(between(packed[-1]))
                parts, _ = lax.optimization_barrier((later[c - 1], packed[-1]))
                got.append(exchange(parts))
                room = tuple(max(cap, per_plane // INNER) for cap in caps)
                packed.append(pack(plan, got[-1], room))
                packed[-1], recv[-1] = lax.optimization_barrier((packed[-1], recv[-1]))
            recv.append(between(packed[-1]))
            inverse = inverse_totals(plan, exponent, first, recv[0], share, per_plane)
            inverses = [inverse] + [swap(inverse, "chan", y) for y in range(1, nchan)]
            out = None
            for c in range(ch):
                skip = 0 if c else share
                part = sum_normal(here, plan, got[c], recv[c], inverses, skip, per_plane)
                normal = exchange(part)
                out = plane_convolve(here, psf, normal, c, out)
            return out

        return run

    branches = [branch(caps) for caps in capacities(INNER * s_dev)]
    return lax.switch(choice[0], branches, here, plan, first, later, exponent, psf)


def shards(*args):
    if lax.axis_size("point") == PLANES * INNER:
        return plane_shards(*args)
    return row_split_shards(*args)


def solution(mesh):
    return jax.shard_map(
        shards,
        mesh=mesh,
        in_specs=(
            P("point", None, "chan", None, None),
            P("point", None, None, None),
            P(),
            P("point", None),
            P("point"),
            P(),
            P("chan", None, None, None),
        ),
        out_specs=P("point", "chan", None, None),
        check_vma=False,
    )
```
